128 devices in a mesh: gx: 16 (over z, x), gy: 8 (over y, core).
Axes of the slice: x: 4, y: 4, z: 4, core: 2. Of those that a mesh axis runs over, the one named last changes fastest.
Arguments:
- positions: float32 [3, 1048576], P(None, ('gx', 'gy')), may hold values from -5 to 5, as said below
- noise: float32 [3, 1048576], P(None, ('gx', 'gy')), may hold values from -0.6 to 0.6
- route: int32 [1048576], P(('gx', 'gy')), may hold values from 0 to 16383, as said below
- node_perm: int32 [16, 8, 16384], P(None, 'gy'), may hold values from 0 to 16383, each once within a row
- pair_first: int32 [128, 1024], P(('gx', 'gy')), may hold values from 0 to 255
- pair_second: int32 [128, 1024], P(('gx', 'gy')), may hold values from 0 to 511
- pair_count: int32 [128], P(('gx', 'gy')), may hold values from 512 to 1024, as said below
Outputs:
- moved: float32 [3, 1048576], P(None, ('gx', 'gy'))
- drift: float32 [3, 1048576], P(None, ('gx', 'gy'))
The draws below stay inside these ranges and needn't reach their ends.
Inputs may be any that keep to these rules, and one draw needn't show every extreme that they name: `positions`: consecutive beads of a chain lie between 0.25 and 0.95 apart. `route`: within one device the values are distinct and rise along its beads; at most 128 beads of one device go to one device, and every device sends exactly 128 beads to some device. `pair_count`: some device's count is 1024.
All inputs are finite; a program needn't handle non-finite values.
Results may differ from the reference program's by a relative error of at most 0.015.
Values sent between devices are 32-bit elements; how exact they have to be, the bound alone decides.
A program may use at most 128 MiB of HBM per device.

```python
import math
import jax
import jax.numpy as jnp
from jax import lax

G = 128
BEAD_CH = 64
CELL = 64
PAIRS_DEV = 1024
SLOTS_DEV = 16384
CAP = 128
BEADS_DEV = 8192
BEADS = 1048576
BLK_DEV = 256
N_GX = 16
N_GY = 8
DEVICES = 128


def draw_positions(key, part):
    keys = jax.random.split(key, 3)
    chains = BEADS // BEAD_CH
    centre = jax.random.uniform(keys[0], (3, chains), jnp.float32, -1.5, 1.5)
    twist = jax.random.uniform(keys[1], (chains,), jnp.float32, -math.pi, math.pi)
    jitter = jax.random.uniform(keys[2], (3, BEADS), jnp.float32, -0.1, 0.1)
    along = jnp.arange(BEAD_CH, dtype=jnp.float32)
    angle = twist[:, None] + 0.6 * along[None, :]
    rise = jnp.broadcast_to(0.1 * (along[None, :] - 31.5), angle.shape)
    helix = jnp.stack([jnp.cos(angle), jnp.sin(angle), rise])
    return (centre[:, :, None] + helix).reshape(3, BEADS) + jitter


def draw_route(key, part):

    def one_device(device_key):
        keys = jax.random.split(device_key, 2)
        order = jax.random.permutation(keys[0], DEVICES * CAP).astype(jnp.int32)
        chosen = jax.random.randint(keys[1], (), 0, DEVICES)
        place = jnp.arange(DEVICES * CAP, dtype=jnp.int32)
        priority = order + jnp.where(place // CAP == chosen, DEVICES * CAP, 0).astype(jnp.int32)
        _, picked = lax.top_k(priority, BEADS_DEV)
        return jnp.sort(picked.astype(jnp.int32))
    return jax.vmap(one_device)(jax.random.split(key, DEVICES)).reshape(BEADS)


def draw_pair_count(key, part):
    keys = jax.random.split(key, 2)
    halving = jax.random.randint(keys[0], (DEVICES,), 0, 2)
    counts = jnp.right_shift(jnp.full((DEVICES,), PAIRS_DEV, jnp.int32), halving.astype(jnp.int32))
    fullest = jax.random.randint(keys[1], (), 0, DEVICES)
    return jnp.where(jnp.arange(DEVICES) == fullest, PAIRS_DEV, counts).astype(jnp.int32)


def plant(drawn, stream_key, low, high):
    dims = drawn.shape
    spot = [jax.random.randint(jax.random.fold_in(stream_key, axis), (), 0, dims[axis]) for axis in range(len(dims))]
    drawn = drawn.at[tuple(spot)].set(low)
    longest = dims.index(max(dims))
    spot[longest] = (spot[longest] + 1) % dims[longest]
    return drawn.at[tuple(spot)].set(high)


def block_scale(rng, shape, cuts, low, high):
    factor_of = 1.0
    for dim, parts in cuts:
        steps = jax.random.uniform(jax.random.fold_in(jax.random.fold_in(rng, 6), dim), (parts,), jnp.float32, low / len(cuts), high / len(cuts))
        factor_of = factor_of * jnp.repeat(jnp.exp(steps), shape[dim] // parts).reshape((-1,) + (1,) * (len(shape) - 1 - dim))
    return factor_of


def scatter_about(stream_key, shape, width, bound, cuts=(), kind=jnp.bfloat16):
    values = width * jax.random.normal(stream_key, shape, jnp.float32)
    if cuts:
        values = values * block_scale(stream_key, shape, cuts, -0.22, 0.18)
    return jnp.clip(values, -bound, bound).astype(kind)


def setup_inputs(seed: int = 0) -> dict:
    streams_of = jax.random.split(jax.random.key(seed), 8)
    return {
        "positions": draw_positions(jax.random.fold_in(streams_of[7], 71), 0),
        "noise": scatter_about(streams_of[1], (3, BEADS), 0.1, 0.6, ((1, 128),), jnp.float32),
        "route": draw_route(jax.random.fold_in(streams_of[7], 71), 0),
        "node_perm": jax.vmap(lambda own: jax.random.permutation(own, SLOTS_DEV))(jax.random.split(streams_of[3], N_GX * N_GY)).reshape((N_GX, N_GY, SLOTS_DEV)).astype(jnp.int32),
        "pair_first": plant(jax.random.randint(streams_of[4], (DEVICES, PAIRS_DEV), 0, BLK_DEV), jax.random.fold_in(streams_of[4], 1), 0, BLK_DEV - 1).astype(jnp.int32),
        "pair_second": plant(jax.random.randint(streams_of[5], (DEVICES, PAIRS_DEV), 0, 2 * BLK_DEV), jax.random.fold_in(streams_of[5], 1), 0, (2 * BLK_DEV) - 1).astype(jnp.int32),
        "pair_count": draw_pair_count(jax.random.fold_in(streams_of[7], 71), 0),
    }


bead_radius = 0.5
split_xi = 0.5
time_step = 0.01
fene_k = 30.0
fene_reach = 1.5
bend_k = 2.0
grid_spacing = 4.0
pair_block = 64

def bonded_forces(positions):
    chains = positions.reshape(3, -1, BEAD_CH)

    def energy(coords):
        bond = coords[:, :, 1:] - coords[:, :, :-1]
        square = lax.optimization_barrier(jnp.sum(bond * bond, axis=0))
        stretch = -0.5 * fene_k * fene_reach ** 2 * jnp.sum(jnp.log(1.0 - square / fene_reach ** 2))
        length = jnp.sqrt(square)
        cosine = lax.optimization_barrier(jnp.sum(bond[:, :, 1:] * bond[:, :, :-1], axis=0)) / (length[:, 1:] * length[:, :-1])
        return stretch + bend_k * jnp.sum(1.0 - cosine)
    return (-jax.grad(energy)(chains)).reshape(3, -1)

def tile_pairs(near_pos, near_force, far_pos, far_force):
    offsets = [near_pos[channel][:, :, None] - far_pos[channel][:, None, :] for channel in range(3)]
    square = offsets[0] * offsets[0] + offsets[1] * offsets[1] + offsets[2] * offsets[2] + bead_radius ** 2
    distance = jnp.sqrt(square)
    scaled = bead_radius / distance
    scaled_cube = scaled * scaled * scaled
    screen = jax.scipy.special.erfc(split_xi * distance)
    gauss_part = 0.5 * split_xi * bead_radius * jnp.exp(-split_xi ** 2 * square)
    along_part = screen * (0.75 * scaled + 0.5 * scaled_cube) + gauss_part
    across = (screen * (0.75 * scaled - 1.5 * scaled_cube) - gauss_part) / square
    onto_far = across * sum((offsets[channel] * far_force[channel][:, None, :] for channel in range(3)))
    onto_near = across * sum((offsets[channel] * near_force[channel][:, :, None] for channel in range(3)))
    near_vel = jnp.stack([lax.optimization_barrier(jnp.sum(along_part * far_force[channel][:, None, :] + onto_far * offsets[channel], axis=2)) for channel in range(3)])
    far_vel = jnp.stack([lax.optimization_barrier(jnp.sum(along_part * near_force[channel][:, :, None] + onto_near * offsets[channel], axis=1)) for channel in range(3)])
    return (near_vel, far_vel)

def real_space(cells, pair_first, pair_second, pair_count):
    devices = N_GX * N_GY
    owner = jnp.arange(devices, dtype=jnp.int32)[:, None]
    beside = (owner // N_GY + 1) % N_GX * N_GY + owner % N_GY
    first_glob = owner * BLK_DEV + pair_first
    second_glob = jnp.where(pair_second < BLK_DEV, owner * BLK_DEV + pair_second, beside * BLK_DEV + pair_second - BLK_DEV)
    live_mask = (jnp.arange(PAIRS_DEV, dtype=jnp.int32)[None, :] < pair_count[:, None]).astype(jnp.float32)
    batches = (first_glob.reshape(-1, pair_block), second_glob.reshape(-1, pair_block), live_mask.reshape(-1, pair_block))

    def turn(velocity_sum, batch):
        near_idx, far_idx, live_row = batch
        near_cells = jnp.take(cells, near_idx, axis=1)
        far_cells = jnp.take(cells, far_idx, axis=1)
        near_vel, far_vel = tile_pairs(near_cells[:3], near_cells[3:], far_cells[:3], far_cells[3:])
        cross_mask = live_row * (near_idx != far_idx).astype(jnp.float32)
        velocity_sum = velocity_sum.at[:, near_idx].add(near_vel * live_row[None, :, None])
        velocity_sum = velocity_sum.at[:, far_idx].add(far_vel * cross_mask[None, :, None])
        return (velocity_sum, None)
    start_sum = jnp.zeros((3, cells.shape[1], CELL), jnp.float32)
    velocity_sum, _ = lax.scan(turn, start_sum, batches)
    return velocity_sum

def kspace(force_grid):
    spectrum = jnp.fft.fftn(force_grid, axes=(1, 2, 3))
    wave = jnp.fft.fftfreq(G) * (2.0 * math.pi / grid_spacing)
    wave_x = wave[:, None, None]
    wave_y = wave[None, :, None]
    wave_z = wave[None, None, :]
    wave_sq = wave_x * wave_x + wave_y * wave_y + wave_z * wave_z
    wave_safe = jnp.where(wave_sq > 0, wave_sq, 1.0)
    spread_sq = wave_sq / (4.0 * split_xi ** 2)
    green_fn = jnp.where(wave_sq > 0, (1.0 - bead_radius ** 2 * wave_sq / 3.0) * (1.0 + spread_sq) * jnp.exp(-spread_sq) / wave_safe, 0.0)
    along_wave = (wave_x * spectrum[0] + wave_y * spectrum[1] + wave_z * spectrum[2]) / wave_safe
    flow = jnp.stack([green_fn * (spectrum[0] - wave_x * along_wave), green_fn * (spectrum[1] - wave_y * along_wave), green_fn * (spectrum[2] - wave_z * along_wave)])
    return jnp.real(jnp.fft.ifftn(flow, axes=(1, 2, 3)))

def reference(positions, noise, route, node_perm, pair_first, pair_second, pair_count):
    forces = bonded_forces(positions)
    devices = N_GX * N_GY
    source = jnp.arange(BEADS_DEV * devices, dtype=jnp.int32) // BEADS_DEV
    target = route // CAP
    message = source * CAP + route % CAP
    node_at = node_perm[target // N_GY, target % N_GY, message]
    place_at = target * SLOTS_DEV + node_at
    layout = jnp.zeros((6, devices * SLOTS_DEV), jnp.float32).at[:, place_at].set(jnp.concatenate([positions, forces], axis=0))
    local_x = G // N_GX
    local_y = G // N_GY
    force_grid = layout[3:].reshape(3, N_GX, N_GY, local_x, local_y, G).transpose(0, 1, 3, 2, 4, 5).reshape(3, G, G, G)
    wave_vel = kspace(force_grid).reshape(3, N_GX, local_x, N_GY, local_y, G).transpose(0, 1, 3, 2, 4, 5).reshape(3, devices * SLOTS_DEV)
    real_vel = real_space(layout.reshape(6, devices * BLK_DEV, CELL), pair_first, pair_second, pair_count).reshape(3, devices * SLOTS_DEV)
    velocity = (real_vel + wave_vel)[:, place_at]
    drift = time_step * velocity
    moved = positions + drift + noise
    return (moved, drift)
```

```python
from functools import partial
import math

import numpy as np
import jax
import jax.numpy as jnp
from jax import lax
from jax.experimental import pallas as pl
from jax.experimental.pallas import tpu as pltpu
from jax.sharding import PartitionSpec as P

G = 128
BLOCKS = 256
PAIRS = 1024
STEP = 4
W_ROWS = 24
TRASH = 2 * BLOCKS

fene_k = 30.0
fene_reach = 1.5
bend_k = 2.0
time_step = 0.01
grid_spacing = 4.0

f32 = jnp.float32
bf16 = jnp.bfloat16
VMEM_LIMIT = 60 * 1024 * 1024


def dot(a, b):
    return lax.dot_general(a, b, (((1,), (0,)), ((), ())), preferred_element_type=f32)


def dot_t(a, b):
    return lax.dot_general(a, b, (((1,), (1,)), ((), ())), preferred_element_type=f32)


def split2(x):
    hi = x.astype(bf16)
    return hi, (x - hi.astype(f32)).astype(bf16)


def split3(x):
    hi = x.astype(bf16).astype(f32)
    rest = x - hi
    mid = rest.astype(bf16).astype(f32)
    return hi, mid, (rest - mid).astype(bf16).astype(f32)


def dot3(a_hi, a_lo, b_hi, b_lo, form=dot):
    return form(a_hi, b_hi) + form(a_hi, b_lo) + form(a_lo, b_hi)


def split_table(table):
    table = np.asarray(table, np.float64)
    hi = table.astype(np.float32).astype(jnp.bfloat16)
    lo = (table - hi.astype(np.float64)).astype(np.float32).astype(jnp.bfloat16)
    return np.stack([hi, lo])


def tables():
    n = np.arange(G)
    turn = 2.0 * np.pi / G
    member = np.arange(128)
    freq = np.where(member < 64, member + 1, (member - 63) % 64)
    wave = turn * (freq[:, None] * n[None, :] % G)
    even, odd = np.cos(wave), -np.sin(wave)
    special = (member % 64) == 63
    first = (member < 64)[:, None]
    even = np.where(special[:, None], np.cos(wave), even)
    z_xy = np.where(special[:, None] | first, even, odd)
    z_z = np.where(special[:, None] | ~first, even, odd)
    k1, k2 = n // 8, n % 8
    outer = 2.0 * np.pi * (k1[:, None] * k1[None, :] / 16.0 + k2[:, None] * k2[None, :] / 8.0)
    a, b = n // 16, n % 16
    inner = 2.0 * np.pi * (a[:, None] * a[None, :] / 8.0 + b[:, None] * b[None, :] / 16.0)
    twist = turn * (k1[:, None] * a[None, :] + k2[:, None] * b[None, :])
    c_out, s_out, c_in, s_in = np.cos(outer), np.sin(outer), np.cos(inner), np.sin(inner)
    return {
        "z": split_table(np.stack([z_xy, z_z])),
        "outer": split_table(np.concatenate([c_out, -s_out], 0)),
        "outer_back": split_table(np.concatenate([c_out, -s_out], 1)),
        "inner": split_table(np.block([[c_in, -s_in], [s_in, c_in]])),
        "inner_back": split_table(np.block([[c_in, s_in], [-s_in, c_in]])),
        "twist": np.stack([np.cos(twist), np.sin(twist)]).astype(np.float32),
    }


def onehot(index, size, width):
    rows = lax.broadcasted_iota(jnp.int32, (size, width), 0)
    return jnp.where(rows == index, 1.0, 0.0).astype(bf16)


def high_part(place):
    return (place >> 7) & 63


def low_part(place):
    return ((place >> 13) << 7) | (place & 127)


def scatter_rows(channels, rows, value_row, place_ref, left_ref, sum_ref):
    group = left_ref.shape[1] // 128
    span = 128 * group

    def turn(g, _):
        low = []
        for j in range(group):
            place = place_ref[pl.ds(g * group + j, 1), :]
            high_hot = onehot(high_part(place), 64, 128)
            low.append(onehot(low_part(place), 256, 128))
            for c in range(channels):
                hi, lo = split2(value_row(c, g * group + j))
                left_ref[c * 128 : c * 128 + 64, j * 128 : (j + 1) * 128] = high_hot * hi
                left_ref[c * 128 + 64 : c * 128 + 128, j * 128 : (j + 1) * 128] = high_hot * lo
        moved = dot_t(left_ref[...], jnp.concatenate(low, axis=1))
        for c in range(channels):
            sum_ref[c * 64 : (c + 1) * 64, :] += (
                moved[c * 128 : c * 128 + 64] + moved[c * 128 + 64 : c * 128 + 128]
            )
        return 0

    sum_ref[...] = jnp.zeros_like(sum_ref)
    lax.fori_loop(0, rows // group, turn, 0)


def gather_rows(channels, rows, table_hi_ref, table_lo_ref, place_ref, put):
    def turn(g, _):
        low, high = [], []
        for j in range(2):
            place = place_ref[pl.ds(g * 2 + j, 1), :]
            low.append(onehot(low_part(place), 256, 128))
            high.append(high_part(place))
        low = jnp.concatenate(low, axis=1)
        high = jnp.concatenate(high, axis=1)
        found = dot(table_hi_ref[...], low) + dot(table_lo_ref[...], low)
        rows_of = lax.broadcasted_iota(jnp.int32, (64, 256), 0) == high
        for c in range(channels):
            got = jnp.sum(
                jnp.where(rows_of, found[c * 64 : (c + 1) * 64], 0.0), axis=0, keepdims=True
            )
            for j in range(2):
                put(c, g * 2 + j, got[:, j * 128 : (j + 1) * 128])
        return 0

    lax.fori_loop(0, rows // 2, turn, 0)


def fill_table(c, plane, table_hi_ref, table_lo_ref):
    hi, lo = split2(plane)
    for ref, part in ((table_hi_ref, hi), (table_lo_ref, lo)):
        ref[c * 64 : (c + 1) * 64, 0:128] = part[0:64]
        ref[c * 64 : (c + 1) * 64, 128:256] = part[64:128]


def chain_forces(x):
    lane = lax.broadcasted_iota(jnp.int32, x[0].shape, 1) & 63
    last = lane == 63
    ahead = lambda v: pltpu.roll(v, 127, 1)
    behind = lambda v: pltpu.roll(v, 1, 1)
    bond = [jnp.where(last, 0.5, ahead(v) - v) for v in x]
    square = bond[0] * bond[0] + bond[1] * bond[1] + bond[2] * bond[2]
    inverse = lax.rsqrt(square)
    unit = [v * inverse for v in bond]
    following = [ahead(v) for v in unit]
    cosine = unit[0] * following[0] + unit[1] * following[1] + unit[2] * following[2]
    bends = lane < 62
    stretch = fene_k / (1.0 - square / fene_reach**2)
    before = behind(jnp.where(bends, 1.0, 0.0))
    cosine_before = behind(cosine)
    grad = []
    for c in range(3):
        pull = jnp.where(bends, following[c] - cosine * unit[c], 0.0)
        push = before * (behind(unit[c]) - cosine_before * unit[c])
        push = jnp.where(lane == 0, 0.0, push)
        grad.append(
            jnp.where(last, 0.0, stretch * bond[c] - bend_k * inverse * (pull + push))
        )
    return [g - jnp.where(lane == 0, 0.0, behind(g)) for g in grad]


def send_kernel(pos_ref, route_ref, out_ref, plane_ref, left_ref, sum_ref):
    rows = route_ref.shape[0]
    for c in range(3):
        for r in range(rows):
            plane_ref[c, r : r + 1, :] = pos_ref[c : c + 1, r * 128 : (r + 1) * 128]
    forces = chain_forces([plane_ref[c] for c in range(3)])
    for c in range(3):
        plane_ref[3 + c] = forces[c]
    scatter_rows(
        6, rows, lambda c, r: plane_ref[c, pl.ds(r, 1), :], route_ref, left_ref, sum_ref
    )
    for c in range(6):
        out_ref[c, 0:64, :] = sum_ref[c * 64 : (c + 1) * 64, 0:128]
        out_ref[c, 64:128, :] = sum_ref[c * 64 : (c + 1) * 64, 128:256]


def vmem(n):
    return [pl.BlockSpec(memory_space=pltpu.VMEM)] * n


def send_message(positions, route):
    return pl.pallas_call(
        send_kernel,
        out_shape=jax.ShapeDtypeStruct((6, 128, 128), f32),
        in_specs=vmem(2),
        out_specs=pl.BlockSpec(memory_space=pltpu.VMEM),
        scratch_shapes=[
            pltpu.VMEM((6, 64, 128), f32),
            pltpu.VMEM((768, 1024), bf16),
            pltpu.VMEM((384, 256), f32),
        ],
        compiler_params=pltpu.CompilerParams(vmem_limit_bytes=VMEM_LIMIT),
        name="send",
    )(positions, route)


def place_kernel(in_ref, order_ref, z_ref, out_ref, spec_ref, left_ref, sum_ref):
    scatter_rows(6, 128, lambda c, r: in_ref[c, pl.ds(r, 1), :], order_ref, left_ref, sum_ref)
    for c in range(6):
        out_ref[c, 0:64, :] = sum_ref[c * 64 : (c + 1) * 64, 0:128]
        out_ref[c, 64:128, :] = sum_ref[c * 64 : (c + 1) * 64, 128:256]
    for c in range(3):
        hi, lo = split2(out_ref[3 + c])
        kind = 0 if c < 2 else 1
        spec_ref[c] = dot3(z_ref[0, kind], z_ref[1, kind], hi, lo, dot_t)


def place_on_grid(incoming, order, z_table):
    return pl.pallas_call(
        place_kernel,
        out_shape=[
            jax.ShapeDtypeStruct((6, 128, 128), f32),
            jax.ShapeDtypeStruct((3, 128, 128), f32),
        ],
        in_specs=vmem(3),
        out_specs=vmem(2),
        scratch_shapes=[pltpu.VMEM((768, 1024), bf16), pltpu.VMEM((384, 256), f32)],
        compiler_params=pltpu.CompilerParams(vmem_limit_bytes=VMEM_LIMIT),
        name="place",
    )(incoming, order, z_table)


def wave_kernel(
    part_ref, in_ref, outer_ref, outer_back_ref, inner_ref, inner_back_ref, twist_ref,
    out_ref, mid_ref,
):
    freq, turn_re, turn_im, weight = (part_ref[i] for i in range(4))
    cos_t, sin_t = twist_ref[0], twist_ref[1]
    spectrum = []
    for c in range(3):
        hi, lo = split2(in_ref[c])
        both = dot3(outer_ref[0], outer_ref[1], hi, lo)
        re, im = both[0:128], both[128:256]
        mid_ref[:, 0:128] = re * cos_t + im * sin_t
        mid_ref[:, 128:256] = im * cos_t - re * sin_t
        hi, lo = split2(mid_ref[...])
        both = dot3(hi, lo, inner_ref[0], inner_ref[1])
        spectrum.append((both[:, 0:128], both[:, 128:256]))
    row = lax.broadcasted_iota(jnp.int32, (128, 128), 0)
    col = lax.broadcasted_iota(jnp.int32, (128, 128), 1)
    n_x = (row >> 3) + 16 * (col >> 4)
    n_y = (row & 7) + 8 * (col & 15)
    unit = 2.0 * math.pi / (G * grid_spacing)
    signed = lambda n: jnp.where(n < G // 2, n, n - G).astype(f32) * unit
    k_x, k_y = signed(n_x), signed(n_y)
    k_z = jnp.full((128, 128), freq * unit, f32)
    edge_x = jnp.where(n_x == G // 2, 1.0, 0.0)
    edge_y = jnp.where(n_y == G // 2, 1.0, 0.0)
    edge_z = jnp.where(jnp.full((128, 128), freq, f32) < -63.5, 1.0, 0.0)
    square = k_x * k_x + k_y * k_y + k_z * k_z
    positive = square > 0.0
    safe = jnp.where(positive, square, 1.0)
    green = jnp.where(
        positive,
        (1.0 - 0.25 * square / 3.0) * (1.0 + square) * jnp.exp(-square) / safe,
        0.0,
    ) * (weight / float(G**3))
    over = green / safe
    g_xy = jnp.where(edge_x == edge_y, -over * k_x * k_y, 0.0)
    g_xz = jnp.where(edge_x == edge_z, -over * k_x * k_z, 0.0)
    g_yz = jnp.where(edge_y == edge_z, -over * k_y * k_z, 0.0)
    g_xx = green - over * k_x * k_x
    g_yy = green - over * k_y * k_y
    g_zz = green - over * k_z * k_z
    (x_re, x_im), (y_re, y_im), (z_re, z_im) = spectrum
    z_re, z_im = turn_re * z_re - turn_im * z_im, turn_re * z_im + turn_im * z_re
    flow = [
        (g_xx * x_re + g_xy * y_re + g_xz * z_re, g_xx * x_im + g_xy * y_im + g_xz * z_im),
        (g_xy * x_re + g_yy * y_re + g_yz * z_re, g_xy * x_im + g_yy * y_im + g_yz * z_im),
    ]
    w_re = g_xz * x_re + g_yz * y_re + g_zz * z_re
    w_im = g_xz * x_im + g_yz * y_im + g_zz * z_im
    flow.append((turn_re * w_re + turn_im * w_im, turn_re * w_im - turn_im * w_re))
    for c in range(3):
        mid_ref[:, 0:128], mid_ref[:, 128:256] = flow[c]
        hi, lo = split2(mid_ref[...])
        both = dot3(hi, lo, inner_back_ref[0], inner_back_ref[1])
        re, im = both[:, 0:128], both[:, 128:256]
        hi, lo = split2(
            jnp.concatenate([re * cos_t - im * sin_t, im * cos_t + re * sin_t], axis=0)
        )
        out_ref[c] = dot3(outer_back_ref[0], outer_back_ref[1], hi, lo)


def wave_flow(spec, table, member):
    special = member % 64 == 63
    freq = jnp.where(member < 64, member + 1, (member - 63) % 64)
    freq = jnp.where(member == 63, -64, freq)
    side = jnp.where(member < 64, 1.0, -1.0)
    part = jnp.stack(
        [
            freq.astype(f32),
            jnp.where(special, 1.0, 0.0),
            jnp.where(special, 0.0, side),
            jnp.where(special, 1.0, 2.0),
        ]
    ).astype(f32)
    return pl.pallas_call(
        wave_kernel,
        out_shape=jax.ShapeDtypeStruct((3, 128, 128), f32),
        in_specs=[pl.BlockSpec(memory_space=pltpu.SMEM)] + vmem(6),
        out_specs=pl.BlockSpec(memory_space=pltpu.VMEM),
        scratch_shapes=[pltpu.VMEM((128, 256), f32)],
        compiler_params=pltpu.CompilerParams(vmem_limit_bytes=VMEM_LIMIT),
        name="wave",
    )(
        part, spec, table["outer"], table["outer_back"], table["inner"],
        table["inner_back"], table["twist"],
    )


ERFC_SHIFT = 4.0
ERFC_POLY = (
    -5.9986000529477224e-05, 1.1337793270330845, 4.308175452878655, 20.093023854033866,
    -8.594175483206275, 489.91788674098177, -1701.7584635921016, 1704.126720738659,
)


def pair_scalars(s2):
    u = lax.rsqrt(s2)
    gauss = jnp.exp2(s2 * (-0.25 * math.log2(math.e)))
    t = pl.reciprocal(s2 * u + ERFC_SHIFT, approx=True)
    w = ERFC_POLY[-1]
    for coefficient in ERFC_POLY[-2::-1]:
        w = w * t + coefficient
    u2 = u * u
    wu = w * u
    along = gauss * (wu * (0.0625 * u2 + 0.375) + 0.125)
    across = (gauss * u2) * (wu * (0.375 - 0.1875 * u2) - 0.125)
    return along, across


def pair_kernel(
    near_ref, far_ref, near_out_ref, far_out_ref, steps_ref, own_ref, beside_ref,
    own_vel_ref, far_vel_ref,
    weight_ref, left_ref, right_ref, acc_ref, weight_stage, left_stage, right_stage,
    s2_a, s2_b, tile_a, tile_b,
):
    lane = lax.broadcasted_iota(jnp.int32, (1, 128), 1)

    zero = jnp.zeros((128, 128), f32)
    one = jnp.ones((128, 128), f32)
    for side, ref in ((0, own_ref), (1, beside_ref)):
        x = [ref[c] for c in range(3)]
        f = [ref[3 + c] for c in range(3)]
        xf = x[0] * f[0] + x[1] * f[1] + x[2] * f[2]
        rows = f + [xf]
        rows += [x[a] * f[b] for a in range(3) for b in range(3)]
        rows += [x[a] * xf for a in range(3)]
        rows += f
        rows += [zero] * (W_ROWS - len(rows))
        for c, plane in enumerate(rows):
            weight_stage[pl.ds(side * 128 * W_ROWS + c, 128, stride=W_ROWS), :] = plane
        norm = x[0] * x[0] + x[1] * x[1] + x[2] * x[2]
        parts = [split3(v) for v in x]
        first, second = [], []
        for h, m, l in parts:
            first += [h, h, m, m, h, l]
            second += [h, m, h, m, l, h]
        second += [one] * 3 + list(split3(norm + 0.25))
        second += [zero] * (32 - len(second))
        for c, plane in enumerate(second):
            right_stage[pl.ds(side * 128 * 32 + c, 128, stride=32), :] = plane
        if side == 0:
            first = [-2.0 * v for v in first] + list(split3(norm)) + [one] * 3
            first += [zero] * (32 - len(first))
            for c, plane in enumerate(first):
                left_stage[pl.ds(c, 128, stride=32), :] = plane

    low_half = lane < 64

    def both_halves(v):
        other = pltpu.roll(v, 64, 1)
        return jnp.where(low_half, v, other), jnp.where(low_half, other, v)

    def build(r, _):
        w = weight_stage[pl.ds(pl.multiple_of(r * W_ROWS, 8), W_ROWS), :]
        for k, v in enumerate(both_halves(w)):
            hi = v.astype(bf16).astype(f32)
            lo = v - hi
            weight_ref[2 * r + k] = jnp.concatenate(
                [hi[0:16], lo[0:16], hi[16:24], lo[16:24]], axis=0
            ).astype(bf16)
        w = right_stage[pl.ds(pl.multiple_of(r * 32, 8), 32), :]
        for k, v in enumerate(both_halves(w)):
            right_ref[2 * r + k] = v.astype(bf16)
        return 0

    lax.fori_loop(0, 256, build, 0, unroll=4)

    eye = jnp.where(
        lax.broadcasted_iota(jnp.int32, (128, 128), 0)
        == lax.broadcasted_iota(jnp.int32, (128, 128), 1),
        1.0,
        0.0,
    ).astype(bf16)

    def turn_left(r, _):
        v = left_stage[pl.ds(pl.multiple_of(r * 32, 8), 32), :].astype(bf16)
        nodes = dot_t(eye, jnp.concatenate([v] * 4, axis=0)).astype(bf16)
        left_ref[2 * r] = nodes[0:64]
        left_ref[2 * r + 1] = nodes[64:128]
        return 0

    lax.fori_loop(0, 128, turn_left, 0, unroll=4)

    def clear(r, _):
        acc_ref[pl.ds(pl.multiple_of(r * W_ROWS, 8), W_ROWS), :] = jnp.zeros((W_ROWS, 128), f32)
        return 0

    lax.fori_loop(0, 2 * BLOCKS, clear, 0, unroll=8)

    slot_mask = [jnp.where((lane >> 5) == s, 1.0, 0.0).astype(bf16) for s in range(STEP)]
    half_mask = [jnp.where((lane >> 6) == s, 1.0, 0.0).astype(bf16) for s in range(2)]
    half_keep = [(lane >> 6) == s for s in range(2)]
    blank = jnp.zeros((64, 128), bf16)

    def distances(step, s2_ref):
        at = step * STEP
        left = sum(left_ref[near_ref[at + s]] * slot_mask[s] for s in range(STEP))
        right = [right_ref[far_ref[at + s]] * half_mask[s % 2] for s in range(STEP)]
        right = jnp.concatenate(
            [
                jnp.concatenate([right[0], right[1], blank], axis=0),
                jnp.concatenate([blank, right[2], right[3]], axis=0),
            ],
            axis=1,
        )
        s2_ref[...] = dot(left, right)

    def scalars(s2_ref, tile_ref):
        along, across = pair_scalars(s2_ref[...])
        for at, value in ((0, across), (128, along)):
            hi, lo = split2(value)
            tile_ref[at : at + 64, :] = hi
            tile_ref[at + 64 : at + 128, :] = lo

    def sums(step, tile_ref):
        at = step * STEP
        for half in range(2):
            tile_h = tile_ref[0:128, half * 128 : (half + 1) * 128]
            tile_f = tile_ref[128:256, half * 128 : (half + 1) * 128]
            pairs = [at + half * 2 + s for s in range(2)]
            a = [weight_ref[near_ref[p]] for p in pairs]
            b = [weight_ref[far_ref[p]] * half_mask[s] for s, p in enumerate(pairs)]
            to_far_h = dot(jnp.concatenate([v[0:32] for v in a], axis=0), tile_h)
            to_far_f = dot(jnp.concatenate([v[32:48] for v in a], axis=0), tile_f)
            to_near_h = dot_t(jnp.concatenate([v[0:32] for v in b], axis=0), tile_h)
            to_near_f = dot_t(jnp.concatenate([v[32:48] for v in b], axis=0), tile_f)
            for s, p in enumerate(pairs):
                for h, f, out_ref, keep in (
                    (to_near_h, to_near_f, near_out_ref, None),
                    (to_far_h, to_far_f, far_out_ref, half_keep[s]),
                ):
                    add_h = h[32 * s : 32 * s + 16] + h[32 * s + 16 : 32 * s + 32]
                    add_f = f[16 * s : 16 * s + 8] + f[16 * s + 8 : 16 * s + 16]
                    add = jnp.concatenate([add_h, add_f], axis=0)
                    if keep is not None:
                        add = jnp.where(keep, add, 0.0)
                    rows = pl.ds(pl.multiple_of(out_ref[p], 8), W_ROWS)
                    acc_ref[rows, :] += add

    steps = steps_ref[0]
    distances(0, s2_a)
    scalars(s2_a, tile_a)
    distances(1, s2_b)

    def body(j, _):
        k = 2 * j + 1
        distances(k + 1, s2_a)
        scalars(s2_b, tile_b)
        sums(k - 1, tile_a)
        distances(k + 2, s2_b)
        scalars(s2_a, tile_a)
        sums(k, tile_b)
        return 0

    lax.fori_loop(0, (steps + 1) // 2, body, 0)

    chunk = 32
    for side, ref, out_ref in ((0, own_ref, own_vel_ref), (1, beside_ref, far_vel_ref)):
        for top in range(0, 128, chunk):
            base = (side * 256 + 2 * top) * W_ROWS
            planes = []
            for c in range(19):
                even = acc_ref[pl.ds(base + c, chunk, stride=2 * W_ROWS), :]
                odd = acc_ref[pl.ds(base + W_ROWS + c, chunk, stride=2 * W_ROWS), :]
                even = even + pltpu.roll(even, 64, 1)
                odd = odd + pltpu.roll(odd, 64, 1)
                planes.append(jnp.where(low_half, even, odd))
            x = [ref[c, top : top + chunk, :] for c in range(3)]
            h_f, h_xf, h_x_f, h_x_xf, along = (
                planes[0:3], planes[3], planes[4:13], planes[13:16], planes[16:19],
            )
            x_h_f = x[0] * h_f[0] + x[1] * h_f[1] + x[2] * h_f[2] - h_xf
            for c in range(3):
                out_ref[c, top : top + chunk, :] = (
                    along[c]
                    + x[c] * x_h_f
                    - (x[0] * h_x_f[3 * c] + x[1] * h_x_f[3 * c + 1] + x[2] * h_x_f[3 * c + 2])
                    + h_x_xf[c]
                )


def pair_velocities(own, beside, first_list, second_list, count):
    pad = 16
    place = jnp.arange(PAIRS, dtype=jnp.int32)
    live = place < count
    near_out = jnp.where(live, first_list, TRASH) * W_ROWS
    far_out = jnp.where(live & (first_list != second_list), second_list, TRASH) * W_ROWS
    near = jnp.pad(first_list, (0, pad))
    far = jnp.pad(second_list, (0, pad))
    near_out = jnp.pad(near_out, (0, pad), constant_values=TRASH * W_ROWS)
    far_out = jnp.pad(far_out, (0, pad), constant_values=TRASH * W_ROWS)
    steps = ((count + STEP - 1) // STEP).reshape(1)
    plane = jax.ShapeDtypeStruct((3, 128, 128), f32)
    return pl.pallas_call(
        pair_kernel,
        out_shape=[plane, plane],
        in_specs=[pl.BlockSpec(memory_space=pltpu.SMEM)] * 5 + vmem(2),
        out_specs=vmem(2),
        scratch_shapes=[
            pltpu.VMEM((2 * BLOCKS, 48, 128), bf16),
            pltpu.VMEM((BLOCKS, 64, 128), bf16),
            pltpu.VMEM((2 * BLOCKS, 32, 128), bf16),
            pltpu.VMEM(((2 * BLOCKS + 1) * W_ROWS, 128), f32),
            pltpu.VMEM((256 * W_ROWS, 128), f32),
            pltpu.VMEM((128 * 32, 128), f32),
            pltpu.VMEM((256 * 32, 128), f32),
            pltpu.VMEM((64, 256), f32),
            pltpu.VMEM((64, 256), f32),
            pltpu.VMEM((256, 256), bf16),
            pltpu.VMEM((256, 256), bf16),
        ],
        compiler_params=pltpu.CompilerParams(vmem_limit_bytes=VMEM_LIMIT),
        name="pairs",
    )(near, far, near_out, far_out, steps, own, beside)


def reply_kernel(own_ref, far_ref, wave_ref, order_ref, z_ref, out_ref, hi_ref, lo_ref):
    for c in range(3):
        kind = 0 if c < 2 else 1
        hi, lo = split2(jnp.transpose(wave_ref[c]))
        wave = dot3(hi, lo, z_ref[0, kind], z_ref[1, kind])
        fill_table(c, own_ref[c] + far_ref[c] + wave, hi_ref, lo_ref)

    def put(c, r, row):
        out_ref[c, pl.ds(r, 1), :] = row

    gather_rows(3, 128, hi_ref, lo_ref, order_ref, put)


def reply_message(own_vel, far_vel, wave, order, z_table):
    return pl.pallas_call(
        reply_kernel,
        out_shape=jax.ShapeDtypeStruct((3, 128, 128), f32),
        in_specs=vmem(5),
        out_specs=pl.BlockSpec(memory_space=pltpu.VMEM),
        scratch_shapes=[pltpu.VMEM((192, 256), bf16), pltpu.VMEM((192, 256), bf16)],
        compiler_params=pltpu.CompilerParams(vmem_limit_bytes=VMEM_LIMIT),
        name="reply",
    )(own_vel, far_vel, wave, order, z_table)


def move_kernel(in_ref, route_ref, pos_ref, noise_ref, moved_ref, drift_ref, hi_ref, lo_ref, vel_ref):
    rows = route_ref.shape[0]
    for c in range(3):
        fill_table(c, in_ref[c], hi_ref, lo_ref)

    def put(c, r, row):
        vel_ref[c, pl.ds(r, 1), :] = row

    gather_rows(3, rows, hi_ref, lo_ref, route_ref, put)
    for c in range(3):
        for r in range(rows):
            drift_ref[c : c + 1, r * 128 : (r + 1) * 128] = time_step * vel_ref[c, r : r + 1, :]
    moved_ref[...] = pos_ref[...] + drift_ref[...] + noise_ref[...]


def move_beads(arrived, route, positions, noise):
    flat = jax.ShapeDtypeStruct(positions.shape, f32)
    return pl.pallas_call(
        move_kernel,
        out_shape=[flat, flat],
        in_specs=vmem(4),
        out_specs=vmem(2),
        scratch_shapes=[
            pltpu.VMEM((192, 256), bf16),
            pltpu.VMEM((192, 256), bf16),
            pltpu.VMEM((3, 64, 128), f32),
        ],
        compiler_params=pltpu.CompilerParams(vmem_limit_bytes=VMEM_LIMIT),
        name="move",
    )(arrived, route, positions, noise)


def shifted(value, axis, by):
    devices = lax.axis_size(axis)
    return lax.ppermute(value, axis, [(i, (i + by) % devices) for i in range(devices)])


def exchange(value):
    return lax.all_to_all(value, ("gx", "gy"), split_axis=1, concat_axis=1, tiled=True)


def shards(positions, noise, route, node_perm, pair_first, pair_second, pair_count):
    table = {name: jnp.asarray(value) for name, value in tables().items()}
    row_gx = lax.axis_index("gx")
    member = row_gx * lax.axis_size("gy") + lax.axis_index("gy")
    route = route.reshape(64, 128)
    order = lax.dynamic_index_in_dim(node_perm, row_gx, 0, keepdims=False).reshape(128, 128)
    incoming = exchange(send_message(positions, route))
    grid, spec = place_on_grid(incoming, order, table["z"])
    beside = shifted(grid, "gx", -1)
    wave = exchange(wave_flow(exchange(spec), table, member))
    own_vel, far_vel = pair_velocities(
        grid, beside, pair_first[0], pair_second[0], pair_count[0]
    )
    far_vel = shifted(far_vel, "gx", 1)
    reply = exchange(reply_message(own_vel, far_vel, wave, order, table["z"]))
    return tuple(move_beads(reply, route, positions, noise))


def solution(mesh):
    in_specs = (
        P(None, ("gx", "gy")),
        P(None, ("gx", "gy")),
        P(("gx", "gy")),
        P(None, "gy", None),
        P(("gx", "gy"), None),
        P(("gx", "gy"), None),
        P(("gx", "gy")),
    )
    out_specs = (P(None, ("gx", "gy")), P(None, ("gx", "gy")))
    return jax.shard_map(shards, mesh=mesh, in_specs=in_specs, out_specs=out_specs, check_vma=False)
```

```python
from functools import partial
import math

import numpy as np
import jax
import jax.numpy as jnp
from jax import lax
from jax.experimental import pallas as pl
from jax.experimental.pallas import tpu as pltpu
from jax.sharding import PartitionSpec as P

G = 128
BLOCKS = 256
PAIRS = 1024
STEP = 4
W_ROWS = 24
GROUPS = 2
FEATURES = 24

fene_k = 30.0
fene_reach = 1.5
bend_k = 2.0
time_step = 0.01
grid_spacing = 4.0

f32 = jnp.float32
bf16 = jnp.bfloat16
VMEM_LIMIT = 24 * 1024 * 1024
SMALL_VMEM = 24 * 1024 * 1024


def dot(a, b):
    return lax.dot_general(a, b, (((1,), (0,)), ((), ())), preferred_element_type=f32)


def dot_t(a, b):
    return lax.dot_general(a, b, (((1,), (1,)), ((), ())), preferred_element_type=f32)


def split2(x):
    hi = x.astype(bf16)
    return hi, (x - hi.astype(f32)).astype(bf16)


def split3(x):
    hi = x.astype(bf16).astype(f32)
    rest = x - hi
    mid = rest.astype(bf16).astype(f32)
    return hi, mid, (rest - mid).astype(bf16).astype(f32)


def dot3(a_hi, a_lo, b_hi, b_lo, form=dot):
    return form(a_hi, b_hi) + form(a_hi, b_lo) + form(a_lo, b_hi)


def split_table(table):
    table = np.asarray(table, np.float64)
    hi = table.astype(np.float32).astype(jnp.bfloat16)
    lo = (table - hi.astype(np.float64)).astype(np.float32).astype(jnp.bfloat16)
    return np.stack([hi, lo])


def tables():
    n = np.arange(G)
    turn = 2.0 * np.pi / G
    member = np.arange(128)
    freq = np.where(member < 64, member + 1, (member - 63) % 64)
    wave = turn * (freq[:, None] * n[None, :] % G)
    even, odd = np.cos(wave), -np.sin(wave)
    special = (member % 64) == 63
    first = (member < 64)[:, None]
    even = np.where(special[:, None], np.cos(wave), even)
    z_xy = np.where(special[:, None] | first, even, odd)
    z_z = np.where(special[:, None] | ~first, even, odd)
    k1, k2 = n // 8, n % 8
    outer = 2.0 * np.pi * (k1[:, None] * k1[None, :] / 16.0 + k2[:, None] * k2[None, :] / 8.0)
    a, b = n // 16, n % 16
    inner = 2.0 * np.pi * (a[:, None] * a[None, :] / 8.0 + b[:, None] * b[None, :] / 16.0)
    twist = turn * (k1[:, None] * a[None, :] + k2[:, None] * b[None, :])
    c_out, s_out, c_in, s_in = np.cos(outer), np.sin(outer), np.cos(inner), np.sin(inner)
    return {
        "z": split_table(np.stack([z_xy, z_z])),
        "outer": split_table(np.concatenate([c_out, -s_out], 0)),
        "outer_back": split_table(np.concatenate([c_out, -s_out], 1)),
        "inner": split_table(np.block([[c_in, -s_in], [s_in, c_in]])),
        "inner_back": split_table(np.block([[c_in, s_in], [-s_in, c_in]])),
        "twist": np.stack([np.cos(twist), np.sin(twist)]).astype(np.float32),
    }


def cost(micros):
    return pl.CostEstimate(flops=int(micros * 1e9), bytes_accessed=1 << 20, transcendentals=0)


def onehot(index, size, width):
    rows = lax.broadcasted_iota(jnp.int32, (size, width), 0)
    return jnp.where(rows == index, 1.0, 0.0).astype(bf16)


def high_part(place):
    return (place >> 7) & 63


def low_part(place):
    return ((place >> 13) << 7) | (place & 127)


def scatter_rows(channels, rows, value_row, place_ref, left_ref, sum_ref):
    group = left_ref.shape[1] // 128
    span = 128 * group

    def turn(g, _):
        low = []
        for j in range(group):
            place = place_ref[pl.ds(g * group + j, 1), :]
            high_hot = onehot(high_part(place), 64, 128)
            low.append(onehot(low_part(place), 256, 128))
            for c in range(channels):
                hi, lo = split2(value_row(c, g * group + j))
                left_ref[c * 128 : c * 128 + 64, j * 128 : (j + 1) * 128] = high_hot * hi
                left_ref[c * 128 + 64 : c * 128 + 128, j * 128 : (j + 1) * 128] = high_hot * lo
        moved = dot_t(left_ref[...], jnp.concatenate(low, axis=1))
        for c in range(channels):
            sum_ref[c * 64 : (c + 1) * 64, :] += (
                moved[c * 128 : c * 128 + 64] + moved[c * 128 + 64 : c * 128 + 128]
            )
        return 0

    sum_ref[...] = jnp.zeros_like(sum_ref)
    lax.fori_loop(0, rows // group, turn, 0)


def gather_rows(channels, rows, table_hi_ref, table_lo_ref, place_ref, put):
    width = 4

    def turn(g, _):
        low, high = [], []
        for j in range(width):
            place = place_ref[pl.ds(g * width + j, 1), :]
            low.append(onehot(low_part(place), 256, 128))
            high.append(high_part(place))
        low = jnp.concatenate(low, axis=1)
        high = jnp.concatenate(high, axis=1)
        found = dot(table_hi_ref[...], low) + dot(table_lo_ref[...], low)
        rows_of = lax.broadcasted_iota(jnp.int32, (64, width * 128), 0) == high
        for c in range(channels):
            got = jnp.sum(
                jnp.where(rows_of, found[c * 64 : (c + 1) * 64], 0.0), axis=0, keepdims=True
            )
            for j in range(width):
                put(c, g * width + j, got[:, j * 128 : (j + 1) * 128])
        return 0

    lax.fori_loop(0, rows // width, turn, 0)


def fill_table(c, plane, table_hi_ref, table_lo_ref):
    hi, lo = split2(plane)
    for ref, part in ((table_hi_ref, hi), (table_lo_ref, lo)):
        ref[c * 64 : (c + 1) * 64, 0:128] = part[0:64]
        ref[c * 64 : (c + 1) * 64, 128:256] = part[64:128]


def chain_forces(x):
    lane = lax.broadcasted_iota(jnp.int32, x[0].shape, 1) & 63
    last = lane == 63
    ahead = lambda v: pltpu.roll(v, 127, 1)
    behind = lambda v: pltpu.roll(v, 1, 1)
    bond = [jnp.where(last, 0.5, ahead(v) - v) for v in x]
    square = bond[0] * bond[0] + bond[1] * bond[1] + bond[2] * bond[2]
    inverse = lax.rsqrt(square)
    unit = [v * inverse for v in bond]
    following = [ahead(v) for v in unit]
    cosine = unit[0] * following[0] + unit[1] * following[1] + unit[2] * following[2]
    bends = lane < 62
    stretch = fene_k / (1.0 - square / fene_reach**2)
    before = behind(jnp.where(bends, 1.0, 0.0))
    cosine_before = behind(cosine)
    grad = []
    for c in range(3):
        pull = jnp.where(bends, following[c] - cosine * unit[c], 0.0)
        push = before * (behind(unit[c]) - cosine_before * unit[c])
        push = jnp.where(lane == 0, 0.0, push)
        grad.append(
            jnp.where(last, 0.0, stretch * bond[c] - bend_k * inverse * (pull + push))
        )
    return [g - jnp.where(lane == 0, 0.0, behind(g)) for g in grad]


def send_kernel(pos_ref, route_ref, out_ref, plane_ref, left_ref, sum_ref):
    rows = route_ref.shape[0]
    for c in range(3):
        for r in range(rows):
            plane_ref[c, r : r + 1, :] = pos_ref[c : c + 1, r * 128 : (r + 1) * 128]
    forces = chain_forces([plane_ref[c] for c in range(3)])
    for c in range(3):
        plane_ref[3 + c] = forces[c]
    scatter_rows(
        6, rows, lambda c, r: plane_ref[c, pl.ds(r, 1), :], route_ref, left_ref, sum_ref
    )
    for c in range(6):
        out_ref[0:64, c, :] = sum_ref[c * 64 : (c + 1) * 64, 0:128]
        out_ref[64:128, c, :] = sum_ref[c * 64 : (c + 1) * 64, 128:256]


def vmem(n):
    return [pl.BlockSpec(memory_space=pltpu.VMEM)] * n


def send_message(positions, route):
    return pl.pallas_call(
        send_kernel,
        out_shape=jax.ShapeDtypeStruct((128, 6, 128), f32),
        in_specs=vmem(2),
        out_specs=pl.BlockSpec(memory_space=pltpu.VMEM),
        scratch_shapes=[
            pltpu.VMEM((6, 64, 128), f32),
            pltpu.VMEM((768, 1024), bf16),
            pltpu.VMEM((384, 256), f32),
        ],
        compiler_params=pltpu.CompilerParams(vmem_limit_bytes=VMEM_LIMIT),
        name="send",
    )(positions, route)


def place_kernel(in_ref, order_ref, z_ref, out_ref, spec_ref, left_ref, sum_ref):
    scatter_rows(6, 128, lambda c, r: in_ref[r, c : c + 1, :], order_ref, left_ref, sum_ref)
    for c in range(6):
        out_ref[c, 0:64, :] = sum_ref[c * 64 : (c + 1) * 64, 0:128]
        out_ref[c, 64:128, :] = sum_ref[c * 64 : (c + 1) * 64, 128:256]
    for c in range(3):
        hi, lo = split2(out_ref[3 + c])
        kind = 0 if c < 2 else 1
        spec_ref[:, c, :] = dot3(z_ref[0, kind], z_ref[1, kind], hi, lo, dot_t)


def place_on_grid(incoming, order, z_table):
    return pl.pallas_call(
        place_kernel,
        out_shape=[
            jax.ShapeDtypeStruct((6, 128, 128), f32),
            jax.ShapeDtypeStruct((128, 3, 128), f32),
        ],
        in_specs=vmem(3),
        out_specs=vmem(2),
        scratch_shapes=[pltpu.VMEM((768, 1024), bf16), pltpu.VMEM((384, 256), f32)],
        compiler_params=pltpu.CompilerParams(vmem_limit_bytes=VMEM_LIMIT),
        name="place",
    )(incoming, order, z_table)


def wave_kernel(
    part_ref, in_ref, outer_ref, outer_back_ref, inner_ref, inner_back_ref, twist_ref,
    out_ref, mid_ref,
):
    freq, turn_re, turn_im, weight = (part_ref[i] for i in range(4))
    cos_t, sin_t = twist_ref[0], twist_ref[1]
    spectrum = []
    for c in range(3):
        hi, lo = split2(in_ref[:, c, :])
        both = dot3(outer_ref[0], outer_ref[1], hi, lo)
        re, im = both[0:128], both[128:256]
        mid_ref[:, 0:128] = re * cos_t + im * sin_t
        mid_ref[:, 128:256] = im * cos_t - re * sin_t
        hi, lo = split2(mid_ref[...])
        both = dot3(hi, lo, inner_ref[0], inner_ref[1])
        spectrum.append((both[:, 0:128], both[:, 128:256]))
    row = lax.broadcasted_iota(jnp.int32, (128, 128), 0)
    col = lax.broadcasted_iota(jnp.int32, (128, 128), 1)
    n_x = (row >> 3) + 16 * (col >> 4)
    n_y = (row & 7) + 8 * (col & 15)
    unit = 2.0 * math.pi / (G * grid_spacing)
    signed = lambda n: jnp.where(n < G // 2, n, n - G).astype(f32) * unit
    k_x, k_y = signed(n_x), signed(n_y)
    k_z = jnp.full((128, 128), freq * unit, f32)
    edge_x = jnp.where(n_x == G // 2, 1.0, 0.0)
    edge_y = jnp.where(n_y == G // 2, 1.0, 0.0)
    edge_z = jnp.where(jnp.full((128, 128), freq, f32) < -63.5, 1.0, 0.0)
    square = k_x * k_x + k_y * k_y + k_z * k_z
    positive = square > 0.0
    safe = jnp.where(positive, square, 1.0)
    green = jnp.where(
        positive,
        (1.0 - 0.25 * square / 3.0) * (1.0 + square) * jnp.exp(-square) / safe,
        0.0,
    ) * (weight / float(G**3))
    over = green / safe
    g_xy = jnp.where(edge_x == edge_y, -over * k_x * k_y, 0.0)
    g_xz = jnp.where(edge_x == edge_z, -over * k_x * k_z, 0.0)
    g_yz = jnp.where(edge_y == edge_z, -over * k_y * k_z, 0.0)
    g_xx = green - over * k_x * k_x
    g_yy = green - over * k_y * k_y
    g_zz = green - over * k_z * k_z
    (x_re, x_im), (y_re, y_im), (z_re, z_im) = spectrum
    z_re, z_im = turn_re * z_re - turn_im * z_im, turn_re * z_im + turn_im * z_re
    flow = [
        (g_xx * x_re + g_xy * y_re + g_xz * z_re, g_xx * x_im + g_xy * y_im + g_xz * z_im),
        (g_xy * x_re + g_yy * y_re + g_yz * z_re, g_xy * x_im + g_yy * y_im + g_yz * z_im),
    ]
    w_re = g_xz * x_re + g_yz * y_re + g_zz * z_re
    w_im = g_xz * x_im + g_yz * y_im + g_zz * z_im
    flow.append((turn_re * w_re + turn_im * w_im, turn_re * w_im - turn_im * w_re))
    for c in range(3):
        mid_ref[:, 0:128], mid_ref[:, 128:256] = flow[c]
        hi, lo = split2(mid_ref[...])
        both = dot3(hi, lo, inner_back_ref[0], inner_back_ref[1])
        re, im = both[:, 0:128], both[:, 128:256]
        hi, lo = split2(
            jnp.concatenate([re * cos_t - im * sin_t, im * cos_t + re * sin_t], axis=0)
        )
        out_ref[:, c, :] = dot3(outer_back_ref[0], outer_back_ref[1], hi, lo)


def wave_flow(spec, table, member):
    special = member % 64 == 63
    freq = jnp.where(member < 64, member + 1, (member - 63) % 64)
    freq = jnp.where(member == 63, -64, freq)
    side = jnp.where(member < 64, 1.0, -1.0)
    part = jnp.stack(
        [
            freq.astype(f32),
            jnp.where(special, 1.0, 0.0),
            jnp.where(special, 0.0, side),
            jnp.where(special, 1.0, 2.0),
        ]
    ).astype(f32)
    return pl.pallas_call(
        wave_kernel,
        out_shape=jax.ShapeDtypeStruct((128, 3, 128), f32),
        in_specs=[pl.BlockSpec(memory_space=pltpu.SMEM)] + vmem(6),
        out_specs=pl.BlockSpec(memory_space=pltpu.VMEM),
        scratch_shapes=[pltpu.VMEM((128, 256), f32)],
        compiler_params=pltpu.CompilerParams(vmem_limit_bytes=VMEM_LIMIT),
        name="wave",
    )(
        part, spec, table["outer"], table["outer_back"], table["inner"],
        table["inner_back"], table["twist"],
    )


ERFC_SHIFT = 4.0
ERFC_POLY = (
    -5.9986000529477224e-05, 1.1337793270330845, 4.308175452878655, 20.093023854033866,
    -8.594175483206275, 489.91788674098177, -1701.7584635921016, 1704.126720738659,
)


def pair_scalars(s2):
    u = lax.rsqrt(s2)
    gauss = jnp.exp2(s2 * (-0.25 * math.log2(math.e)))
    t = pl.reciprocal(s2 * u + ERFC_SHIFT, approx=True)
    w = ERFC_POLY[-1]
    for coefficient in ERFC_POLY[-2::-1]:
        w = w * t + coefficient
    u2 = u * u
    wu = w * u
    along = gauss * (wu * (0.0625 * u2 + 0.375) + 0.125)
    across = (gauss * u2) * (wu * (0.375 - 0.1875 * u2) - 0.125)
    return along, across


def both_halves(v):
    low_half = lax.broadcasted_iota(jnp.int32, (1, 128), 1) < 64
    other = pltpu.roll(v, 64, 1)
    return jnp.where(low_half, v, other), jnp.where(low_half, other, v)


def stage_nodes(ref, weight_stage, right_stage):
    x = [ref[c] for c in range(3)]
    f = [ref[3 + c] for c in range(3)]
    xf = x[0] * f[0] + x[1] * f[1] + x[2] * f[2]
    rows = f + [xf]
    rows += [x[a] * f[b] for a in range(3) for b in range(3)]
    rows += [x[a] * xf for a in range(3)]
    for c, plane in enumerate(rows):
        weight_stage[pl.ds(c, 128, stride=16), :] = plane
    norm = x[0] * x[0] + x[1] * x[1] + x[2] * x[2]
    first, second = [], []
    for h, m, l in [split3(v) for v in x]:
        first += [h, h, m, m, h, l]
        second += [h, m, h, m, l, h]
    one = jnp.ones((128, 128), f32)
    first = [-2.0 * v for v in first] + list(split3(norm)) + [one] * 3
    second += [one] * 3 + list(split3(norm + 0.25))
    for c, plane in enumerate(second):
        right_stage[pl.ds(c, 128, stride=FEATURES), :] = plane
    return first


def build_tables(base, weight_stage, right_stage, weight_ref, right_ref):
    blank = jnp.zeros((32 - FEATURES, 128), f32)

    def build(r, _):
        w = weight_stage[pl.ds(pl.multiple_of(r * 16, 8), 16), :]
        for k, v in enumerate(both_halves(w)):
            hi = v.astype(bf16)
            lo = (v - hi.astype(f32)).astype(bf16)
            weight_ref[base + 2 * r + k] = jnp.concatenate([hi, lo], axis=0)
        w = right_stage[pl.ds(pl.multiple_of(r * FEATURES, 8), FEATURES), :]
        for k, v in enumerate(both_halves(w)):
            right_ref[base + 2 * r + k] = jnp.concatenate([v, blank], axis=0).astype(bf16)
        return 0

    lax.fori_loop(0, 128, build, 0, unroll=16)


def own_tables_kernel(
    own_ref, weight_ref, right_ref, left_ref, weight_stage, right_stage, left_stage
):
    first = stage_nodes(own_ref, weight_stage, right_stage)
    for c, plane in enumerate(first):
        left_stage[pl.ds(c, 128, stride=FEATURES), :] = plane
    eye = jnp.where(
        lax.broadcasted_iota(jnp.int32, (128, 128), 0)
        == lax.broadcasted_iota(jnp.int32, (128, 128), 1),
        1.0,
        0.0,
    ).astype(bf16)
    blank = jnp.zeros((32 - FEATURES, 128), f32)

    def turn_left(r, _):
        v = left_stage[pl.ds(pl.multiple_of(r * FEATURES, 8), FEATURES), :]
        v = jnp.concatenate([v, blank], axis=0).astype(bf16)
        nodes = dot_t(eye, jnp.concatenate([v] * 4, axis=0)).astype(bf16)
        left_ref[2 * r] = nodes[0:64]
        left_ref[2 * r + 1] = nodes[64:128]
        return 0

    lax.fori_loop(0, 128, turn_left, 0, unroll=8)
    build_tables(0, weight_stage, right_stage, weight_ref, right_ref)


def beside_tables_kernel(
    beside_ref, weight_in, right_in, weight_ref, right_ref, weight_stage, right_stage
):
    stage_nodes(beside_ref, weight_stage, right_stage)
    build_tables(BLOCKS, weight_stage, right_stage, weight_ref, right_ref)


WEIGHT_TABLE = jax.ShapeDtypeStruct((2 * BLOCKS, 32, 128), bf16)
RIGHT_TABLE = jax.ShapeDtypeStruct((2 * BLOCKS, 32, 128), bf16)
LEFT_TABLE = jax.ShapeDtypeStruct((BLOCKS, 64, 128), bf16)


def own_tables(own):
    return pl.pallas_call(
        own_tables_kernel,
        out_shape=[WEIGHT_TABLE, RIGHT_TABLE, LEFT_TABLE],
        in_specs=vmem(1),
        out_specs=vmem(3),
        scratch_shapes=[
            pltpu.VMEM((128 * 16, 128), f32),
            pltpu.VMEM((128 * FEATURES, 128), f32),
            pltpu.VMEM((128 * FEATURES, 128), f32),
        ],
        compiler_params=pltpu.CompilerParams(vmem_limit_bytes=SMALL_VMEM),
        cost_estimate=cost(8),
        name="own_tables",
    )(own)


def beside_tables(beside, weight, right):
    return pl.pallas_call(
        beside_tables_kernel,
        out_shape=[WEIGHT_TABLE, RIGHT_TABLE],
        in_specs=vmem(1) + [pl.BlockSpec(memory_space=pl.ANY)] * 2,
        out_specs=vmem(2),
        input_output_aliases={1: 0, 2: 1},
        scratch_shapes=[
            pltpu.VMEM((128 * 16, 128), f32),
            pltpu.VMEM((128 * FEATURES, 128), f32),
        ],
        compiler_params=pltpu.CompilerParams(vmem_limit_bytes=SMALL_VMEM),
        cost_estimate=cost(4),
        name="beside_tables",
    )(beside, weight, right)


def pair_kernel(
    list_ref, count_ref, weight_ref, right_ref, left_ref, own_ref, beside_ref,
    own_vel_ref, far_vel_ref, near_acc, far_acc, s2_a, s2_b, tile_a, tile_b,
):
    lane = lax.broadcasted_iota(jnp.int32, (1, 128), 1)
    low_half = lane < 64
    count = count_ref[0]

    def clear(r, _):
        blank = jnp.zeros((W_ROWS, 128), f32)
        far_acc[pl.ds(pl.multiple_of(r * 2 * W_ROWS, 8), W_ROWS), :] = blank
        far_acc[pl.ds(pl.multiple_of(r * 2 * W_ROWS + W_ROWS, 8), W_ROWS), :] = blank
        near_acc[pl.ds(pl.multiple_of(r * W_ROWS, 8), W_ROWS), :] = blank
        return 0

    lax.fori_loop(0, BLOCKS, clear, 0, unroll=8)

    wide = lax.broadcasted_iota(jnp.int32, (64, 128), 1)
    wide_low = wide < 64
    wide_even = (wide & 32) == 0
    narrow = lax.broadcasted_iota(jnp.int32, (32, 128), 1) < 64
    nothing = jnp.zeros((32, 128), bf16)

    def half_of(v, half):
        return jnp.where(narrow, nothing, v) if half else jnp.where(narrow, v, nothing)

    half_keep = [(lane >> 6) == s for s in range(2)]
    blank = jnp.zeros((64, 128), bf16)

    def blocks_of(pair):
        return list_ref[0, pair], list_ref[1, pair]

    def distance_dots(step):
        found = []
        for g in range(GROUPS):
            pairs = [blocks_of((step * GROUPS + g) * STEP + s) for s in range(STEP)]
            left = [left_ref[pairs[s][0]] for s in range(STEP)]
            left = jnp.where(
                wide_low,
                jnp.where(wide_even, left[0], left[1]),
                jnp.where(wide_even, left[2], left[3]),
            )
            right = [half_of(right_ref[pairs[s][1]], s % 2) for s in range(STEP)]
            right = jnp.concatenate(
                [
                    jnp.concatenate([right[0], right[1], blank], axis=0),
                    jnp.concatenate([blank, right[2], right[3]], axis=0),
                ],
                axis=1,
            )
            found.append(dot(left, right))
        return found

    def scalars(s2_ref, tile_ref, pack):
        half = pack % 2
        along, across = pair_scalars(s2_ref[pack // 2, :, half * 128 : (half + 1) * 128])
        for at, value in ((0, across), (128, along)):
            hi, lo = split2(value)
            tile_ref[pack, at : at + 64, :] = hi
            tile_ref[pack, at + 64 : at + 128, :] = lo

    def sum_dots(step, tile_ref, pack):
        tile = tile_ref[pack]
        pairs = [blocks_of((step * 2 * GROUPS + pack) * 2 + s) for s in range(2)]
        a = jnp.concatenate([weight_ref[i] for i, _ in pairs], axis=0)
        b = jnp.concatenate(
            [half_of(weight_ref[j], s) for s, (_, j) in enumerate(pairs)], axis=0
        )
        to_far = dot(a, jnp.concatenate([tile[0:128], tile[128:256]], axis=1))
        return dot_t(b, tile), to_far

    def add_sums(step, pack, to_near, to_far):
        for s in range(2):
            number = (step * 2 * GROUPS + pack) * 2 + s
            for out, acc_ref, row, keep in (
                (to_near, near_acc, list_ref[2, number], None),
                (to_far, far_acc, list_ref[3, number], half_keep[s]),
            ):
                top = 32 * s
                add_h = out[top : top + 16, 0:128] + out[top + 16 : top + 32, 0:128]
                add_f = out[top : top + 8, 128:256] + out[top + 16 : top + 24, 128:256]
                add = jnp.concatenate([add_h, add_f], axis=0)
                if keep is not None:
                    add = jnp.where(keep, add, 0.0)
                acc_ref[pl.ds(pl.multiple_of(row, 8), W_ROWS), :] += add

    packs = range(2 * GROUPS)

    def keep_distances(found, s2_ref):
        for g in range(GROUPS):
            s2_ref[g] = found[g]

    def stage(k, s2_next, s2_now, tile_now, tile_last):
        for pack in packs:
            scalars(s2_now, tile_now, pack)
        for pack in packs:
            add_sums(k - 1, pack, *sum_dots(k - 1, tile_last, pack))
        keep_distances(distance_dots(k + 1), s2_next)

    steps = (count + (STEP * GROUPS - 1)) // (STEP * GROUPS)
    keep_distances(distance_dots(0), s2_a)
    for pack in packs:
        scalars(s2_a, tile_a, pack)
    keep_distances(distance_dots(1), s2_b)

    def body(j, _):
        k = 2 * j + 1
        stage(k, s2_a, s2_b, tile_b, tile_a)
        stage(k + 1, s2_b, s2_a, tile_a, tile_b)
        return 0

    lax.fori_loop(0, (steps + 1) // 2, body, 0)

    chunk = 32
    for side, ref, out_ref in ((0, own_ref, own_vel_ref), (1, beside_ref, far_vel_ref)):
        for top in range(0, 128, chunk):
            planes = []
            for c in range(19):
                at = (2 * top) * W_ROWS + c
                even = far_acc[pl.ds(side * BLOCKS * W_ROWS + at, chunk, stride=2 * W_ROWS), :]
                at += W_ROWS
                odd = far_acc[pl.ds(side * BLOCKS * W_ROWS + at, chunk, stride=2 * W_ROWS), :]
                if side == 0:
                    even += near_acc[pl.ds(at - W_ROWS, chunk, stride=2 * W_ROWS), :]
                    odd += near_acc[pl.ds(at, chunk, stride=2 * W_ROWS), :]
                even = even + pltpu.roll(even, 64, 1)
                odd = odd + pltpu.roll(odd, 64, 1)
                planes.append(jnp.where(low_half, even, odd))
            x = [ref[c, top : top + chunk, :] for c in range(3)]
            h_f, h_xf, h_x_f, h_x_xf, along = (
                planes[0:3], planes[3], planes[4:13], planes[13:16], planes[16:19],
            )
            x_h_f = x[0] * h_f[0] + x[1] * h_f[1] + x[2] * h_f[2] - h_xf
            for c in range(3):
                out_ref[c, top : top + chunk, :] = (
                    along[c]
                    + x[c] * x_h_f
                    - (x[0] * h_x_f[3 * c] + x[1] * h_x_f[3 * c + 1] + x[2] * h_x_f[3 * c + 2])
                    + h_x_xf[c]
                )


def pair_lists(first_list, second_list, count):
    live = jnp.arange(PAIRS, dtype=jnp.int32) < count
    lists = jnp.stack(
        [
            first_list,
            second_list,
            jnp.where(live, first_list, BLOCKS) * W_ROWS,
            jnp.where(live & (first_list != second_list), second_list, 2 * BLOCKS) * W_ROWS,
        ]
    )
    spare = jnp.array([0, 0, BLOCKS * W_ROWS, 2 * BLOCKS * W_ROWS], jnp.int32)
    return jnp.concatenate([lists, jnp.broadcast_to(spare[:, None], (4, 128))], axis=1)


def pair_velocities(own, beside, tables_of, lists, count):
    plane = jax.ShapeDtypeStruct((3, 128, 128), f32)
    return pl.pallas_call(
        pair_kernel,
        out_shape=[plane, plane],
        in_specs=[pl.BlockSpec(memory_space=pltpu.SMEM)] * 2 + vmem(5),
        out_specs=vmem(2),
        scratch_shapes=[
            pltpu.VMEM(((BLOCKS + 1) * W_ROWS, 128), f32),
            pltpu.VMEM(((2 * BLOCKS + 1) * W_ROWS, 128), f32),
            pltpu.VMEM((GROUPS, 64, 256), f32),
            pltpu.VMEM((GROUPS, 64, 256), f32),
            pltpu.VMEM((2 * GROUPS, 256, 128), bf16),
            pltpu.VMEM((2 * GROUPS, 256, 128), bf16),
        ],
        compiler_params=pltpu.CompilerParams(vmem_limit_bytes=SMALL_VMEM),
        cost_estimate=cost(40),
        name="pairs",
    )(lists, count, *tables_of, own, beside)


def reply_kernel(own_ref, far_ref, wave_ref, order_ref, z_ref, out_ref, hi_ref, lo_ref):
    for c in range(3):
        kind = 0 if c < 2 else 1
        hi, lo = split2(jnp.transpose(wave_ref[:, c, :]))
        wave = dot3(hi, lo, z_ref[0, kind], z_ref[1, kind])
        fill_table(c, own_ref[c] + far_ref[c] + wave, hi_ref, lo_ref)

    def put(c, r, row):
        out_ref[r, c : c + 1, :] = row

    gather_rows(3, 128, hi_ref, lo_ref, order_ref, put)


def reply_message(own_vel, far_vel, wave, order, z_table):
    return pl.pallas_call(
        reply_kernel,
        out_shape=jax.ShapeDtypeStruct((128, 3, 128), f32),
        in_specs=vmem(5),
        out_specs=pl.BlockSpec(memory_space=pltpu.VMEM),
        scratch_shapes=[pltpu.VMEM((192, 256), bf16), pltpu.VMEM((192, 256), bf16)],
        compiler_params=pltpu.CompilerParams(vmem_limit_bytes=VMEM_LIMIT),
        name="reply",
    )(own_vel, far_vel, wave, order, z_table)


def move_kernel(in_ref, route_ref, pos_ref, noise_ref, moved_ref, drift_ref, hi_ref, lo_ref, vel_ref):
    rows = route_ref.shape[0]
    for c in range(3):
        fill_table(c, in_ref[:, c, :], hi_ref, lo_ref)

    def put(c, r, row):
        vel_ref[c, pl.ds(r, 1), :] = row

    gather_rows(3, rows, hi_ref, lo_ref, route_ref, put)
    for c in range(3):
        for r in range(rows):
            drift_ref[c : c + 1, r * 128 : (r + 1) * 128] = time_step * vel_ref[c, r : r + 1, :]
    moved_ref[...] = pos_ref[...] + drift_ref[...] + noise_ref[...]


def move_beads(arrived, route, positions, noise):
    flat = jax.ShapeDtypeStruct(positions.shape, f32)
    return pl.pallas_call(
        move_kernel,
        out_shape=[flat, flat],
        in_specs=vmem(4),
        out_specs=vmem(2),
        scratch_shapes=[
            pltpu.VMEM((192, 256), bf16),
            pltpu.VMEM((192, 256), bf16),
            pltpu.VMEM((3, 64, 128), f32),
        ],
        compiler_params=pltpu.CompilerParams(vmem_limit_bytes=VMEM_LIMIT),
        name="move",
    )(arrived, route, positions, noise)


def shifted(value, axis, by):
    devices = lax.axis_size(axis)
    return lax.ppermute(value, axis, [(i, (i + by) % devices) for i in range(devices)])


def exchange(value):
    return lax.all_to_all(value, ("gx", "gy"), split_axis=0, concat_axis=0, tiled=True)


def shards(positions, noise, route, node_perm, pair_first, pair_second, pair_count):
    table = {name: jnp.asarray(value) for name, value in tables().items()}
    row_gx = lax.axis_index("gx")
    member = row_gx * lax.axis_size("gy") + lax.axis_index("gy")
    route = route.reshape(64, 128)
    order = lax.dynamic_index_in_dim(node_perm, row_gx, 0, keepdims=False).reshape(128, 128)
    incoming = exchange(send_message(positions, route))
    grid, spec = place_on_grid(incoming, order, table["z"])
    beside = shifted(grid, "gx", -1)
    weight, right, left = own_tables(grid)
    weight, right = beside_tables(beside, weight, right)
    wave = wave_flow(exchange(spec), table, member)
    grid, wave = lax.optimization_barrier((grid, wave))
    wave = exchange(wave)
    lists = pair_lists(pair_first[0], pair_second[0], pair_count[0])
    own_vel, far_vel = pair_velocities(grid, beside, (weight, right, left), lists, pair_count)
    far_vel, wave = lax.optimization_barrier((far_vel, wave))
    far_vel = shifted(far_vel, "gx", 1)
    reply = exchange(reply_message(own_vel, far_vel, wave, order, table["z"]))
    return tuple(move_beads(reply, route, positions, noise))


def solution(mesh):
    in_specs = (
        P(None, ("gx", "gy")),
        P(None, ("gx", "gy")),
        P(("gx", "gy")),
        P(None, "gy", None),
        P(("gx", "gy"), None),
        P(("gx", "gy"), None),
        P(("gx", "gy")),
    )
    out_specs = (P(None, ("gx", "gy")), P(None, ("gx", "gy")))
    return jax.shard_map(shards, mesh=mesh, in_specs=in_specs, out_specs=out_specs, check_vma=False)
```

```python
from functools import partial
import math

import numpy as np
import jax
import jax.numpy as jnp
from jax import lax
from jax.experimental import pallas as pl
from jax.experimental.pallas import tpu as pltpu
from jax.sharding import PartitionSpec as P

G = 128
BLOCKS = 256
PAIRS = 1024
STEP = 4
W_ROWS = 24
GROUPS = 2
FEATURES = 24

fene_k = 30.0
fene_reach = 1.5
bend_k = 2.0
time_step = 0.01
grid_spacing = 4.0

f32 = jnp.float32
bf16 = jnp.bfloat16
VMEM_LIMIT = 24 * 1024 * 1024
PAIR_VMEM = 40 * 1024 * 1024


def dot(a, b):
    return lax.dot_general(a, b, (((1,), (0,)), ((), ())), preferred_element_type=f32)


def dot_t(a, b):
    return lax.dot_general(a, b, (((1,), (1,)), ((), ())), preferred_element_type=f32)


def split2(x):
    hi = x.astype(bf16)
    return hi, (x - hi.astype(f32)).astype(bf16)


def split3(x):
    hi = x.astype(bf16).astype(f32)
    rest = x - hi
    mid = rest.astype(bf16).astype(f32)
    return hi, mid, (rest - mid).astype(bf16).astype(f32)


def dot3(a_hi, a_lo, b_hi, b_lo, form=dot):
    return form(a_hi, b_hi) + form(a_hi, b_lo) + form(a_lo, b_hi)


def split_table(table):
    table = np.asarray(table, np.float64)
    hi = table.astype(np.float32).astype(jnp.bfloat16)
    lo = (table - hi.astype(np.float64)).astype(np.float32).astype(jnp.bfloat16)
    return np.stack([hi, lo])


def tables():
    n = np.arange(G)
    turn = 2.0 * np.pi / G
    member = np.arange(128)
    freq = np.where(member < 64, member + 1, (member - 63) % 64)
    wave = turn * (freq[:, None] * n[None, :] % G)
    even, odd = np.cos(wave), -np.sin(wave)
    special = (member % 64) == 63
    first = (member < 64)[:, None]
    even = np.where(special[:, None], np.cos(wave), even)
    z_xy = np.where(special[:, None] | first, even, odd)
    z_z = np.where(special[:, None] | ~first, even, odd)
    k1, k2 = n // 8, n % 8
    outer = 2.0 * np.pi * (k1[:, None] * k1[None, :] / 16.0 + k2[:, None] * k2[None, :] / 8.0)
    a, b = n // 16, n % 16
    inner = 2.0 * np.pi * (a[:, None] * a[None, :] / 8.0 + b[:, None] * b[None, :] / 16.0)
    twist = turn * (k1[:, None] * a[None, :] + k2[:, None] * b[None, :])
    c_out, s_out, c_in, s_in = np.cos(outer), np.sin(outer), np.cos(inner), np.sin(inner)
    return {
        "z": split_table(np.stack([z_xy, z_z])),
        "outer": split_table(np.concatenate([c_out, -s_out], 0)),
        "outer_back": split_table(np.concatenate([c_out, -s_out], 1)),
        "inner": split_table(np.block([[c_in, -s_in], [s_in, c_in]])),
        "inner_back": split_table(np.block([[c_in, s_in], [-s_in, c_in]])),
        "twist": np.stack([np.cos(twist), np.sin(twist)]).astype(np.float32),
    }


def cost(micros):
    return pl.CostEstimate(flops=int(micros * 1e9), bytes_accessed=1 << 20, transcendentals=0)


def onehot(index, size, width):
    rows = lax.broadcasted_iota(jnp.int32, (size, width), 0)
    return jnp.where(rows == index, 1.0, 0.0).astype(bf16)


def high_part(place):
    return (place >> 7) & 63


def low_part(place):
    return ((place >> 13) << 7) | (place & 127)


def scatter_rows(channels, rows, value_row, place_ref, left_ref, sum_ref):
    group = left_ref.shape[1] // 128
    span = 128 * group

    def turn(g, _):
        low = []
        for j in range(group):
            place = place_ref[pl.ds(g * group + j, 1), :]
            high_hot = onehot(high_part(place), 64, 128)
            low.append(onehot(low_part(place), 256, 128))
            for c in range(channels):
                hi, lo = split2(value_row(c, g * group + j))
                left_ref[c * 128 : c * 128 + 64, j * 128 : (j + 1) * 128] = high_hot * hi
                left_ref[c * 128 + 64 : c * 128 + 128, j * 128 : (j + 1) * 128] = high_hot * lo
        moved = dot_t(left_ref[...], jnp.concatenate(low, axis=1))
        for c in range(channels):
            sum_ref[c * 64 : (c + 1) * 64, :] += (
                moved[c * 128 : c * 128 + 64] + moved[c * 128 + 64 : c * 128 + 128]
            )
        return 0

    sum_ref[...] = jnp.zeros_like(sum_ref)
    lax.fori_loop(0, rows // group, turn, 0)


def gather_rows(channels, table_hi_ref, table_lo_ref, place_ref, rows, put):
    low, high = [], []
    for r in rows:
        place = place_ref[pl.ds(r, 1), :]
        low.append(onehot(low_part(place), 256, 128))
        high.append(high_part(place))
    low = jnp.concatenate(low, axis=1)
    high = jnp.concatenate(high, axis=1)
    found = dot(table_hi_ref[...], low) + dot(table_lo_ref[...], low)
    rows_of = lax.broadcasted_iota(jnp.int32, (64, len(rows) * 128), 0) == high
    for c in range(channels):
        got = jnp.sum(
            jnp.where(rows_of, found[c * 64 : (c + 1) * 64], 0.0), axis=0, keepdims=True
        )
        for n in range(len(rows)):
            put(c, n, got[:, n * 128 : (n + 1) * 128])


WIDTH = 4


def fill_table(c, plane, table_hi_ref, table_lo_ref):
    hi, lo = split2(plane)
    for ref, part in ((table_hi_ref, hi), (table_lo_ref, lo)):
        ref[c * 64 : (c + 1) * 64, 0:128] = part[0:64]
        ref[c * 64 : (c + 1) * 64, 128:256] = part[64:128]


def greet_all(me, n_gy, members):
    barrier = pltpu.get_barrier_semaphore()

    def greet(d, _):
        there = lax.rem(me + d, members)
        pl.semaphore_signal(
            barrier,
            inc=1,
            device_id=(there // n_gy, lax.rem(there, n_gy)),
            device_id_type=pl.DeviceIdType.MESH,
        )
        return 0

    lax.fori_loop(1, members, greet, 0)


def wait_for_all(members):
    pl.semaphore_wait(pltpu.get_barrier_semaphore(), members - 1)


def send_row(out_ref, in_ref, me, there, n_gy, send_sem, recv_sem):
    pltpu.make_async_remote_copy(
        src_ref=out_ref.at[there],
        dst_ref=in_ref.at[me],
        send_sem=send_sem,
        recv_sem=recv_sem,
        device_id=(there // n_gy, lax.rem(there, n_gy)),
        device_id_type=pl.DeviceIdType.MESH,
    ).start()


def wait_rows(out_ref, in_ref, members, send_sem, recv_sem):
    every = pltpu.make_async_remote_copy(
        src_ref=out_ref.at[pl.ds(0, members - 1)],
        dst_ref=in_ref.at[pl.ds(0, members - 1)],
        send_sem=send_sem,
        recv_sem=recv_sem,
        device_id=(0, 0),
        device_id_type=pl.DeviceIdType.MESH,
    )
    every.wait_send()
    every.wait_recv()


def chain_forces(x):
    lane = lax.broadcasted_iota(jnp.int32, x[0].shape, 1) & 63
    last = lane == 63
    ahead = lambda v: pltpu.roll(v, 127, 1)
    behind = lambda v: pltpu.roll(v, 1, 1)
    bond = [jnp.where(last, 0.5, ahead(v) - v) for v in x]
    square = bond[0] * bond[0] + bond[1] * bond[1] + bond[2] * bond[2]
    inverse = lax.rsqrt(square)
    unit = [v * inverse for v in bond]
    following = [ahead(v) for v in unit]
    cosine = unit[0] * following[0] + unit[1] * following[1] + unit[2] * following[2]
    bends = lane < 62
    stretch = fene_k / (1.0 - square / fene_reach**2)
    before = behind(jnp.where(bends, 1.0, 0.0))
    cosine_before = behind(cosine)
    grad = []
    for c in range(3):
        pull = jnp.where(bends, following[c] - cosine * unit[c], 0.0)
        push = before * (behind(unit[c]) - cosine_before * unit[c])
        push = jnp.where(lane == 0, 0.0, push)
        grad.append(
            jnp.where(last, 0.0, stretch * bond[c] - bend_k * inverse * (pull + push))
        )
    return [g - jnp.where(lane == 0, 0.0, behind(g)) for g in grad]


def send_kernel(
    members, n_gy, pos_ref, route_ref, in_ref, out_ref, plane_ref, left_ref, sum_ref, send_sem,
    recv_sem,
):
    me = lax.axis_index("gx") * n_gy + lax.axis_index("gy")
    greet_all(me, n_gy, members)
    rows = route_ref.shape[0]
    for c in range(3):
        for r in range(rows):
            plane_ref[c, r : r + 1, :] = pos_ref[c : c + 1, r * 128 : (r + 1) * 128]
    forces = chain_forces([plane_ref[c] for c in range(3)])
    for c in range(3):
        plane_ref[3 + c] = forces[c]
    scatter_rows(
        6, rows, lambda c, r: plane_ref[c, pl.ds(r, 1), :], route_ref, left_ref, sum_ref
    )
    for c in range(6):
        out_ref[0:64, c, :] = sum_ref[c * 64 : (c + 1) * 64, 0:128]
        out_ref[64:128, c, :] = sum_ref[c * 64 : (c + 1) * 64, 128:256]
    wait_for_all(members)

    def go(d, _):
        send_row(out_ref, in_ref, me, lax.rem(me + d, members), n_gy, send_sem, recv_sem)
        return 0

    lax.fori_loop(1, members, go, 0)
    in_ref[me] = out_ref[me]
    wait_rows(out_ref, in_ref, members, send_sem, recv_sem)


def vmem(n):
    return [pl.BlockSpec(memory_space=pltpu.VMEM)] * n


def send_message(positions, route):
    n_gy = lax.axis_size("gy")
    members = lax.axis_size("gx") * n_gy
    return pl.pallas_call(
        partial(send_kernel, members, n_gy),
        out_shape=jax.ShapeDtypeStruct((128, 6, 128), f32),
        in_specs=vmem(2),
        out_specs=pl.BlockSpec(memory_space=pltpu.VMEM),
        scratch_shapes=[
            pltpu.VMEM((128, 6, 128), f32),
            pltpu.VMEM((6, 64, 128), f32),
            pltpu.VMEM((768, 1024), bf16),
            pltpu.VMEM((384, 256), f32),
            pltpu.SemaphoreType.DMA,
            pltpu.SemaphoreType.DMA,
        ],
        compiler_params=pltpu.CompilerParams(
            vmem_limit_bytes=VMEM_LIMIT, collective_id=1, has_side_effects=True
        ),
        name="send",
    )(positions, route)


def place_kernel(in_ref, order_ref, z_ref, out_ref, spec_ref, left_ref, sum_ref):
    scatter_rows(6, 128, lambda c, r: in_ref[r, c : c + 1, :], order_ref, left_ref, sum_ref)
    for c in range(6):
        out_ref[c, 0:64, :] = sum_ref[c * 64 : (c + 1) * 64, 0:128]
        out_ref[c, 64:128, :] = sum_ref[c * 64 : (c + 1) * 64, 128:256]
    for c in range(3):
        hi, lo = split2(out_ref[3 + c])
        kind = 0 if c < 2 else 1
        spec_ref[:, c, :] = dot3(z_ref[0, kind], z_ref[1, kind], hi, lo, dot_t)


def place_on_grid(incoming, order, z_table):
    return pl.pallas_call(
        place_kernel,
        out_shape=[
            jax.ShapeDtypeStruct((6, 128, 128), f32),
            jax.ShapeDtypeStruct((128, 3, 128), f32),
        ],
        in_specs=vmem(3),
        out_specs=vmem(2),
        scratch_shapes=[pltpu.VMEM((768, 1024), bf16), pltpu.VMEM((384, 256), f32)],
        compiler_params=pltpu.CompilerParams(vmem_limit_bytes=VMEM_LIMIT),
        name="place",
    )(incoming, order, z_table)


def wave_kernel(
    part_ref, in_ref, outer_ref, outer_back_ref, inner_ref, inner_back_ref, twist_ref,
    out_ref, mid_ref,
):
    freq, turn_re, turn_im, weight = (part_ref[i] for i in range(4))
    cos_t, sin_t = twist_ref[0], twist_ref[1]
    spectrum = []
    for c in range(3):
        hi, lo = split2(in_ref[:, c, :])
        both = dot3(outer_ref[0], outer_ref[1], hi, lo)
        re, im = both[0:128], both[128:256]
        mid_ref[:, 0:128] = re * cos_t + im * sin_t
        mid_ref[:, 128:256] = im * cos_t - re * sin_t
        hi, lo = split2(mid_ref[...])
        both = dot3(hi, lo, inner_ref[0], inner_ref[1])
        spectrum.append((both[:, 0:128], both[:, 128:256]))
    row = lax.broadcasted_iota(jnp.int32, (128, 128), 0)
    col = lax.broadcasted_iota(jnp.int32, (128, 128), 1)
    n_x = (row >> 3) + 16 * (col >> 4)
    n_y = (row & 7) + 8 * (col & 15)
    unit = 2.0 * math.pi / (G * grid_spacing)
    signed = lambda n: jnp.where(n < G // 2, n, n - G).astype(f32) * unit
    k_x, k_y = signed(n_x), signed(n_y)
    k_z = jnp.full((128, 128), freq * unit, f32)
    edge_x = jnp.where(n_x == G // 2, 1.0, 0.0)
    edge_y = jnp.where(n_y == G // 2, 1.0, 0.0)
    edge_z = jnp.where(jnp.full((128, 128), freq, f32) < -63.5, 1.0, 0.0)
    square = k_x * k_x + k_y * k_y + k_z * k_z
    positive = square > 0.0
    safe = jnp.where(positive, square, 1.0)
    green = jnp.where(
        positive,
        (1.0 - 0.25 * square / 3.0) * (1.0 + square) * jnp.exp(-square) / safe,
        0.0,
    ) * (weight / float(G**3))
    over = green / safe
    g_xy = jnp.where(edge_x == edge_y, -over * k_x * k_y, 0.0)
    g_xz = jnp.where(edge_x == edge_z, -over * k_x * k_z, 0.0)
    g_yz = jnp.where(edge_y == edge_z, -over * k_y * k_z, 0.0)
    g_xx = green - over * k_x * k_x
    g_yy = green - over * k_y * k_y
    g_zz = green - over * k_z * k_z
    (x_re, x_im), (y_re, y_im), (z_re, z_im) = spectrum
    z_re, z_im = turn_re * z_re - turn_im * z_im, turn_re * z_im + turn_im * z_re
    flow = [
        (g_xx * x_re + g_xy * y_re + g_xz * z_re, g_xx * x_im + g_xy * y_im + g_xz * z_im),
        (g_xy * x_re + g_yy * y_re + g_yz * z_re, g_xy * x_im + g_yy * y_im + g_yz * z_im),
    ]
    w_re = g_xz * x_re + g_yz * y_re + g_zz * z_re
    w_im = g_xz * x_im + g_yz * y_im + g_zz * z_im
    flow.append((turn_re * w_re + turn_im * w_im, turn_re * w_im - turn_im * w_re))
    for c in range(3):
        mid_ref[:, 0:128], mid_ref[:, 128:256] = flow[c]
        hi, lo = split2(mid_ref[...])
        both = dot3(hi, lo, inner_back_ref[0], inner_back_ref[1])
        re, im = both[:, 0:128], both[:, 128:256]
        hi, lo = split2(
            jnp.concatenate([re * cos_t - im * sin_t, im * cos_t + re * sin_t], axis=0)
        )
        out_ref[:, c, :] = dot3(outer_back_ref[0], outer_back_ref[1], hi, lo)


def wave_flow(spec, table, member):
    special = member % 64 == 63
    freq = jnp.where(member < 64, member + 1, (member - 63) % 64)
    freq = jnp.where(member == 63, -64, freq)
    side = jnp.where(member < 64, 1.0, -1.0)
    part = jnp.stack(
        [
            freq.astype(f32),
            jnp.where(special, 1.0, 0.0),
            jnp.where(special, 0.0, side),
            jnp.where(special, 1.0, 2.0),
        ]
    ).astype(f32)
    return pl.pallas_call(
        wave_kernel,
        out_shape=jax.ShapeDtypeStruct((128, 3, 128), f32),
        in_specs=[pl.BlockSpec(memory_space=pltpu.SMEM)] + vmem(6),
        out_specs=pl.BlockSpec(memory_space=pltpu.VMEM),
        scratch_shapes=[pltpu.VMEM((128, 256), f32)],
        compiler_params=pltpu.CompilerParams(vmem_limit_bytes=VMEM_LIMIT),
        name="wave",
    )(
        part, spec, table["outer"], table["outer_back"], table["inner"],
        table["inner_back"], table["twist"],
    )


ERFC_SHIFT = 4.0
ERFC_POLY = (
    -5.9986000529477224e-05, 1.1337793270330845, 4.308175452878655, 20.093023854033866,
    -8.594175483206275, 489.91788674098177, -1701.7584635921016, 1704.126720738659,
)


def pair_scalars(s2):
    u = lax.rsqrt(s2)
    gauss = jnp.exp2(s2 * (-0.25 * math.log2(math.e)))
    t = pl.reciprocal(s2 * u + ERFC_SHIFT, approx=True)
    w = ERFC_POLY[-1]
    for coefficient in ERFC_POLY[-2::-1]:
        w = w * t + coefficient
    u2 = u * u
    wu = w * u
    along = gauss * (wu * (0.0625 * u2 + 0.375) + 0.125)
    across = (gauss * u2) * (wu * (0.375 - 0.1875 * u2) - 0.125)
    return along, across


def both_halves(v):
    low_half = lax.broadcasted_iota(jnp.int32, (1, 128), 1) < 64
    other = pltpu.roll(v, 64, 1)
    return jnp.where(low_half, v, other), jnp.where(low_half, other, v)


def stage_nodes(ref, weight_stage, right_stage):
    x = [ref[c] for c in range(3)]
    f = [ref[3 + c] for c in range(3)]
    xf = x[0] * f[0] + x[1] * f[1] + x[2] * f[2]
    rows = f + [xf]
    rows += [x[a] * f[b] for a in range(3) for b in range(3)]
    rows += [x[a] * xf for a in range(3)]
    for c, plane in enumerate(rows):
        weight_stage[pl.ds(c, 128, stride=16), :] = plane
    norm = x[0] * x[0] + x[1] * x[1] + x[2] * x[2]
    first, second = [], []
    for h, m, l in [split3(v) for v in x]:
        first += [h, h, m, m, h, l]
        second += [h, m, h, m, l, h]
    one = jnp.ones((128, 128), f32)
    first = [-2.0 * v for v in first] + list(split3(norm)) + [one] * 3
    second += [one] * 3 + list(split3(norm + 0.25))
    for c, plane in enumerate(second):
        right_stage[pl.ds(c, 128, stride=FEATURES), :] = plane
    return first


def build_tables(base, weight_stage, right_stage, weight_ref, right_ref):
    blank = jnp.zeros((32 - FEATURES, 128), f32)

    def build(r, _):
        w = weight_stage[pl.ds(pl.multiple_of(r * 16, 8), 16), :]
        for k, v in enumerate(both_halves(w)):
            hi = v.astype(bf16)
            lo = (v - hi.astype(f32)).astype(bf16)
            weight_ref[base + 2 * r + k] = jnp.concatenate([hi, lo], axis=0)
        w = right_stage[pl.ds(pl.multiple_of(r * FEATURES, 8), FEATURES), :]
        for k, v in enumerate(both_halves(w)):
            right_ref[base + 2 * r + k] = jnp.concatenate([v, blank], axis=0).astype(bf16)
        return 0

    lax.fori_loop(0, 128, build, 0, unroll=16)


def build_left(first, left_stage, left_ref):
    for c, plane in enumerate(first):
        left_stage[pl.ds(c, 128, stride=FEATURES), :] = plane
    eye = jnp.where(
        lax.broadcasted_iota(jnp.int32, (128, 128), 0)
        == lax.broadcasted_iota(jnp.int32, (128, 128), 1),
        1.0,
        0.0,
    ).astype(bf16)
    blank = jnp.zeros((32 - FEATURES, 128), f32)

    def turn_left(r, _):
        v = left_stage[pl.ds(pl.multiple_of(r * FEATURES, 8), FEATURES), :]
        v = jnp.concatenate([v, blank], axis=0).astype(bf16)
        nodes = dot_t(eye, jnp.concatenate([v] * 4, axis=0)).astype(bf16)
        left_ref[2 * r] = nodes[0:64]
        left_ref[2 * r + 1] = nodes[64:128]
        return 0

    lax.fori_loop(0, 128, turn_left, 0, unroll=8)


def pair_kernel(
    list_ref, count_ref, own_ref, beside_ref, own_vel_ref, far_vel_ref,
    weight_ref, right_ref, left_ref, weight_stage, right_stage, left_stage,
    near_acc, far_acc, s2_a, s2_b, tile_a, tile_b,
):
    first = stage_nodes(own_ref, weight_stage, right_stage)
    build_left(first, left_stage, left_ref)
    build_tables(0, weight_stage, right_stage, weight_ref, right_ref)
    stage_nodes(beside_ref, weight_stage, right_stage)
    build_tables(BLOCKS, weight_stage, right_stage, weight_ref, right_ref)

    lane = lax.broadcasted_iota(jnp.int32, (1, 128), 1)
    low_half = lane < 64
    count = count_ref[0]

    def clear(r, _):
        blank = jnp.zeros((W_ROWS, 128), f32)
        far_acc[pl.ds(pl.multiple_of(r * 2 * W_ROWS, 8), W_ROWS), :] = blank
        far_acc[pl.ds(pl.multiple_of(r * 2 * W_ROWS + W_ROWS, 8), W_ROWS), :] = blank
        near_acc[pl.ds(pl.multiple_of(r * W_ROWS, 8), W_ROWS), :] = blank
        return 0

    lax.fori_loop(0, BLOCKS, clear, 0, unroll=8)

    wide = lax.broadcasted_iota(jnp.int32, (64, 128), 1)
    wide_low = wide < 64
    wide_even = (wide & 32) == 0
    narrow = lax.broadcasted_iota(jnp.int32, (32, 128), 1) < 64
    nothing = jnp.zeros((32, 128), bf16)

    def half_of(v, half):
        return jnp.where(narrow, nothing, v) if half else jnp.where(narrow, v, nothing)

    half_keep = [(lane >> 6) == s for s in range(2)]
    blank = jnp.zeros((64, 128), bf16)

    def blocks_of(pair):
        return list_ref[0, pair], list_ref[1, pair]

    def distance_dots(step):
        found = []
        for g in range(GROUPS):
            pairs = [blocks_of((step * GROUPS + g) * STEP + s) for s in range(STEP)]
            left = [left_ref[pairs[s][0]] for s in range(STEP)]
            left = jnp.where(
                wide_low,
                jnp.where(wide_even, left[0], left[1]),
                jnp.where(wide_even, left[2], left[3]),
            )
            right = [half_of(right_ref[pairs[s][1]], s % 2) for s in range(STEP)]
            right = jnp.concatenate(
                [
                    jnp.concatenate([right[0], right[1], blank], axis=0),
                    jnp.concatenate([blank, right[2], right[3]], axis=0),
                ],
                axis=1,
            )
            found.append(dot(left, right))
        return found

    def scalars(s2_ref, tile_ref, pack):
        half = pack % 2
        along, across = pair_scalars(s2_ref[pack // 2, :, half * 128 : (half + 1) * 128])
        for at, value in ((0, across), (128, along)):
            hi, lo = split2(value)
            tile_ref[pack, at : at + 64, :] = hi
            tile_ref[pack, at + 64 : at + 128, :] = lo

    def sum_dots(step, tile_ref, pack):
        tile = tile_ref[pack]
        pairs = [blocks_of((step * 2 * GROUPS + pack) * 2 + s) for s in range(2)]
        a = jnp.concatenate([weight_ref[i] for i, _ in pairs], axis=0)
        b = jnp.concatenate(
            [half_of(weight_ref[j], s) for s, (_, j) in enumerate(pairs)], axis=0
        )
        to_far = dot(a, jnp.concatenate([tile[0:128], tile[128:256]], axis=1))
        return dot_t(b, tile), to_far

    def add_sums(step, pack, to_near, to_far):
        for s in range(2):
            number = (step * 2 * GROUPS + pack) * 2 + s
            for out, acc_ref, row, keep in (
                (to_near, near_acc, list_ref[2, number], None),
                (to_far, far_acc, list_ref[3, number], half_keep[s]),
            ):
                top = 32 * s
                add_h = out[top : top + 16, 0:128] + out[top + 16 : top + 32, 0:128]
                add_f = out[top : top + 8, 128:256] + out[top + 16 : top + 24, 128:256]
                add = jnp.concatenate([add_h, add_f], axis=0)
                if keep is not None:
                    add = jnp.where(keep, add, 0.0)
                acc_ref[pl.ds(pl.multiple_of(row, 8), W_ROWS), :] += add

    packs = range(2 * GROUPS)

    def keep_distances(found, s2_ref):
        for g in range(GROUPS):
            s2_ref[g] = found[g]

    def stage(k, s2_next, s2_now, tile_now, tile_last):
        for pack in packs:
            scalars(s2_now, tile_now, pack)
        for pack in packs:
            add_sums(k - 1, pack, *sum_dots(k - 1, tile_last, pack))
        keep_distances(distance_dots(k + 1), s2_next)

    steps = (count + (STEP * GROUPS - 1)) // (STEP * GROUPS)
    keep_distances(distance_dots(0), s2_a)
    for pack in packs:
        scalars(s2_a, tile_a, pack)
    keep_distances(distance_dots(1), s2_b)

    def body(j, _):
        k = 2 * j + 1
        stage(k, s2_a, s2_b, tile_b, tile_a)
        stage(k + 1, s2_b, s2_a, tile_a, tile_b)
        return 0

    lax.fori_loop(0, (steps + 1) // 2, body, 0)

    chunk = 32
    for side, ref, out_ref in ((0, own_ref, own_vel_ref), (1, beside_ref, far_vel_ref)):
        for top in range(0, 128, chunk):
            planes = []
            for c in range(19):
                at = (2 * top) * W_ROWS + c
                even = far_acc[pl.ds(side * BLOCKS * W_ROWS + at, chunk, stride=2 * W_ROWS), :]
                at += W_ROWS
                odd = far_acc[pl.ds(side * BLOCKS * W_ROWS + at, chunk, stride=2 * W_ROWS), :]
                if side == 0:
                    even += near_acc[pl.ds(at - W_ROWS, chunk, stride=2 * W_ROWS), :]
                    odd += near_acc[pl.ds(at, chunk, stride=2 * W_ROWS), :]
                even = even + pltpu.roll(even, 64, 1)
                odd = odd + pltpu.roll(odd, 64, 1)
                planes.append(jnp.where(low_half, even, odd))
            x = [ref[c, top : top + chunk, :] for c in range(3)]
            h_f, h_xf, h_x_f, h_x_xf, along = (
                planes[0:3], planes[3], planes[4:13], planes[13:16], planes[16:19],
            )
            x_h_f = x[0] * h_f[0] + x[1] * h_f[1] + x[2] * h_f[2] - h_xf
            for c in range(3):
                out_ref[c, top : top + chunk, :] = (
                    along[c]
                    + x[c] * x_h_f
                    - (x[0] * h_x_f[3 * c] + x[1] * h_x_f[3 * c + 1] + x[2] * h_x_f[3 * c + 2])
                    + h_x_xf[c]
                )


def pair_lists(first_list, second_list, count):
    live = jnp.arange(PAIRS, dtype=jnp.int32) < count
    lists = jnp.stack(
        [
            first_list,
            second_list,
            jnp.where(live, first_list, BLOCKS) * W_ROWS,
            jnp.where(live & (first_list != second_list), second_list, 2 * BLOCKS) * W_ROWS,
        ]
    )
    spare = jnp.array([0, 0, BLOCKS * W_ROWS, 2 * BLOCKS * W_ROWS], jnp.int32)
    return jnp.concatenate([lists, jnp.broadcast_to(spare[:, None], (4, 128))], axis=1)


def pair_velocities(own, beside, lists, count):
    plane = jax.ShapeDtypeStruct((3, 128, 128), f32)
    return pl.pallas_call(
        pair_kernel,
        out_shape=[plane, plane],
        in_specs=[pl.BlockSpec(memory_space=pltpu.SMEM)] * 2 + vmem(2),
        out_specs=vmem(2),
        scratch_shapes=[
            pltpu.VMEM((2 * BLOCKS, 32, 128), bf16),
            pltpu.VMEM((2 * BLOCKS, 32, 128), bf16),
            pltpu.VMEM((BLOCKS, 64, 128), bf16),
            pltpu.VMEM((128 * 16, 128), f32),
            pltpu.VMEM((128 * FEATURES, 128), f32),
            pltpu.VMEM((128 * FEATURES, 128), f32),
            pltpu.VMEM(((BLOCKS + 1) * W_ROWS, 128), f32),
            pltpu.VMEM(((2 * BLOCKS + 1) * W_ROWS, 128), f32),
            pltpu.VMEM((GROUPS, 64, 256), f32),
            pltpu.VMEM((GROUPS, 64, 256), f32),
            pltpu.VMEM((2 * GROUPS, 256, 128), bf16),
            pltpu.VMEM((2 * GROUPS, 256, 128), bf16),
        ],
        compiler_params=pltpu.CompilerParams(vmem_limit_bytes=PAIR_VMEM),
        cost_estimate=cost(50),
        name="pairs",
    )(lists, count, own, beside)


def reply_kernel(
    members, n_gx, n_gy, own_ref, far_ref, wave_ref, order_ref, z_ref, in_ref, out_ref,
    beside_ref, hi_ref, lo_ref, send_sem, recv_sem, far_send, far_recv,
):
    g_x = lax.axis_index("gx")
    me = g_x * n_gy + lax.axis_index("gy")
    greet_all(me, n_gy, members)
    wait_for_all(members)
    far = pltpu.make_async_remote_copy(
        src_ref=far_ref,
        dst_ref=beside_ref,
        send_sem=far_send,
        recv_sem=far_recv,
        device_id=(lax.rem(g_x + 1, n_gx), lax.axis_index("gy")),
        device_id_type=pl.DeviceIdType.MESH,
    )
    far.start()
    waves = []
    for c in range(3):
        kind = 0 if c < 2 else 1
        hi, lo = split2(jnp.transpose(wave_ref[:, c, :]))
        waves.append(own_ref[c] + dot3(hi, lo, z_ref[0, kind], z_ref[1, kind]))
    far.wait()
    for c in range(3):
        fill_table(c, waves[c] + beside_ref[c], hi_ref, lo_ref)

    def turn(g, _):
        rows = [lax.rem(me + 1 + g * WIDTH + j, members) for j in range(WIDTH)]

        def put(c, n, row):
            out_ref[rows[n], c : c + 1, :] = row

        gather_rows(3, hi_ref, lo_ref, order_ref, rows, put)
        for j, row in enumerate(rows):
            pl.when(g * WIDTH + j < members - 1)(
                partial(send_row, out_ref, in_ref, me, row, n_gy, send_sem, recv_sem)
            )
        return 0

    lax.fori_loop(0, members // WIDTH, turn, 0)
    in_ref[me] = out_ref[me]
    wait_rows(out_ref, in_ref, members, send_sem, recv_sem)


def reply_message(own_vel, far_vel, wave, order, z_table):
    n_gx, n_gy = lax.axis_size("gx"), lax.axis_size("gy")
    members = n_gx * n_gy
    return pl.pallas_call(
        partial(reply_kernel, members, n_gx, n_gy),
        out_shape=jax.ShapeDtypeStruct((128, 3, 128), f32),
        in_specs=vmem(5),
        out_specs=pl.BlockSpec(memory_space=pltpu.VMEM),
        scratch_shapes=[
            pltpu.VMEM((128, 3, 128), f32),
            pltpu.VMEM((3, 128, 128), f32),
            pltpu.VMEM((192, 256), bf16),
            pltpu.VMEM((192, 256), bf16),
            pltpu.SemaphoreType.DMA,
            pltpu.SemaphoreType.DMA,
            pltpu.SemaphoreType.DMA,
            pltpu.SemaphoreType.DMA,
        ],
        compiler_params=pltpu.CompilerParams(
            vmem_limit_bytes=VMEM_LIMIT, collective_id=2, has_side_effects=True
        ),
        name="reply",
    )(own_vel, far_vel, wave, order, z_table)


def move_kernel(in_ref, route_ref, pos_ref, noise_ref, moved_ref, drift_ref, hi_ref, lo_ref, vel_ref):
    rows = route_ref.shape[0]
    for c in range(3):
        fill_table(c, in_ref[:, c, :], hi_ref, lo_ref)

    def turn(g, _):
        def put(c, n, row):
            vel_ref[c, pl.ds(g * WIDTH + n, 1), :] = row

        gather_rows(3, hi_ref, lo_ref, route_ref, [g * WIDTH + j for j in range(WIDTH)], put)
        return 0

    lax.fori_loop(0, rows // WIDTH, turn, 0)
    for c in range(3):
        for r in range(rows):
            drift_ref[c : c + 1, r * 128 : (r + 1) * 128] = time_step * vel_ref[c, r : r + 1, :]
    moved_ref[...] = pos_ref[...] + drift_ref[...] + noise_ref[...]


def move_beads(arrived, route, positions, noise):
    flat = jax.ShapeDtypeStruct(positions.shape, f32)
    return pl.pallas_call(
        move_kernel,
        out_shape=[flat, flat],
        in_specs=vmem(4),
        out_specs=vmem(2),
        scratch_shapes=[
            pltpu.VMEM((192, 256), bf16),
            pltpu.VMEM((192, 256), bf16),
            pltpu.VMEM((3, 64, 128), f32),
        ],
        compiler_params=pltpu.CompilerParams(vmem_limit_bytes=VMEM_LIMIT),
        name="move",
    )(arrived, route, positions, noise)


def shifted(value, axis, by):
    devices = lax.axis_size(axis)
    return lax.ppermute(value, axis, [(i, (i + by) % devices) for i in range(devices)])


def exchange(value):
    return lax.all_to_all(value, ("gx", "gy"), split_axis=0, concat_axis=0, tiled=True)


def shards(positions, noise, route, node_perm, pair_first, pair_second, pair_count):
    table = {name: jnp.asarray(value) for name, value in tables().items()}
    row_gx = lax.axis_index("gx")
    member = row_gx * lax.axis_size("gy") + lax.axis_index("gy")
    route = route.reshape(64, 128)
    order = lax.dynamic_index_in_dim(node_perm, row_gx, 0, keepdims=False).reshape(128, 128)
    incoming = send_message(positions, route)
    grid, spec = place_on_grid(incoming, order, table["z"])
    beside = shifted(grid, "gx", -1)
    wave = wave_flow(exchange(spec), table, member)
    grid, wave = lax.optimization_barrier((grid, wave))
    wave = exchange(wave)
    lists = pair_lists(pair_first[0], pair_second[0], pair_count[0])
    own_vel, far_vel = pair_velocities(grid, beside, lists, pair_count)
    reply = reply_message(own_vel, far_vel, wave, order, table["z"])
    return tuple(move_beads(reply, route, positions, noise))


def solution(mesh):
    in_specs = (
        P(None, ("gx", "gy")),
        P(None, ("gx", "gy")),
        P(("gx", "gy")),
        P(None, "gy", None),
        P(("gx", "gy"), None),
        P(("gx", "gy"), None),
        P(("gx", "gy")),
    )
    out_specs = (P(None, ("gx", "gy")), P(None, ("gx", "gy")))
    return jax.shard_map(shards, mesh=mesh, in_specs=in_specs, out_specs=out_specs, check_vma=False)
```

```python
from functools import partial
import math

import numpy as np
import jax
import jax.numpy as jnp
from jax import lax
from jax.experimental import pallas as pl
from jax.experimental.pallas import tpu as pltpu
from jax.sharding import PartitionSpec as P

G = 128
BLOCKS = 256
PAIRS = 1024
STEP = 4
W_ROWS = 24
GROUPS = 2
FEATURES = 24

fene_k = 30.0
fene_reach = 1.5
bend_k = 2.0
time_step = 0.01
grid_spacing = 4.0

f32 = jnp.float32
bf16 = jnp.bfloat16
VMEM_LIMIT = 24 * 1024 * 1024
PAIR_VMEM = 40 * 1024 * 1024


def dot(a, b):
    return lax.dot_general(a, b, (((1,), (0,)), ((), ())), preferred_element_type=f32)


def dot_t(a, b):
    return lax.dot_general(a, b, (((1,), (1,)), ((), ())), preferred_element_type=f32)


def split2(x):
    hi = x.astype(bf16)
    return hi, (x - hi.astype(f32)).astype(bf16)


def split3(x):
    hi = x.astype(bf16).astype(f32)
    rest = x - hi
    mid = rest.astype(bf16).astype(f32)
    return hi, mid, (rest - mid).astype(bf16).astype(f32)


def dot3(a_hi, a_lo, b_hi, b_lo, form=dot):
    return form(a_hi, b_hi) + form(a_hi, b_lo) + form(a_lo, b_hi)


def split_table(table):
    table = np.asarray(table, np.float64)
    hi = table.astype(np.float32).astype(jnp.bfloat16)
    lo = (table - hi.astype(np.float64)).astype(np.float32).astype(jnp.bfloat16)
    return np.stack([hi, lo])


def tables():
    n = np.arange(G)
    turn = 2.0 * np.pi / G
    member = np.arange(128)
    freq = np.where(member < 64, member + 1, (member - 63) % 64)
    wave = turn * (freq[:, None] * n[None, :] % G)
    even, odd = np.cos(wave), -np.sin(wave)
    special = (member % 64) == 63
    first = (member < 64)[:, None]
    even = np.where(special[:, None], np.cos(wave), even)
    z_xy = np.where(special[:, None] | first, even, odd)
    z_z = np.where(special[:, None] | ~first, even, odd)
    k1, k2 = n // 8, n % 8
    outer = 2.0 * np.pi * (k1[:, None] * k1[None, :] / 16.0 + k2[:, None] * k2[None, :] / 8.0)
    a, b = n // 16, n % 16
    inner = 2.0 * np.pi * (a[:, None] * a[None, :] / 8.0 + b[:, None] * b[None, :] / 16.0)
    twist = turn * (k1[:, None] * a[None, :] + k2[:, None] * b[None, :])
    c_out, s_out, c_in, s_in = np.cos(outer), np.sin(outer), np.cos(inner), np.sin(inner)
    return {
        "z": split_table(np.stack([z_xy, z_z])),
        "outer": split_table(np.concatenate([c_out, -s_out], 0)),
        "outer_back": split_table(np.concatenate([c_out, -s_out], 1)),
        "inner": split_table(np.block([[c_in, -s_in], [s_in, c_in]])),
        "inner_back": split_table(np.block([[c_in, s_in], [-s_in, c_in]])),
        "twist": np.stack([np.cos(twist), np.sin(twist)]).astype(np.float32),
    }


def cost(micros):
    return pl.CostEstimate(flops=int(micros * 1e9), bytes_accessed=1 << 20, transcendentals=0)


def onehot(index, size, width):
    rows = lax.broadcasted_iota(jnp.int32, (size, width), 0)
    return jnp.where(rows == index, 1.0, 0.0).astype(bf16)


def high_part(place):
    return (place >> 7) & 63


def low_part(place):
    return ((place >> 13) << 7) | (place & 127)


GROUP = 8
WIDTH = 4


def scatter_rows(channels, rows, row_at, value_row, place_ref, left, low, sum_ref, ready=None):
    def build(g, side):
        if ready is not None:
            ready(g)
        for j in range(GROUP):
            r = row_at(g * GROUP + j)
            place = place_ref[pl.ds(r, 1), :]
            high_hot = onehot(high_part(place), 64, 128)
            low[side][:, j * 128 : (j + 1) * 128] = onehot(low_part(place), 256, 128)
            for c in range(channels):
                hi, lo = split2(value_row(c, r))
                left[side][c * 128 : c * 128 + 64, j * 128 : (j + 1) * 128] = high_hot * hi
                left[side][c * 128 + 64 : c * 128 + 128, j * 128 : (j + 1) * 128] = high_hot * lo

    def use(side):
        moved = dot_t(left[side][...], low[side][...])
        for c in range(channels):
            sum_ref[c * 64 : (c + 1) * 64, :] += (
                moved[c * 128 : c * 128 + 64] + moved[c * 128 + 64 : c * 128 + 128]
            )

    groups = rows // GROUP
    sum_ref[...] = jnp.zeros_like(sum_ref)
    build(0, 0)

    def turn(h, _):
        build(2 * h + 1, 1)
        use(0)
        build(2 * h + 2, 0)
        use(1)
        return 0

    lax.fori_loop(0, groups // 2 - 1, turn, 0)
    build(groups - 1, 1)
    use(0)
    use(1)


def unpack_sums(channels, sum_ref, put):
    for c in range(channels):
        for half in range(2):
            put(c, half, sum_ref[c * 64 : (c + 1) * 64, half * 128 : (half + 1) * 128])


def gather_rows(channels, turns, row_at, table_hi_ref, table_lo_ref, place_ref, low, put):
    def build(g, side):
        for n in range(WIDTH):
            place = place_ref[pl.ds(row_at(g, n), 1), :]
            low[side][:, n * 128 : (n + 1) * 128] = onehot(low_part(place), 256, 128)

    def use(g, side):
        found = dot(table_hi_ref[...], low[side][...]) + dot(table_lo_ref[...], low[side][...])
        for n in range(WIDTH):
            high = high_part(place_ref[pl.ds(row_at(g, n), 1), :])
            rows_of = lax.broadcasted_iota(jnp.int32, (64, 128), 0) == high
            for c in range(channels):
                part = found[c * 64 : (c + 1) * 64, n * 128 : (n + 1) * 128]
                put(g, c, n, jnp.sum(jnp.where(rows_of, part, 0.0), axis=0, keepdims=True))

    build(0, 0)

    def turn(h, _):
        build(2 * h + 1, 1)
        use(2 * h, 0)
        build(2 * h + 2, 0)
        use(2 * h + 1, 1)
        return 0

    lax.fori_loop(0, turns // 2 - 1, turn, 0)
    build(turns - 1, 1)
    use(turns - 2, 0)
    use(turns - 1, 1)


def fill_table(c, plane, table_hi_ref, table_lo_ref):
    hi, lo = split2(plane)
    for ref, part in ((table_hi_ref, hi), (table_lo_ref, lo)):
        ref[c * 64 : (c + 1) * 64, 0:128] = part[0:64]
        ref[c * 64 : (c + 1) * 64, 128:256] = part[64:128]


def greet_all(me, n_gy, members):
    barrier = pltpu.get_barrier_semaphore()

    def greet(d, _):
        there = lax.rem(me + d, members)
        pl.semaphore_signal(
            barrier,
            inc=1,
            device_id=(there // n_gy, lax.rem(there, n_gy)),
            device_id_type=pl.DeviceIdType.MESH,
        )
        return 0

    lax.fori_loop(1, members, greet, 0)


def wait_for_all(members):
    pl.semaphore_wait(pltpu.get_barrier_semaphore(), members - 1)


def send_row(out_ref, in_ref, me, there, n_gy, send_sem, recv_sem):
    pltpu.make_async_remote_copy(
        src_ref=out_ref.at[there],
        dst_ref=in_ref.at[me],
        send_sem=send_sem,
        recv_sem=recv_sem,
        device_id=(there // n_gy, lax.rem(there, n_gy)),
        device_id_type=pl.DeviceIdType.MESH,
    ).start()


def wait_rows(out_ref, in_ref, members, send_sem, recv_sem):
    every = pltpu.make_async_remote_copy(
        src_ref=out_ref.at[pl.ds(0, members - 1)],
        dst_ref=in_ref.at[pl.ds(0, members - 1)],
        send_sem=send_sem,
        recv_sem=recv_sem,
        device_id=(0, 0),
        device_id_type=pl.DeviceIdType.MESH,
    )
    every.wait_send()
    every.wait_recv()


def chain_forces(x):
    lane = lax.broadcasted_iota(jnp.int32, x[0].shape, 1) & 63
    last = lane == 63
    ahead = lambda v: pltpu.roll(v, 127, 1)
    behind = lambda v: pltpu.roll(v, 1, 1)
    bond = [jnp.where(last, 0.5, ahead(v) - v) for v in x]
    square = bond[0] * bond[0] + bond[1] * bond[1] + bond[2] * bond[2]
    inverse = lax.rsqrt(square)
    unit = [v * inverse for v in bond]
    following = [ahead(v) for v in unit]
    cosine = unit[0] * following[0] + unit[1] * following[1] + unit[2] * following[2]
    bends = lane < 62
    stretch = fene_k / (1.0 - square / fene_reach**2)
    before = behind(jnp.where(bends, 1.0, 0.0))
    cosine_before = behind(cosine)
    grad = []
    for c in range(3):
        pull = jnp.where(bends, following[c] - cosine * unit[c], 0.0)
        push = before * (behind(unit[c]) - cosine_before * unit[c])
        push = jnp.where(lane == 0, 0.0, push)
        grad.append(
            jnp.where(last, 0.0, stretch * bond[c] - bend_k * inverse * (pull + push))
        )
    return [g - jnp.where(lane == 0, 0.0, behind(g)) for g in grad]


def arrive_kernel(
    members, n_gx, n_gy, pos_ref, route_ref, order_ref, z_ref, grid_ref, beside_ref, spec_in_ref,
    plane_ref, left_a, left_b, low_a, low_b, sum_ref, out_ref, in_ref, spec_ref,
    send_sem, recv_sems, spec_send, spec_recv, side_send, side_recv,
):
    g_x = lax.axis_index("gx")
    me = g_x * n_gy + lax.axis_index("gy")
    greet_all(me, n_gy, members)
    rows = route_ref.shape[0]
    for c in range(3):
        for r in range(rows):
            plane_ref[c, r : r + 1, :] = pos_ref[c : c + 1, r * 128 : (r + 1) * 128]
    forces = chain_forces([plane_ref[c] for c in range(3)])
    for c in range(3):
        plane_ref[3 + c] = forces[c]
    left, low = (left_a, left_b), (low_a, low_b)
    scatter_rows(
        6, rows, lambda n: n, lambda c, r: plane_ref[c, pl.ds(r, 1), :], route_ref, left, low, sum_ref
    )

    def to_message(c, half, value):
        out_ref[half * 64 : (half + 1) * 64, c, :] = value

    unpack_sums(6, sum_ref, to_message)
    wait_for_all(members)
    in_ref[me] = out_ref[me]
    groups = members // GROUP

    def send_group(g):
        for j in range(GROUP):
            if isinstance(g, int) and g * GROUP + j == 0:
                continue
            there = lax.rem(me + g * GROUP + j, members)
            send_row(out_ref, in_ref, me, there, n_gy, send_sem, recv_sems.at[g])

    def group_here(g):
        if isinstance(g, int):
            if g + 2 < groups:
                send_group(g + 2)
        else:
            pl.when(g + 2 < groups)(partial(send_group, g + 2))
        count = GROUP - 1 if isinstance(g, int) and g == 0 else GROUP
        pltpu.make_async_remote_copy(
            src_ref=out_ref.at[pl.ds(0, count)],
            dst_ref=in_ref.at[pl.ds(0, count)],
            send_sem=send_sem,
            recv_sem=recv_sems.at[g],
            device_id=(0, 0),
            device_id_type=pl.DeviceIdType.MESH,
        ).wait_recv()

    send_group(0)
    send_group(1)
    scatter_rows(
        6,
        members,
        lambda n: lax.rem(me + members - n, members),
        lambda c, r: in_ref[r, c : c + 1, :],
        order_ref,
        left,
        low,
        sum_ref,
        group_here,
    )

    def to_grid(c, half, value):
        grid_ref[c, half * 64 : (half + 1) * 64, :] = value

    unpack_sums(6, sum_ref, to_grid)
    side = pltpu.make_async_remote_copy(
        src_ref=grid_ref,
        dst_ref=beside_ref,
        send_sem=side_send,
        recv_sem=side_recv,
        device_id=(lax.rem(g_x + n_gx - 1, n_gx), lax.axis_index("gy")),
        device_id_type=pl.DeviceIdType.MESH,
    )
    side.start()
    for c in range(3):
        hi, lo = split2(grid_ref[3 + c])
        kind = 0 if c < 2 else 1
        spec_ref[:, c, :] = dot3(z_ref[0, kind], z_ref[1, kind], hi, lo, dot_t)

    def go(d, _):
        there = lax.rem(me + d, members)
        send_row(spec_ref, spec_in_ref, me, there, n_gy, spec_send, spec_recv)
        return 0

    lax.fori_loop(1, members, go, 0)
    spec_in_ref[me] = spec_ref[me]
    pltpu.make_async_remote_copy(
        src_ref=out_ref.at[pl.ds(0, members - 1)],
        dst_ref=in_ref.at[pl.ds(0, members - 1)],
        send_sem=send_sem,
        recv_sem=recv_sems.at[0],
        device_id=(0, 0),
        device_id_type=pl.DeviceIdType.MESH,
    ).wait_send()
    wait_rows(spec_ref, spec_in_ref, members, spec_send, spec_recv)
    side.wait()


def vmem(n):
    return [pl.BlockSpec(memory_space=pltpu.VMEM)] * n


def arrive_on_grid(positions, route, order, z_table):
    n_gx, n_gy = lax.axis_size("gx"), lax.axis_size("gy")
    members = n_gx * n_gy
    return pl.pallas_call(
        partial(arrive_kernel, members, n_gx, n_gy),
        out_shape=[
            jax.ShapeDtypeStruct((6, 128, 128), f32),
            jax.ShapeDtypeStruct((6, 128, 128), f32),
            jax.ShapeDtypeStruct((128, 3, 128), f32),
        ],
        in_specs=vmem(4),
        out_specs=vmem(3),
        scratch_shapes=[
            pltpu.VMEM((6, 64, 128), f32),
            pltpu.VMEM((768, 1024), bf16),
            pltpu.VMEM((768, 1024), bf16),
            pltpu.VMEM((256, 1024), bf16),
            pltpu.VMEM((256, 1024), bf16),
            pltpu.VMEM((384, 256), f32),
            pltpu.VMEM((128, 6, 128), f32),
            pltpu.VMEM((128, 6, 128), f32),
            pltpu.VMEM((128, 3, 128), f32),
            pltpu.SemaphoreType.DMA,
            pltpu.SemaphoreType.DMA((128 // GROUP,)),
            pltpu.SemaphoreType.DMA,
            pltpu.SemaphoreType.DMA,
            pltpu.SemaphoreType.DMA,
            pltpu.SemaphoreType.DMA,
        ],
        compiler_params=pltpu.CompilerParams(
            vmem_limit_bytes=VMEM_LIMIT, collective_id=1, has_side_effects=True
        ),
        name="arrive",
    )(positions, route, order, z_table)


def wave_kernel(
    part_ref, in_ref, outer_ref, outer_back_ref, inner_ref, inner_back_ref, twist_ref,
    out_ref, mid_ref,
):
    freq, turn_re, turn_im, weight = (part_ref[i] for i in range(4))
    cos_t, sin_t = twist_ref[0], twist_ref[1]
    spectrum = []
    for c in range(3):
        hi, lo = split2(in_ref[:, c, :])
        both = dot3(outer_ref[0], outer_ref[1], hi, lo)
        re, im = both[0:128], both[128:256]
        mid_ref[:, 0:128] = re * cos_t + im * sin_t
        mid_ref[:, 128:256] = im * cos_t - re * sin_t
        hi, lo = split2(mid_ref[...])
        both = dot3(hi, lo, inner_ref[0], inner_ref[1])
        spectrum.append((both[:, 0:128], both[:, 128:256]))
    row = lax.broadcasted_iota(jnp.int32, (128, 128), 0)
    col = lax.broadcasted_iota(jnp.int32, (128, 128), 1)
    n_x = (row >> 3) + 16 * (col >> 4)
    n_y = (row & 7) + 8 * (col & 15)
    unit = 2.0 * math.pi / (G * grid_spacing)
    signed = lambda n: jnp.where(n < G // 2, n, n - G).astype(f32) * unit
    k_x, k_y = signed(n_x), signed(n_y)
    k_z = jnp.full((128, 128), freq * unit, f32)
    edge_x = jnp.where(n_x == G // 2, 1.0, 0.0)
    edge_y = jnp.where(n_y == G // 2, 1.0, 0.0)
    edge_z = jnp.where(jnp.full((128, 128), freq, f32) < -63.5, 1.0, 0.0)
    square = k_x * k_x + k_y * k_y + k_z * k_z
    positive = square > 0.0
    safe = jnp.where(positive, square, 1.0)
    green = jnp.where(
        positive,
        (1.0 - 0.25 * square / 3.0) * (1.0 + square) * jnp.exp(-square) / safe,
        0.0,
    ) * (weight / float(G**3))
    over = green / safe
    g_xy = jnp.where(edge_x == edge_y, -over * k_x * k_y, 0.0)
    g_xz = jnp.where(edge_x == edge_z, -over * k_x * k_z, 0.0)
    g_yz = jnp.where(edge_y == edge_z, -over * k_y * k_z, 0.0)
    g_xx = green - over * k_x * k_x
    g_yy = green - over * k_y * k_y
    g_zz = green - over * k_z * k_z
    (x_re, x_im), (y_re, y_im), (z_re, z_im) = spectrum
    z_re, z_im = turn_re * z_re - turn_im * z_im, turn_re * z_im + turn_im * z_re
    flow = [
        (g_xx * x_re + g_xy * y_re + g_xz * z_re, g_xx * x_im + g_xy * y_im + g_xz * z_im),
        (g_xy * x_re + g_yy * y_re + g_yz * z_re, g_xy * x_im + g_yy * y_im + g_yz * z_im),
    ]
    w_re = g_xz * x_re + g_yz * y_re + g_zz * z_re
    w_im = g_xz * x_im + g_yz * y_im + g_zz * z_im
    flow.append((turn_re * w_re + turn_im * w_im, turn_re * w_im - turn_im * w_re))
    for c in range(3):
        mid_ref[:, 0:128], mid_ref[:, 128:256] = flow[c]
        hi, lo = split2(mid_ref[...])
        both = dot3(hi, lo, inner_back_ref[0], inner_back_ref[1])
        re, im = both[:, 0:128], both[:, 128:256]
        hi, lo = split2(
            jnp.concatenate([re * cos_t - im * sin_t, im * cos_t + re * sin_t], axis=0)
        )
        out_ref[:, c, :] = dot3(outer_back_ref[0], outer_back_ref[1], hi, lo)


def wave_flow(spec, table, member):
    special = member % 64 == 63
    freq = jnp.where(member < 64, member + 1, (member - 63) % 64)
    freq = jnp.where(member == 63, -64, freq)
    side = jnp.where(member < 64, 1.0, -1.0)
    part = jnp.stack(
        [
            freq.astype(f32),
            jnp.where(special, 1.0, 0.0),
            jnp.where(special, 0.0, side),
            jnp.where(special, 1.0, 2.0),
        ]
    ).astype(f32)
    return pl.pallas_call(
        wave_kernel,
        out_shape=jax.ShapeDtypeStruct((128, 3, 128), f32),
        in_specs=[pl.BlockSpec(memory_space=pltpu.SMEM)] + vmem(6),
        out_specs=pl.BlockSpec(memory_space=pltpu.VMEM),
        scratch_shapes=[pltpu.VMEM((128, 256), f32)],
        compiler_params=pltpu.CompilerParams(vmem_limit_bytes=VMEM_LIMIT),
        name="wave",
    )(
        part, spec, table["outer"], table["outer_back"], table["inner"],
        table["inner_back"], table["twist"],
    )


ERFC_SHIFT = 4.0
ERFC_POLY = (
    -5.9986000529477224e-05, 1.1337793270330845, 4.308175452878655, 20.093023854033866,
    -8.594175483206275, 489.91788674098177, -1701.7584635921016, 1704.126720738659,
)


def pair_scalars(s2):
    u = lax.rsqrt(s2)
    gauss = jnp.exp2(s2 * (-0.25 * math.log2(math.e)))
    t = pl.reciprocal(s2 * u + ERFC_SHIFT, approx=True)
    w = ERFC_POLY[-1]
    for coefficient in ERFC_POLY[-2::-1]:
        w = w * t + coefficient
    u2 = u * u
    wu = w * u
    along = gauss * (wu * (0.0625 * u2 + 0.375) + 0.125)
    across = (gauss * u2) * (wu * (0.375 - 0.1875 * u2) - 0.125)
    return along, across


def both_halves(v):
    low_half = lax.broadcasted_iota(jnp.int32, (1, 128), 1) < 64
    other = pltpu.roll(v, 64, 1)
    return jnp.where(low_half, v, other), jnp.where(low_half, other, v)


def stage_nodes(ref, weight_stage, right_stage):
    x = [ref[c] for c in range(3)]
    f = [ref[3 + c] for c in range(3)]
    xf = x[0] * f[0] + x[1] * f[1] + x[2] * f[2]
    rows = f + [xf]
    rows += [x[a] * f[b] for a in range(3) for b in range(3)]
    rows += [x[a] * xf for a in range(3)]
    for c, plane in enumerate(rows):
        weight_stage[pl.ds(c, 128, stride=16), :] = plane
    norm = x[0] * x[0] + x[1] * x[1] + x[2] * x[2]
    first, second = [], []
    for h, m, l in [split3(v) for v in x]:
        first += [h, h, m, m, h, l]
        second += [h, m, h, m, l, h]
    one = jnp.ones((128, 128), f32)
    first = [-2.0 * v for v in first] + list(split3(norm)) + [one] * 3
    second += [one] * 3 + list(split3(norm + 0.25))
    for c, plane in enumerate(second):
        right_stage[pl.ds(c, 128, stride=FEATURES), :] = plane
    return first


def build_tables(base, weight_stage, right_stage, weight_ref, right_ref):
    blank = jnp.zeros((32 - FEATURES, 128), f32)

    def build(r, _):
        w = weight_stage[pl.ds(pl.multiple_of(r * 16, 8), 16), :]
        for k, v in enumerate(both_halves(w)):
            hi = v.astype(bf16)
            lo = (v - hi.astype(f32)).astype(bf16)
            weight_ref[base + 2 * r + k] = jnp.concatenate([hi, lo], axis=0)
        w = right_stage[pl.ds(pl.multiple_of(r * FEATURES, 8), FEATURES), :]
        for k, v in enumerate(both_halves(w)):
            right_ref[base + 2 * r + k] = jnp.concatenate([v, blank], axis=0).astype(bf16)
        return 0

    lax.fori_loop(0, 128, build, 0, unroll=16)


def build_left(first, left_stage, left_ref):
    for c, plane in enumerate(first):
        left_stage[pl.ds(c, 128, stride=FEATURES), :] = plane
    eye = jnp.where(
        lax.broadcasted_iota(jnp.int32, (128, 128), 0)
        == lax.broadcasted_iota(jnp.int32, (128, 128), 1),
        1.0,
        0.0,
    ).astype(bf16)
    blank = jnp.zeros((32 - FEATURES, 128), f32)

    def turn_left(r, _):
        v = left_stage[pl.ds(pl.multiple_of(r * FEATURES, 8), FEATURES), :]
        v = jnp.concatenate([v, blank], axis=0).astype(bf16)
        nodes = dot_t(eye, jnp.concatenate([v] * 4, axis=0)).astype(bf16)
        left_ref[2 * r] = nodes[0:64]
        left_ref[2 * r + 1] = nodes[64:128]
        return 0

    lax.fori_loop(0, 128, turn_left, 0, unroll=8)


def pair_kernel(
    list_ref, count_ref, own_ref, beside_ref, own_vel_ref, far_vel_ref,
    weight_ref, right_ref, left_ref, weight_stage, right_stage, left_stage,
    near_acc, far_acc, s2_a, s2_b, tile_a, tile_b,
):
    first = stage_nodes(own_ref, weight_stage, right_stage)
    build_left(first, left_stage, left_ref)
    build_tables(0, weight_stage, right_stage, weight_ref, right_ref)
    stage_nodes(beside_ref, weight_stage, right_stage)
    build_tables(BLOCKS, weight_stage, right_stage, weight_ref, right_ref)

    lane = lax.broadcasted_iota(jnp.int32, (1, 128), 1)
    low_half = lane < 64
    count = count_ref[0]

    def clear(r, _):
        blank = jnp.zeros((W_ROWS, 128), f32)
        far_acc[pl.ds(pl.multiple_of(r * 2 * W_ROWS, 8), W_ROWS), :] = blank
        far_acc[pl.ds(pl.multiple_of(r * 2 * W_ROWS + W_ROWS, 8), W_ROWS), :] = blank
        near_acc[pl.ds(pl.multiple_of(r * W_ROWS, 8), W_ROWS), :] = blank
        return 0

    lax.fori_loop(0, BLOCKS, clear, 0, unroll=8)

    wide = lax.broadcasted_iota(jnp.int32, (64, 128), 1)
    wide_low = wide < 64
    wide_even = (wide & 32) == 0
    narrow = lax.broadcasted_iota(jnp.int32, (32, 128), 1) < 64
    nothing = jnp.zeros((32, 128), bf16)

    def half_of(v, half):
        return jnp.where(narrow, nothing, v) if half else jnp.where(narrow, v, nothing)

    half_keep = [(lane >> 6) == s for s in range(2)]
    blank = jnp.zeros((64, 128), bf16)

    def blocks_of(pair):
        return list_ref[0, pair], list_ref[1, pair]

    def distance_dots(step):
        found = []
        for g in range(GROUPS):
            pairs = [blocks_of((step * GROUPS + g) * STEP + s) for s in range(STEP)]
            left = [left_ref[pairs[s][0]] for s in range(STEP)]
            left = jnp.where(
                wide_low,
                jnp.where(wide_even, left[0], left[1]),
                jnp.where(wide_even, left[2], left[3]),
            )
            right = [half_of(right_ref[pairs[s][1]], s % 2) for s in range(STEP)]
            right = jnp.concatenate(
                [
                    jnp.concatenate([right[0], right[1], blank], axis=0),
                    jnp.concatenate([blank, right[2], right[3]], axis=0),
                ],
                axis=1,
            )
            found.append(dot(left, right))
        return found

    def scalars(s2_ref, tile_ref, pack):
        half = pack % 2
        along, across = pair_scalars(s2_ref[pack // 2, :, half * 128 : (half + 1) * 128])
        for at, value in ((0, across), (128, along)):
            hi, lo = split2(value)
            tile_ref[pack, at : at + 64, :] = hi
            tile_ref[pack, at + 64 : at + 128, :] = lo

    def sum_dots(step, tile_ref, pack):
        tile = tile_ref[pack]
        pairs = [blocks_of((step * 2 * GROUPS + pack) * 2 + s) for s in range(2)]
        a = jnp.concatenate([weight_ref[i] for i, _ in pairs], axis=0)
        b = jnp.concatenate(
            [half_of(weight_ref[j], s) for s, (_, j) in enumerate(pairs)], axis=0
        )
        to_far = dot(a, jnp.concatenate([tile[0:128], tile[128:256]], axis=1))
        return dot_t(b, tile), to_far

    def add_sums(step, pack, to_near, to_far):
        for s in range(2):
            number = (step * 2 * GROUPS + pack) * 2 + s
            for out, acc_ref, row, keep in (
                (to_near, near_acc, list_ref[2, number], None),
                (to_far, far_acc, list_ref[3, number], half_keep[s]),
            ):
                top = 32 * s
                add_h = out[top : top + 16, 0:128] + out[top + 16 : top + 32, 0:128]
                add_f = out[top : top + 8, 128:256] + out[top + 16 : top + 24, 128:256]
                add = jnp.concatenate([add_h, add_f], axis=0)
                if keep is not None:
                    add = jnp.where(keep, add, 0.0)
                acc_ref[pl.ds(pl.multiple_of(row, 8), W_ROWS), :] += add

    packs = range(2 * GROUPS)

    def keep_distances(found, s2_ref):
        for g in range(GROUPS):
            s2_ref[g] = found[g]

    def stage(k, s2_next, s2_now, tile_now, tile_last):
        for pack in packs:
            scalars(s2_now, tile_now, pack)
        for pack in packs:
            add_sums(k - 1, pack, *sum_dots(k - 1, tile_last, pack))
        keep_distances(distance_dots(k + 1), s2_next)

    steps = (count + (STEP * GROUPS - 1)) // (STEP * GROUPS)
    keep_distances(distance_dots(0), s2_a)
    for pack in packs:
        scalars(s2_a, tile_a, pack)
    keep_distances(distance_dots(1), s2_b)

    def body(j, _):
        k = 2 * j + 1
        stage(k, s2_a, s2_b, tile_b, tile_a)
        stage(k + 1, s2_b, s2_a, tile_a, tile_b)
        return 0

    lax.fori_loop(0, (steps + 1) // 2, body, 0)

    chunk = 32
    for side, ref, out_ref in ((0, own_ref, own_vel_ref), (1, beside_ref, far_vel_ref)):
        for top in range(0, 128, chunk):
            planes = []
            for c in range(19):
                at = (2 * top) * W_ROWS + c
                even = far_acc[pl.ds(side * BLOCKS * W_ROWS + at, chunk, stride=2 * W_ROWS), :]
                at += W_ROWS
                odd = far_acc[pl.ds(side * BLOCKS * W_ROWS + at, chunk, stride=2 * W_ROWS), :]
                if side == 0:
                    even += near_acc[pl.ds(at - W_ROWS, chunk, stride=2 * W_ROWS), :]
                    odd += near_acc[pl.ds(at, chunk, stride=2 * W_ROWS), :]
                even = even + pltpu.roll(even, 64, 1)
                odd = odd + pltpu.roll(odd, 64, 1)
                planes.append(jnp.where(low_half, even, odd))
            x = [ref[c, top : top + chunk, :] for c in range(3)]
            h_f, h_xf, h_x_f, h_x_xf, along = (
                planes[0:3], planes[3], planes[4:13], planes[13:16], planes[16:19],
            )
            x_h_f = x[0] * h_f[0] + x[1] * h_f[1] + x[2] * h_f[2] - h_xf
            for c in range(3):
                out_ref[c, top : top + chunk, :] = (
                    along[c]
                    + x[c] * x_h_f
                    - (x[0] * h_x_f[3 * c] + x[1] * h_x_f[3 * c + 1] + x[2] * h_x_f[3 * c + 2])
                    + h_x_xf[c]
                )


def pair_lists(first_list, second_list, count):
    live = jnp.arange(PAIRS, dtype=jnp.int32) < count
    lists = jnp.stack(
        [
            first_list,
            second_list,
            jnp.where(live, first_list, BLOCKS) * W_ROWS,
            jnp.where(live & (first_list != second_list), second_list, 2 * BLOCKS) * W_ROWS,
        ]
    )
    spare = jnp.array([0, 0, BLOCKS * W_ROWS, 2 * BLOCKS * W_ROWS], jnp.int32)
    return jnp.concatenate([lists, jnp.broadcast_to(spare[:, None], (4, 128))], axis=1)


def pair_velocities(own, beside, lists, count):
    plane = jax.ShapeDtypeStruct((3, 128, 128), f32)
    return pl.pallas_call(
        pair_kernel,
        out_shape=[plane, plane],
        in_specs=[pl.BlockSpec(memory_space=pltpu.SMEM)] * 2 + vmem(2),
        out_specs=vmem(2),
        scratch_shapes=[
            pltpu.VMEM((2 * BLOCKS, 32, 128), bf16),
            pltpu.VMEM((2 * BLOCKS, 32, 128), bf16),
            pltpu.VMEM((BLOCKS, 64, 128), bf16),
            pltpu.VMEM((128 * 16, 128), f32),
            pltpu.VMEM((128 * FEATURES, 128), f32),
            pltpu.VMEM((128 * FEATURES, 128), f32),
            pltpu.VMEM(((BLOCKS + 1) * W_ROWS, 128), f32),
            pltpu.VMEM(((2 * BLOCKS + 1) * W_ROWS, 128), f32),
            pltpu.VMEM((GROUPS, 64, 256), f32),
            pltpu.VMEM((GROUPS, 64, 256), f32),
            pltpu.VMEM((2 * GROUPS, 256, 128), bf16),
            pltpu.VMEM((2 * GROUPS, 256, 128), bf16),
        ],
        compiler_params=pltpu.CompilerParams(vmem_limit_bytes=PAIR_VMEM),
        cost_estimate=cost(50),
        name="pairs",
    )(lists, count, own, beside)


def reply_kernel(
    members, n_gx, n_gy, own_ref, far_ref, wave_ref, order_ref, z_ref, in_ref, out_ref,
    beside_ref, hi_ref, lo_ref, low_a, low_b, send_sem, recv_sem, far_send, far_recv,
):
    g_x = lax.axis_index("gx")
    me = g_x * n_gy + lax.axis_index("gy")
    greet_all(me, n_gy, members)
    waves = []
    for c in range(3):
        kind = 0 if c < 2 else 1
        hi, lo = split2(jnp.transpose(wave_ref[:, c, :]))
        waves.append(own_ref[c] + dot3(hi, lo, z_ref[0, kind], z_ref[1, kind]))
    wait_for_all(members)
    far = pltpu.make_async_remote_copy(
        src_ref=far_ref,
        dst_ref=beside_ref,
        send_sem=far_send,
        recv_sem=far_recv,
        device_id=(lax.rem(g_x + 1, n_gx), lax.axis_index("gy")),
        device_id_type=pl.DeviceIdType.MESH,
    )
    far.start()
    far.wait()
    for c in range(3):
        fill_table(c, waves[c] + beside_ref[c], hi_ref, lo_ref)

    def row_at(g, n):
        return lax.rem(me + 1 + g * WIDTH + n, members)

    def put(g, c, n, row):
        there = row_at(g, n)
        out_ref[there, c : c + 1, :] = row
        if c == 2:
            go = partial(send_row, out_ref, in_ref, me, there, n_gy, send_sem, recv_sem)
            pl.when(g * WIDTH + n < members - 1)(go)

    gather_rows(
        3, members // WIDTH, row_at, hi_ref, lo_ref, order_ref, (low_a, low_b), put
    )
    in_ref[me] = out_ref[me]
    wait_rows(out_ref, in_ref, members, send_sem, recv_sem)


def reply_message(own_vel, far_vel, wave, order, z_table):
    n_gx, n_gy = lax.axis_size("gx"), lax.axis_size("gy")
    members = n_gx * n_gy
    return pl.pallas_call(
        partial(reply_kernel, members, n_gx, n_gy),
        out_shape=jax.ShapeDtypeStruct((128, 3, 128), f32),
        in_specs=vmem(5),
        out_specs=pl.BlockSpec(memory_space=pltpu.VMEM),
        scratch_shapes=[
            pltpu.VMEM((128, 3, 128), f32),
            pltpu.VMEM((3, 128, 128), f32),
            pltpu.VMEM((192, 256), bf16),
            pltpu.VMEM((192, 256), bf16),
            pltpu.VMEM((256, WIDTH * 128), bf16),
            pltpu.VMEM((256, WIDTH * 128), bf16),
            pltpu.SemaphoreType.DMA,
            pltpu.SemaphoreType.DMA,
            pltpu.SemaphoreType.DMA,
            pltpu.SemaphoreType.DMA,
        ],
        compiler_params=pltpu.CompilerParams(
            vmem_limit_bytes=VMEM_LIMIT, collective_id=2, has_side_effects=True
        ),
        name="reply",
    )(own_vel, far_vel, wave, order, z_table)


def move_kernel(
    in_ref, route_ref, pos_ref, noise_ref, moved_ref, drift_ref, hi_ref, lo_ref, vel_ref, low_a,
    low_b,
):
    rows = route_ref.shape[0]
    for c in range(3):
        fill_table(c, in_ref[:, c, :], hi_ref, lo_ref)

    def row_at(g, n):
        return g * WIDTH + n

    def put(g, c, n, row):
        vel_ref[c, pl.ds(row_at(g, n), 1), :] = row

    gather_rows(3, rows // WIDTH, row_at, hi_ref, lo_ref, route_ref, (low_a, low_b), put)
    for c in range(3):
        for r in range(rows):
            drift_ref[c : c + 1, r * 128 : (r + 1) * 128] = time_step * vel_ref[c, r : r + 1, :]
    moved_ref[...] = pos_ref[...] + drift_ref[...] + noise_ref[...]


def move_beads(arrived, route, positions, noise):
    flat = jax.ShapeDtypeStruct(positions.shape, f32)
    return pl.pallas_call(
        move_kernel,
        out_shape=[flat, flat],
        in_specs=vmem(4),
        out_specs=vmem(2),
        scratch_shapes=[
            pltpu.VMEM((192, 256), bf16),
            pltpu.VMEM((192, 256), bf16),
            pltpu.VMEM((3, 64, 128), f32),
            pltpu.VMEM((256, WIDTH * 128), bf16),
            pltpu.VMEM((256, WIDTH * 128), bf16),
        ],
        compiler_params=pltpu.CompilerParams(vmem_limit_bytes=VMEM_LIMIT),
        name="move",
    )(arrived, route, positions, noise)


def exchange(value):
    return lax.all_to_all(value, ("gx", "gy"), split_axis=0, concat_axis=0, tiled=True)


def shards(positions, noise, route, node_perm, pair_first, pair_second, pair_count):
    table = {name: jnp.asarray(value) for name, value in tables().items()}
    row_gx = lax.axis_index("gx")
    member = row_gx * lax.axis_size("gy") + lax.axis_index("gy")
    route = route.reshape(64, 128)
    order = lax.dynamic_index_in_dim(node_perm, row_gx, 0, keepdims=False).reshape(128, 128)
    grid, beside, spec = arrive_on_grid(positions, route, order, table["z"])
    wave = wave_flow(spec, table, member)
    grid, wave = lax.optimization_barrier((grid, wave))
    wave = exchange(wave)
    lists = pair_lists(pair_first[0], pair_second[0], pair_count[0])
    own_vel, far_vel = pair_velocities(grid, beside, lists, pair_count)
    reply = reply_message(own_vel, far_vel, wave, order, table["z"])
    return tuple(move_beads(reply, route, positions, noise))


def solution(mesh):
    in_specs = (
        P(None, ("gx", "gy")),
        P(None, ("gx", "gy")),
        P(("gx", "gy")),
        P(None, "gy", None),
        P(("gx", "gy"), None),
        P(("gx", "gy"), None),
        P(("gx", "gy")),
    )
    out_specs = (P(None, ("gx", "gy")), P(None, ("gx", "gy")))
    return jax.shard_map(shards, mesh=mesh, in_specs=in_specs, out_specs=out_specs, check_vma=False)
```

```python
from functools import partial
import math

import numpy as np
import jax
import jax.numpy as jnp
from jax import lax
from jax.experimental import pallas as pl
from jax.experimental.pallas import tpu as pltpu
from jax.sharding import PartitionSpec as P

G = 128
BLOCKS = 256
PAIRS = 1024
STEP = 4
W_ROWS = 24
GROUPS = 2
FEATURES = 24

fene_k = 30.0
fene_reach = 1.5
bend_k = 2.0
time_step = 0.01
grid_spacing = 4.0

f32 = jnp.float32
bf16 = jnp.bfloat16
VMEM_LIMIT = 24 * 1024 * 1024
PAIR_VMEM = 40 * 1024 * 1024


def dot(a, b):
    return lax.dot_general(a, b, (((1,), (0,)), ((), ())), preferred_element_type=f32)


def dot_t(a, b):
    return lax.dot_general(a, b, (((1,), (1,)), ((), ())), preferred_element_type=f32)


def split2(x):
    hi = x.astype(bf16)
    return hi, (x - hi.astype(f32)).astype(bf16)


def split3(x):
    hi = x.astype(bf16).astype(f32)
    rest = x - hi
    mid = rest.astype(bf16).astype(f32)
    return hi, mid, (rest - mid).astype(bf16).astype(f32)


def dot3(a_hi, a_lo, b_hi, b_lo, form=dot):
    return form(a_hi, b_hi) + form(a_hi, b_lo) + form(a_lo, b_hi)


def split_table(table):
    table = np.asarray(table, np.float64)
    hi = table.astype(np.float32).astype(jnp.bfloat16)
    lo = (table - hi.astype(np.float64)).astype(np.float32).astype(jnp.bfloat16)
    return np.stack([hi, lo])


def tables():
    n = np.arange(G)
    turn = 2.0 * np.pi / G
    member = np.arange(128)
    freq = np.where(member < 64, member + 1, (member - 63) % 64)
    wave = turn * (freq[:, None] * n[None, :] % G)
    even, odd = np.cos(wave), -np.sin(wave)
    special = (member % 64) == 63
    first = (member < 64)[:, None]
    even = np.where(special[:, None], np.cos(wave), even)
    z_xy = np.where(special[:, None] | first, even, odd)
    z_z = np.where(special[:, None] | ~first, even, odd)
    k1, k2 = n // 8, n % 8
    outer = 2.0 * np.pi * (k1[:, None] * k1[None, :] / 16.0 + k2[:, None] * k2[None, :] / 8.0)
    a, b = n // 16, n % 16
    inner = 2.0 * np.pi * (a[:, None] * a[None, :] / 8.0 + b[:, None] * b[None, :] / 16.0)
    twist = turn * (k1[:, None] * a[None, :] + k2[:, None] * b[None, :])
    c_out, s_out, c_in, s_in = np.cos(outer), np.sin(outer), np.cos(inner), np.sin(inner)
    return {
        "z": split_table(np.stack([z_xy, z_z])),
        "outer": split_table(np.concatenate([c_out, -s_out], 0)),
        "outer_back": split_table(np.concatenate([c_out, -s_out], 1)),
        "inner": split_table(np.block([[c_in, -s_in], [s_in, c_in]])),
        "inner_back": split_table(np.block([[c_in, s_in], [-s_in, c_in]])),
        "twist": np.stack([np.cos(twist), np.sin(twist)]).astype(np.float32),
    }


def cost(micros):
    return pl.CostEstimate(flops=int(micros * 1e9), bytes_accessed=1 << 20, transcendentals=0)


def onehot(index, size, width):
    rows = lax.broadcasted_iota(jnp.int32, (size, width), 0)
    return jnp.where(rows == index, 1.0, 0.0).astype(bf16)


def high_part(place):
    return (place >> 7) & 63


def low_part(place):
    return ((place >> 13) << 7) | (place & 127)


WIDTH = 4


def scatter_rows(channels, rows, value_row, place_ref, left_ref, sum_ref):
    group = left_ref.shape[1] // 128
    span = 128 * group

    def turn(g, _):
        low = []
        for j in range(group):
            place = place_ref[pl.ds(g * group + j, 1), :]
            high_hot = onehot(high_part(place), 64, 128)
            low.append(onehot(low_part(place), 256, 128))
            for c in range(channels):
                hi, lo = split2(value_row(c, g * group + j))
                left_ref[c * 128 : c * 128 + 64, j * 128 : (j + 1) * 128] = high_hot * hi
                left_ref[c * 128 + 64 : c * 128 + 128, j * 128 : (j + 1) * 128] = high_hot * lo
        moved = dot_t(left_ref[...], jnp.concatenate(low, axis=1))
        for c in range(channels):
            sum_ref[c * 64 : (c + 1) * 64, :] += (
                moved[c * 128 : c * 128 + 64] + moved[c * 128 + 64 : c * 128 + 128]
            )
        return 0

    sum_ref[...] = jnp.zeros_like(sum_ref)
    lax.fori_loop(0, rows // group, turn, 0)


def unpack_sums(channels, sum_ref, put):
    for c in range(channels):
        for half in range(2):
            put(c, half, sum_ref[c * 64 : (c + 1) * 64, half * 128 : (half + 1) * 128])


def gather_rows(channels, turns, row_at, table_hi_ref, table_lo_ref, place_ref, low, put):
    def build(g, side):
        for n in range(WIDTH):
            place = place_ref[pl.ds(row_at(g, n), 1), :]
            low[side][:, n * 128 : (n + 1) * 128] = onehot(low_part(place), 256, 128)

    def use(g, side):
        found = dot(table_hi_ref[...], low[side][...]) + dot(table_lo_ref[...], low[side][...])
        for n in range(WIDTH):
            high = high_part(place_ref[pl.ds(row_at(g, n), 1), :])
            rows_of = lax.broadcasted_iota(jnp.int32, (64, 128), 0) == high
            for c in range(channels):
                part = found[c * 64 : (c + 1) * 64, n * 128 : (n + 1) * 128]
                put(g, c, n, jnp.sum(jnp.where(rows_of, part, 0.0), axis=0, keepdims=True))

    build(0, 0)

    def turn(h, _):
        build(2 * h + 1, 1)
        use(2 * h, 0)
        build(2 * h + 2, 0)
        use(2 * h + 1, 1)
        return 0

    lax.fori_loop(0, turns // 2 - 1, turn, 0)
    build(turns - 1, 1)
    use(turns - 2, 0)
    use(turns - 1, 1)


def fill_table(c, plane, table_hi_ref, table_lo_ref):
    hi, lo = split2(plane)
    for ref, part in ((table_hi_ref, hi), (table_lo_ref, lo)):
        ref[c * 64 : (c + 1) * 64, 0:128] = part[0:64]
        ref[c * 64 : (c + 1) * 64, 128:256] = part[64:128]


def greet_all(me, n_gy, members):
    barrier = pltpu.get_barrier_semaphore()

    def greet(d, _):
        there = lax.rem(me + d, members)
        pl.semaphore_signal(
            barrier,
            inc=1,
            device_id=(there // n_gy, lax.rem(there, n_gy)),
            device_id_type=pl.DeviceIdType.MESH,
        )
        return 0

    lax.fori_loop(1, members, greet, 0)


def wait_for_all(members):
    pl.semaphore_wait(pltpu.get_barrier_semaphore(), members - 1)


def send_row(out_ref, in_ref, me, there, n_gy, send_sem, recv_sem):
    pltpu.make_async_remote_copy(
        src_ref=out_ref.at[there],
        dst_ref=in_ref.at[me],
        send_sem=send_sem,
        recv_sem=recv_sem,
        device_id=(there // n_gy, lax.rem(there, n_gy)),
        device_id_type=pl.DeviceIdType.MESH,
    ).start()


def wait_rows(out_ref, in_ref, members, send_sem, recv_sem):
    every = pltpu.make_async_remote_copy(
        src_ref=out_ref.at[pl.ds(0, members - 1)],
        dst_ref=in_ref.at[pl.ds(0, members - 1)],
        send_sem=send_sem,
        recv_sem=recv_sem,
        device_id=(0, 0),
        device_id_type=pl.DeviceIdType.MESH,
    )
    every.wait_send()
    every.wait_recv()


def chain_forces(x):
    lane = lax.broadcasted_iota(jnp.int32, x[0].shape, 1) & 63
    last = lane == 63
    ahead = lambda v: pltpu.roll(v, 127, 1)
    behind = lambda v: pltpu.roll(v, 1, 1)
    bond = [jnp.where(last, 0.5, ahead(v) - v) for v in x]
    square = bond[0] * bond[0] + bond[1] * bond[1] + bond[2] * bond[2]
    inverse = lax.rsqrt(square)
    unit = [v * inverse for v in bond]
    following = [ahead(v) for v in unit]
    cosine = unit[0] * following[0] + unit[1] * following[1] + unit[2] * following[2]
    bends = lane < 62
    stretch = fene_k / (1.0 - square / fene_reach**2)
    before = behind(jnp.where(bends, 1.0, 0.0))
    cosine_before = behind(cosine)
    grad = []
    for c in range(3):
        pull = jnp.where(bends, following[c] - cosine * unit[c], 0.0)
        push = before * (behind(unit[c]) - cosine_before * unit[c])
        push = jnp.where(lane == 0, 0.0, push)
        grad.append(
            jnp.where(last, 0.0, stretch * bond[c] - bend_k * inverse * (pull + push))
        )
    return [g - jnp.where(lane == 0, 0.0, behind(g)) for g in grad]


def send_kernel(
    members, n_gy, pos_ref, route_ref, in_ref, out_ref, plane_ref, left_ref, sum_ref, send_sem,
    recv_sem,
):
    me = lax.axis_index("gx") * n_gy + lax.axis_index("gy")
    greet_all(me, n_gy, members)
    rows = route_ref.shape[0]
    for c in range(3):
        for r in range(rows):
            plane_ref[c, r : r + 1, :] = pos_ref[c : c + 1, r * 128 : (r + 1) * 128]
    forces = chain_forces([plane_ref[c] for c in range(3)])
    for c in range(3):
        plane_ref[3 + c] = forces[c]
    scatter_rows(
        6, rows, lambda c, r: plane_ref[c, pl.ds(r, 1), :], route_ref, left_ref, sum_ref
    )
    for c in range(6):
        out_ref[0:64, c, :] = sum_ref[c * 64 : (c + 1) * 64, 0:128]
        out_ref[64:128, c, :] = sum_ref[c * 64 : (c + 1) * 64, 128:256]
    wait_for_all(members)

    def go(d, _):
        send_row(out_ref, in_ref, me, lax.rem(me + d, members), n_gy, send_sem, recv_sem)
        return 0

    lax.fori_loop(1, members, go, 0)
    in_ref[me] = out_ref[me]
    wait_rows(out_ref, in_ref, members, send_sem, recv_sem)


def vmem(n):
    return [pl.BlockSpec(memory_space=pltpu.VMEM)] * n


def send_message(positions, route):
    n_gy = lax.axis_size("gy")
    members = lax.axis_size("gx") * n_gy
    return pl.pallas_call(
        partial(send_kernel, members, n_gy),
        out_shape=jax.ShapeDtypeStruct((128, 6, 128), f32),
        in_specs=vmem(2),
        out_specs=pl.BlockSpec(memory_space=pltpu.VMEM),
        scratch_shapes=[
            pltpu.VMEM((128, 6, 128), f32),
            pltpu.VMEM((6, 64, 128), f32),
            pltpu.VMEM((768, 1024), bf16),
            pltpu.VMEM((384, 256), f32),
            pltpu.SemaphoreType.DMA,
            pltpu.SemaphoreType.DMA,
        ],
        compiler_params=pltpu.CompilerParams(
            vmem_limit_bytes=VMEM_LIMIT, collective_id=1, has_side_effects=True
        ),
        name="send",
    )(positions, route)


def place_kernel(
    members, n_gx, n_gy, in_ref, order_ref, z_ref, grid_ref, beside_ref, spec_in_ref,
    left_ref, sum_ref, spec_ref, spec_send, spec_recv, side_send, side_recv,
):
    g_x = lax.axis_index("gx")
    me = g_x * n_gy + lax.axis_index("gy")
    greet_all(me, n_gy, members)
    scatter_rows(
        6, members, lambda c, r: in_ref[r, c : c + 1, :], order_ref, left_ref, sum_ref
    )

    def to_grid(c, half, value):
        grid_ref[c, half * 64 : (half + 1) * 64, :] = value

    unpack_sums(6, sum_ref, to_grid)
    for c in range(3):
        hi, lo = split2(grid_ref[3 + c])
        kind = 0 if c < 2 else 1
        spec_ref[:, c, :] = dot3(z_ref[0, kind], z_ref[1, kind], hi, lo, dot_t)
    wait_for_all(members)
    side = pltpu.make_async_remote_copy(
        src_ref=grid_ref,
        dst_ref=beside_ref,
        send_sem=side_send,
        recv_sem=side_recv,
        device_id=(lax.rem(g_x + n_gx - 1, n_gx), lax.axis_index("gy")),
        device_id_type=pl.DeviceIdType.MESH,
    )

    def go(d, _):
        there = lax.rem(me + d, members)
        send_row(spec_ref, spec_in_ref, me, there, n_gy, spec_send, spec_recv)
        return 0

    lax.fori_loop(1, members, go, 0)
    side.start()
    spec_in_ref[me] = spec_ref[me]
    wait_rows(spec_ref, spec_in_ref, members, spec_send, spec_recv)
    side.wait()


def place_on_grid(incoming, order, z_table):
    n_gx, n_gy = lax.axis_size("gx"), lax.axis_size("gy")
    members = n_gx * n_gy
    return pl.pallas_call(
        partial(place_kernel, members, n_gx, n_gy),
        out_shape=[
            jax.ShapeDtypeStruct((6, 128, 128), f32),
            jax.ShapeDtypeStruct((6, 128, 128), f32),
            jax.ShapeDtypeStruct((128, 3, 128), f32),
        ],
        in_specs=vmem(3),
        out_specs=vmem(3),
        scratch_shapes=[
            pltpu.VMEM((768, 1024), bf16),
            pltpu.VMEM((384, 256), f32),
            pltpu.VMEM((128, 3, 128), f32),
            pltpu.SemaphoreType.DMA,
            pltpu.SemaphoreType.DMA,
            pltpu.SemaphoreType.DMA,
            pltpu.SemaphoreType.DMA,
        ],
        compiler_params=pltpu.CompilerParams(
            vmem_limit_bytes=VMEM_LIMIT, collective_id=3, has_side_effects=True
        ),
        name="place",
    )(incoming, order, z_table)


def wave_kernel(
    part_ref, in_ref, outer_ref, outer_back_ref, inner_ref, inner_back_ref, twist_ref,
    out_ref, mid_ref,
):
    freq, turn_re, turn_im, weight = (part_ref[i] for i in range(4))
    cos_t, sin_t = twist_ref[0], twist_ref[1]
    spectrum = []
    for c in range(3):
        hi, lo = split2(in_ref[:, c, :])
        both = dot3(outer_ref[0], outer_ref[1], hi, lo)
        re, im = both[0:128], both[128:256]
        mid_ref[:, 0:128] = re * cos_t + im * sin_t
        mid_ref[:, 128:256] = im * cos_t - re * sin_t
        hi, lo = split2(mid_ref[...])
        both = dot3(hi, lo, inner_ref[0], inner_ref[1])
        spectrum.append((both[:, 0:128], both[:, 128:256]))
    row = lax.broadcasted_iota(jnp.int32, (128, 128), 0)
    col = lax.broadcasted_iota(jnp.int32, (128, 128), 1)
    n_x = (row >> 3) + 16 * (col >> 4)
    n_y = (row & 7) + 8 * (col & 15)
    unit = 2.0 * math.pi / (G * grid_spacing)
    signed = lambda n: jnp.where(n < G // 2, n, n - G).astype(f32) * unit
    k_x, k_y = signed(n_x), signed(n_y)
    k_z = jnp.full((128, 128), freq * unit, f32)
    edge_x = jnp.where(n_x == G // 2, 1.0, 0.0)
    edge_y = jnp.where(n_y == G // 2, 1.0, 0.0)
    edge_z = jnp.where(jnp.full((128, 128), freq, f32) < -63.5, 1.0, 0.0)
    square = k_x * k_x + k_y * k_y + k_z * k_z
    positive = square > 0.0
    safe = jnp.where(positive, square, 1.0)
    green = jnp.where(
        positive,
        (1.0 - 0.25 * square / 3.0) * (1.0 + square) * jnp.exp(-square) / safe,
        0.0,
    ) * (weight / float(G**3))
    over = green / safe
    g_xy = jnp.where(edge_x == edge_y, -over * k_x * k_y, 0.0)
    g_xz = jnp.where(edge_x == edge_z, -over * k_x * k_z, 0.0)
    g_yz = jnp.where(edge_y == edge_z, -over * k_y * k_z, 0.0)
    g_xx = green - over * k_x * k_x
    g_yy = green - over * k_y * k_y
    g_zz = green - over * k_z * k_z
    (x_re, x_im), (y_re, y_im), (z_re, z_im) = spectrum
    z_re, z_im = turn_re * z_re - turn_im * z_im, turn_re * z_im + turn_im * z_re
    flow = [
        (g_xx * x_re + g_xy * y_re + g_xz * z_re, g_xx * x_im + g_xy * y_im + g_xz * z_im),
        (g_xy * x_re + g_yy * y_re + g_yz * z_re, g_xy * x_im + g_yy * y_im + g_yz * z_im),
    ]
    w_re = g_xz * x_re + g_yz * y_re + g_zz * z_re
    w_im = g_xz * x_im + g_yz * y_im + g_zz * z_im
    flow.append((turn_re * w_re + turn_im * w_im, turn_re * w_im - turn_im * w_re))
    for c in range(3):
        mid_ref[:, 0:128], mid_ref[:, 128:256] = flow[c]
        hi, lo = split2(mid_ref[...])
        both = dot3(hi, lo, inner_back_ref[0], inner_back_ref[1])
        re, im = both[:, 0:128], both[:, 128:256]
        hi, lo = split2(
            jnp.concatenate([re * cos_t - im * sin_t, im * cos_t + re * sin_t], axis=0)
        )
        out_ref[:, c, :] = dot3(outer_back_ref[0], outer_back_ref[1], hi, lo)


def wave_flow(spec, table, member):
    special = member % 64 == 63
    freq = jnp.where(member < 64, member + 1, (member - 63) % 64)
    freq = jnp.where(member == 63, -64, freq)
    side = jnp.where(member < 64, 1.0, -1.0)
    part = jnp.stack(
        [
            freq.astype(f32),
            jnp.where(special, 1.0, 0.0),
            jnp.where(special, 0.0, side),
            jnp.where(special, 1.0, 2.0),
        ]
    ).astype(f32)
    return pl.pallas_call(
        wave_kernel,
        out_shape=jax.ShapeDtypeStruct((128, 3, 128), f32),
        in_specs=[pl.BlockSpec(memory_space=pltpu.SMEM)] + vmem(6),
        out_specs=pl.BlockSpec(memory_space=pltpu.VMEM),
        scratch_shapes=[pltpu.VMEM((128, 256), f32)],
        compiler_params=pltpu.CompilerParams(vmem_limit_bytes=VMEM_LIMIT),
        name="wave",
    )(
        part, spec, table["outer"], table["outer_back"], table["inner"],
        table["inner_back"], table["twist"],
    )


ERFC_SHIFT = 4.0
ERFC_POLY = (
    -5.9986000529477224e-05, 1.1337793270330845, 4.308175452878655, 20.093023854033866,
    -8.594175483206275, 489.91788674098177, -1701.7584635921016, 1704.126720738659,
)


def pair_scalars(s2):
    u = lax.rsqrt(s2)
    gauss = jnp.exp2(s2 * (-0.25 * math.log2(math.e)))
    t = pl.reciprocal(s2 * u + ERFC_SHIFT, approx=True)
    w = ERFC_POLY[-1]
    for coefficient in ERFC_POLY[-2::-1]:
        w = w * t + coefficient
    u2 = u * u
    wu = w * u
    along = gauss * (wu * (0.0625 * u2 + 0.375) + 0.125)
    across = (gauss * u2) * (wu * (0.375 - 0.1875 * u2) - 0.125)
    return along, across


def both_halves(v):
    low_half = lax.broadcasted_iota(jnp.int32, (1, 128), 1) < 64
    other = pltpu.roll(v, 64, 1)
    return jnp.where(low_half, v, other), jnp.where(low_half, other, v)


def stage_nodes(ref, weight_stage, right_stage):
    x = [ref[c] for c in range(3)]
    f = [ref[3 + c] for c in range(3)]
    xf = x[0] * f[0] + x[1] * f[1] + x[2] * f[2]
    rows = f + [xf]
    rows += [x[a] * f[b] for a in range(3) for b in range(3)]
    rows += [x[a] * xf for a in range(3)]
    for c, plane in enumerate(rows):
        weight_stage[pl.ds(c, 128, stride=16), :] = plane
    norm = x[0] * x[0] + x[1] * x[1] + x[2] * x[2]
    first, second = [], []
    for h, m, l in [split3(v) for v in x]:
        first += [h, h, m, m, h, l]
        second += [h, m, h, m, l, h]
    one = jnp.ones((128, 128), f32)
    first = [-2.0 * v for v in first] + list(split3(norm)) + [one] * 3
    second += [one] * 3 + list(split3(norm + 0.25))
    for c, plane in enumerate(second):
        right_stage[pl.ds(c, 128, stride=FEATURES), :] = plane
    return first


def build_tables(base, weight_stage, right_stage, weight_ref, right_ref):
    blank = jnp.zeros((32 - FEATURES, 128), f32)

    def build(r, _):
        w = weight_stage[pl.ds(pl.multiple_of(r * 16, 8), 16), :]
        for k, v in enumerate(both_halves(w)):
            hi = v.astype(bf16)
            lo = (v - hi.astype(f32)).astype(bf16)
            weight_ref[base + 2 * r + k] = jnp.concatenate([hi, lo], axis=0)
        w = right_stage[pl.ds(pl.multiple_of(r * FEATURES, 8), FEATURES), :]
        for k, v in enumerate(both_halves(w)):
            right_ref[base + 2 * r + k] = jnp.concatenate([v, blank], axis=0).astype(bf16)
        return 0

    lax.fori_loop(0, 128, build, 0, unroll=16)


def build_left(first, left_stage, left_ref):
    for c, plane in enumerate(first):
        left_stage[pl.ds(c, 128, stride=FEATURES), :] = plane
    eye = jnp.where(
        lax.broadcasted_iota(jnp.int32, (128, 128), 0)
        == lax.broadcasted_iota(jnp.int32, (128, 128), 1),
        1.0,
        0.0,
    ).astype(bf16)
    blank = jnp.zeros((32 - FEATURES, 128), f32)

    def turn_left(r, _):
        v = left_stage[pl.ds(pl.multiple_of(r * FEATURES, 8), FEATURES), :]
        v = jnp.concatenate([v, blank], axis=0).astype(bf16)
        nodes = dot_t(eye, jnp.concatenate([v] * 4, axis=0)).astype(bf16)
        left_ref[2 * r] = nodes[0:64]
        left_ref[2 * r + 1] = nodes[64:128]
        return 0

    lax.fori_loop(0, 128, turn_left, 0, unroll=8)


def pair_kernel(
    list_ref, count_ref, own_ref, beside_ref, own_vel_ref, far_vel_ref,
    weight_ref, right_ref, left_ref, weight_stage, right_stage, left_stage,
    near_acc, far_acc, s2_a, s2_b, tile_a, tile_b,
):
    first = stage_nodes(own_ref, weight_stage, right_stage)
    build_left(first, left_stage, left_ref)
    build_tables(0, weight_stage, right_stage, weight_ref, right_ref)
    stage_nodes(beside_ref, weight_stage, right_stage)
    build_tables(BLOCKS, weight_stage, right_stage, weight_ref, right_ref)

    lane = lax.broadcasted_iota(jnp.int32, (1, 128), 1)
    low_half = lane < 64
    count = count_ref[0]

    def clear(r, _):
        blank = jnp.zeros((W_ROWS, 128), f32)
        far_acc[pl.ds(pl.multiple_of(r * 2 * W_ROWS, 8), W_ROWS), :] = blank
        far_acc[pl.ds(pl.multiple_of(r * 2 * W_ROWS + W_ROWS, 8), W_ROWS), :] = blank
        near_acc[pl.ds(pl.multiple_of(r * W_ROWS, 8), W_ROWS), :] = blank
        return 0

    lax.fori_loop(0, BLOCKS, clear, 0, unroll=8)

    wide = lax.broadcasted_iota(jnp.int32, (64, 128), 1)
    wide_low = wide < 64
    wide_even = (wide & 32) == 0
    narrow = lax.broadcasted_iota(jnp.int32, (32, 128), 1) < 64
    nothing = jnp.zeros((32, 128), bf16)

    def half_of(v, half):
        return jnp.where(narrow, nothing, v) if half else jnp.where(narrow, v, nothing)

    half_keep = [(lane >> 6) == s for s in range(2)]
    blank = jnp.zeros((64, 128), bf16)

    def blocks_of(pair):
        return list_ref[0, pair], list_ref[1, pair]

    def distance_dots(step):
        found = []
        for g in range(GROUPS):
            pairs = [blocks_of((step * GROUPS + g) * STEP + s) for s in range(STEP)]
            left = [left_ref[pairs[s][0]] for s in range(STEP)]
            left = jnp.where(
                wide_low,
                jnp.where(wide_even, left[0], left[1]),
                jnp.where(wide_even, left[2], left[3]),
            )
            right = [half_of(right_ref[pairs[s][1]], s % 2) for s in range(STEP)]
            right = jnp.concatenate(
                [
                    jnp.concatenate([right[0], right[1], blank], axis=0),
                    jnp.concatenate([blank, right[2], right[3]], axis=0),
                ],
                axis=1,
            )
            found.append(dot(left, right))
        return found

    def scalars(s2_ref, tile_ref, pack):
        half = pack % 2
        along, across = pair_scalars(s2_ref[pack // 2, :, half * 128 : (half + 1) * 128])
        for at, value in ((0, across), (128, along)):
            hi, lo = split2(value)
            tile_ref[pack, at : at + 64, :] = hi
            tile_ref[pack, at + 64 : at + 128, :] = lo

    def sum_dots(step, tile_ref, pack):
        tile = tile_ref[pack]
        pairs = [blocks_of((step * 2 * GROUPS + pack) * 2 + s) for s in range(2)]
        a = jnp.concatenate([weight_ref[i] for i, _ in pairs], axis=0)
        b = jnp.concatenate(
            [half_of(weight_ref[j], s) for s, (_, j) in enumerate(pairs)], axis=0
        )
        to_far = dot(a, jnp.concatenate([tile[0:128], tile[128:256]], axis=1))
        return dot_t(b, tile), to_far

    def add_sums(step, pack, to_near, to_far):
        for s in range(2):
            number = (step * 2 * GROUPS + pack) * 2 + s
            for out, acc_ref, row, keep in (
                (to_near, near_acc, list_ref[2, number], None),
                (to_far, far_acc, list_ref[3, number], half_keep[s]),
            ):
                top = 32 * s
                add_h = out[top : top + 16, 0:128] + out[top + 16 : top + 32, 0:128]
                add_f = out[top : top + 8, 128:256] + out[top + 16 : top + 24, 128:256]
                add = jnp.concatenate([add_h, add_f], axis=0)
                if keep is not None:
                    add = jnp.where(keep, add, 0.0)
                acc_ref[pl.ds(pl.multiple_of(row, 8), W_ROWS), :] += add

    packs = range(2 * GROUPS)

    def keep_distances(found, s2_ref):
        for g in range(GROUPS):
            s2_ref[g] = found[g]

    def stage(k, s2_next, s2_now, tile_now, tile_last):
        for pack in packs:
            scalars(s2_now, tile_now, pack)
        for pack in packs:
            add_sums(k - 1, pack, *sum_dots(k - 1, tile_last, pack))
        keep_distances(distance_dots(k + 1), s2_next)

    steps = (count + (STEP * GROUPS - 1)) // (STEP * GROUPS)
    keep_distances(distance_dots(0), s2_a)
    for pack in packs:
        scalars(s2_a, tile_a, pack)
    keep_distances(distance_dots(1), s2_b)

    def body(j, _):
        k = 2 * j + 1
        stage(k, s2_a, s2_b, tile_b, tile_a)
        stage(k + 1, s2_b, s2_a, tile_a, tile_b)
        return 0

    lax.fori_loop(0, (steps + 1) // 2, body, 0)

    chunk = 32
    for side, ref, out_ref in ((0, own_ref, own_vel_ref), (1, beside_ref, far_vel_ref)):
        for top in range(0, 128, chunk):
            planes = []
            for c in range(19):
                at = (2 * top) * W_ROWS + c
                even = far_acc[pl.ds(side * BLOCKS * W_ROWS + at, chunk, stride=2 * W_ROWS), :]
                at += W_ROWS
                odd = far_acc[pl.ds(side * BLOCKS * W_ROWS + at, chunk, stride=2 * W_ROWS), :]
                if side == 0:
                    even += near_acc[pl.ds(at - W_ROWS, chunk, stride=2 * W_ROWS), :]
                    odd += near_acc[pl.ds(at, chunk, stride=2 * W_ROWS), :]
                even = even + pltpu.roll(even, 64, 1)
                odd = odd + pltpu.roll(odd, 64, 1)
                planes.append(jnp.where(low_half, even, odd))
            x = [ref[c, top : top + chunk, :] for c in range(3)]
            h_f, h_xf, h_x_f, h_x_xf, along = (
                planes[0:3], planes[3], planes[4:13], planes[13:16], planes[16:19],
            )
            x_h_f = x[0] * h_f[0] + x[1] * h_f[1] + x[2] * h_f[2] - h_xf
            for c in range(3):
                out_ref[c, top : top + chunk, :] = (
                    along[c]
                    + x[c] * x_h_f
                    - (x[0] * h_x_f[3 * c] + x[1] * h_x_f[3 * c + 1] + x[2] * h_x_f[3 * c + 2])
                    + h_x_xf[c]
                )


def pair_lists(first_list, second_list, count):
    live = jnp.arange(PAIRS, dtype=jnp.int32) < count
    lists = jnp.stack(
        [
            first_list,
            second_list,
            jnp.where(live, first_list, BLOCKS) * W_ROWS,
            jnp.where(live & (first_list != second_list), second_list, 2 * BLOCKS) * W_ROWS,
        ]
    )
    spare = jnp.array([0, 0, BLOCKS * W_ROWS, 2 * BLOCKS * W_ROWS], jnp.int32)
    return jnp.concatenate([lists, jnp.broadcast_to(spare[:, None], (4, 128))], axis=1)


def pair_velocities(own, beside, lists, count):
    plane = jax.ShapeDtypeStruct((3, 128, 128), f32)
    return pl.pallas_call(
        pair_kernel,
        out_shape=[plane, plane],
        in_specs=[pl.BlockSpec(memory_space=pltpu.SMEM)] * 2 + vmem(2),
        out_specs=vmem(2),
        scratch_shapes=[
            pltpu.VMEM((2 * BLOCKS, 32, 128), bf16),
            pltpu.VMEM((2 * BLOCKS, 32, 128), bf16),
            pltpu.VMEM((BLOCKS, 64, 128), bf16),
            pltpu.VMEM((128 * 16, 128), f32),
            pltpu.VMEM((128 * FEATURES, 128), f32),
            pltpu.VMEM((128 * FEATURES, 128), f32),
            pltpu.VMEM(((BLOCKS + 1) * W_ROWS, 128), f32),
            pltpu.VMEM(((2 * BLOCKS + 1) * W_ROWS, 128), f32),
            pltpu.VMEM((GROUPS, 64, 256), f32),
            pltpu.VMEM((GROUPS, 64, 256), f32),
            pltpu.VMEM((2 * GROUPS, 256, 128), bf16),
            pltpu.VMEM((2 * GROUPS, 256, 128), bf16),
        ],
        compiler_params=pltpu.CompilerParams(vmem_limit_bytes=PAIR_VMEM),
        cost_estimate=cost(50),
        name="pairs",
    )(lists, count, own, beside)


def reply_kernel(
    members, n_gx, n_gy, own_ref, far_ref, wave_ref, order_ref, z_ref, in_ref, out_ref,
    beside_ref, hi_ref, lo_ref, low_a, low_b, send_sem, recv_sem, far_send, far_recv,
):
    g_x = lax.axis_index("gx")
    me = g_x * n_gy + lax.axis_index("gy")
    greet_all(me, n_gy, members)
    waves = []
    for c in range(3):
        kind = 0 if c < 2 else 1
        hi, lo = split2(jnp.transpose(wave_ref[:, c, :]))
        waves.append(own_ref[c] + dot3(hi, lo, z_ref[0, kind], z_ref[1, kind]))
    wait_for_all(members)
    far = pltpu.make_async_remote_copy(
        src_ref=far_ref,
        dst_ref=beside_ref,
        send_sem=far_send,
        recv_sem=far_recv,
        device_id=(lax.rem(g_x + 1, n_gx), lax.axis_index("gy")),
        device_id_type=pl.DeviceIdType.MESH,
    )
    far.start()
    far.wait()
    for c in range(3):
        fill_table(c, waves[c] + beside_ref[c], hi_ref, lo_ref)

    def row_at(g, n):
        return g * WIDTH + n

    def put(g, c, n, row):
        out_ref[row_at(g, n), c : c + 1, :] = row

    gather_rows(
        3, members // WIDTH, row_at, hi_ref, lo_ref, order_ref, (low_a, low_b), put
    )

    def go(d, _):
        send_row(out_ref, in_ref, me, lax.rem(me + d, members), n_gy, send_sem, recv_sem)
        return 0

    lax.fori_loop(1, members, go, 0)
    in_ref[me] = out_ref[me]
    wait_rows(out_ref, in_ref, members, send_sem, recv_sem)


def reply_message(own_vel, far_vel, wave, order, z_table):
    n_gx, n_gy = lax.axis_size("gx"), lax.axis_size("gy")
    members = n_gx * n_gy
    return pl.pallas_call(
        partial(reply_kernel, members, n_gx, n_gy),
        out_shape=jax.ShapeDtypeStruct((128, 3, 128), f32),
        in_specs=vmem(5),
        out_specs=pl.BlockSpec(memory_space=pltpu.VMEM),
        scratch_shapes=[
            pltpu.VMEM((128, 3, 128), f32),
            pltpu.VMEM((3, 128, 128), f32),
            pltpu.VMEM((192, 256), bf16),
            pltpu.VMEM((192, 256), bf16),
            pltpu.VMEM((256, WIDTH * 128), bf16),
            pltpu.VMEM((256, WIDTH * 128), bf16),
            pltpu.SemaphoreType.DMA,
            pltpu.SemaphoreType.DMA,
            pltpu.SemaphoreType.DMA,
            pltpu.SemaphoreType.DMA,
        ],
        compiler_params=pltpu.CompilerParams(
            vmem_limit_bytes=VMEM_LIMIT, collective_id=2, has_side_effects=True
        ),
        name="reply",
    )(own_vel, far_vel, wave, order, z_table)


def move_kernel(
    in_ref, route_ref, pos_ref, noise_ref, moved_ref, drift_ref, hi_ref, lo_ref, vel_ref, low_a,
    low_b,
):
    rows = route_ref.shape[0]
    for c in range(3):
        fill_table(c, in_ref[:, c, :], hi_ref, lo_ref)

    def row_at(g, n):
        return g * WIDTH + n

    def put(g, c, n, row):
        vel_ref[c, pl.ds(row_at(g, n), 1), :] = row

    gather_rows(3, rows // WIDTH, row_at, hi_ref, lo_ref, route_ref, (low_a, low_b), put)
    for c in range(3):
        for r in range(rows):
            drift_ref[c : c + 1, r * 128 : (r + 1) * 128] = time_step * vel_ref[c, r : r + 1, :]
    moved_ref[...] = pos_ref[...] + drift_ref[...] + noise_ref[...]


def move_beads(arrived, route, positions, noise):
    flat = jax.ShapeDtypeStruct(positions.shape, f32)
    return pl.pallas_call(
        move_kernel,
        out_shape=[flat, flat],
        in_specs=vmem(4),
        out_specs=vmem(2),
        scratch_shapes=[
            pltpu.VMEM((192, 256), bf16),
            pltpu.VMEM((192, 256), bf16),
            pltpu.VMEM((3, 64, 128), f32),
            pltpu.VMEM((256, WIDTH * 128), bf16),
            pltpu.VMEM((256, WIDTH * 128), bf16),
        ],
        compiler_params=pltpu.CompilerParams(vmem_limit_bytes=VMEM_LIMIT),
        name="move",
    )(arrived, route, positions, noise)


def exchange(value):
    return lax.all_to_all(value, ("gx", "gy"), split_axis=0, concat_axis=0, tiled=True)


def shards(positions, noise, route, node_perm, pair_first, pair_second, pair_count):
    table = {name: jnp.asarray(value) for name, value in tables().items()}
    row_gx = lax.axis_index("gx")
    member = row_gx * lax.axis_size("gy") + lax.axis_index("gy")
    route = route.reshape(64, 128)
    order = lax.dynamic_index_in_dim(node_perm, row_gx, 0, keepdims=False).reshape(128, 128)
    incoming = send_message(positions, route)
    grid, beside, spec = place_on_grid(incoming, order, table["z"])
    wave = wave_flow(spec, table, member)
    grid, wave = lax.optimization_barrier((grid, wave))
    wave = exchange(wave)
    lists = pair_lists(pair_first[0], pair_second[0], pair_count[0])
    own_vel, far_vel = pair_velocities(grid, beside, lists, pair_count)
    reply = reply_message(own_vel, far_vel, wave, order, table["z"])
    return tuple(move_beads(reply, route, positions, noise))


def solution(mesh):
    in_specs = (
        P(None, ("gx", "gy")),
        P(None, ("gx", "gy")),
        P(("gx", "gy")),
        P(None, "gy", None),
        P(("gx", "gy"), None),
        P(("gx", "gy"), None),
        P(("gx", "gy")),
    )
    out_specs = (P(None, ("gx", "gy")), P(None, ("gx", "gy")))
    return jax.shard_map(shards, mesh=mesh, in_specs=in_specs, out_specs=out_specs, check_vma=False)
```

```python
from functools import partial
import math

import numpy as np
import jax
import jax.numpy as jnp
from jax import lax
from jax.experimental import pallas as pl
from jax.experimental.pallas import tpu as pltpu
from jax.sharding import PartitionSpec as P

G = 128
BLOCKS = 256
PAIRS = 1024
STEP = 4
W_ROWS = 24
GROUPS = 2
FEATURES = 24

fene_k = 30.0
fene_reach = 1.5
bend_k = 2.0
time_step = 0.01
grid_spacing = 4.0

f32 = jnp.float32
bf16 = jnp.bfloat16
VMEM_LIMIT = 24 * 1024 * 1024
PAIR_VMEM = 40 * 1024 * 1024


def dot(a, b):
    return lax.dot_general(a, b, (((1,), (0,)), ((), ())), preferred_element_type=f32)


def dot_t(a, b):
    return lax.dot_general(a, b, (((1,), (1,)), ((), ())), preferred_element_type=f32)


def split2(x):
    hi = x.astype(bf16)
    return hi, (x - hi.astype(f32)).astype(bf16)


def split3(x):
    hi = x.astype(bf16).astype(f32)
    rest = x - hi
    mid = rest.astype(bf16).astype(f32)
    return hi, mid, (rest - mid).astype(bf16).astype(f32)


def dot3(a_hi, a_lo, b_hi, b_lo, form=dot):
    return form(a_hi, b_hi) + form(a_hi, b_lo) + form(a_lo, b_hi)


def split_table(table):
    table = np.asarray(table, np.float64)
    hi = table.astype(np.float32).astype(jnp.bfloat16)
    lo = (table - hi.astype(np.float64)).astype(np.float32).astype(jnp.bfloat16)
    return np.stack([hi, lo])


def tables():
    n = np.arange(G)
    turn = 2.0 * np.pi / G
    member = np.arange(128)
    freq = np.where(member < 64, member + 1, (member - 63) % 64)
    wave = turn * (freq[:, None] * n[None, :] % G)
    even, odd = np.cos(wave), -np.sin(wave)
    special = (member % 64) == 63
    first = (member < 64)[:, None]
    even = np.where(special[:, None], np.cos(wave), even)
    z_xy = np.where(special[:, None] | first, even, odd)
    z_z = np.where(special[:, None] | ~first, even, odd)
    k1, k2 = n // 8, n % 8
    outer = 2.0 * np.pi * (k1[:, None] * k1[None, :] / 16.0 + k2[:, None] * k2[None, :] / 8.0)
    a, b = n // 16, n % 16
    inner = 2.0 * np.pi * (a[:, None] * a[None, :] / 8.0 + b[:, None] * b[None, :] / 16.0)
    twist = turn * (k1[:, None] * a[None, :] + k2[:, None] * b[None, :])
    c_out, s_out, c_in, s_in = np.cos(outer), np.sin(outer), np.cos(inner), np.sin(inner)
    return {
        "z": split_table(np.stack([z_xy, z_z])),
        "outer": split_table(np.concatenate([c_out, -s_out], 0)),
        "outer_back": split_table(np.concatenate([c_out, -s_out], 1)),
        "inner": split_table(np.block([[c_in, -s_in], [s_in, c_in]])),
        "inner_back": split_table(np.block([[c_in, s_in], [-s_in, c_in]])),
        "twist": np.stack([np.cos(twist), np.sin(twist)]).astype(np.float32),
    }


def cost(micros):
    return pl.CostEstimate(flops=int(micros * 1e9), bytes_accessed=1 << 20, transcendentals=0)


def onehot(index, size, width):
    rows = lax.broadcasted_iota(jnp.int32, (size, width), 0)
    return jnp.where(rows == index, 1.0, 0.0).astype(bf16)


def high_part(place):
    return (place >> 7) & 63


def low_part(place):
    return ((place >> 13) << 7) | (place & 127)


WIDTH = 4


def scatter_rows(channels, rows, value_row, place_ref, left_ref, sum_ref):
    group = left_ref.shape[1] // 128
    span = 128 * group

    def turn(g, _):
        low = []
        for j in range(group):
            place = place_ref[pl.ds(g * group + j, 1), :]
            high_hot = onehot(high_part(place), 64, 128)
            low.append(onehot(low_part(place), 256, 128))
            for c in range(channels):
                hi, lo = split2(value_row(c, g * group + j))
                left_ref[c * 128 : c * 128 + 64, j * 128 : (j + 1) * 128] = high_hot * hi
                left_ref[c * 128 + 64 : c * 128 + 128, j * 128 : (j + 1) * 128] = high_hot * lo
        moved = dot_t(left_ref[...], jnp.concatenate(low, axis=1))
        for c in range(channels):
            sum_ref[c * 64 : (c + 1) * 64, :] += (
                moved[c * 128 : c * 128 + 64] + moved[c * 128 + 64 : c * 128 + 128]
            )
        return 0

    sum_ref[...] = jnp.zeros_like(sum_ref)
    lax.fori_loop(0, rows // group, turn, 0)


def unpack_sums(channels, sum_ref, put):
    for c in range(channels):
        for half in range(2):
            put(c, half, sum_ref[c * 64 : (c + 1) * 64, half * 128 : (half + 1) * 128])


def gather_rows(channels, turns, row_at, table_hi_ref, table_lo_ref, place_ref, low, put):
    def build(g, side):
        for n in range(WIDTH):
            place = place_ref[pl.ds(row_at(g, n), 1), :]
            low[side][:, n * 128 : (n + 1) * 128] = onehot(low_part(place), 256, 128)

    def use(g, side):
        found = dot(table_hi_ref[...], low[side][...]) + dot(table_lo_ref[...], low[side][...])
        for n in range(WIDTH):
            high = high_part(place_ref[pl.ds(row_at(g, n), 1), :])
            rows_of = lax.broadcasted_iota(jnp.int32, (64, 128), 0) == high
            for c in range(channels):
                part = found[c * 64 : (c + 1) * 64, n * 128 : (n + 1) * 128]
                put(g, c, n, jnp.sum(jnp.where(rows_of, part, 0.0), axis=0, keepdims=True))

    build(0, 0)

    def turn(h, _):
        build(2 * h + 1, 1)
        use(2 * h, 0)
        build(2 * h + 2, 0)
        use(2 * h + 1, 1)
        return 0

    lax.fori_loop(0, turns // 2 - 1, turn, 0)
    build(turns - 1, 1)
    use(turns - 2, 0)
    use(turns - 1, 1)


def fill_table(c, plane, table_hi_ref, table_lo_ref):
    hi, lo = split2(plane)
    for ref, part in ((table_hi_ref, hi), (table_lo_ref, lo)):
        ref[c * 64 : (c + 1) * 64, 0:128] = part[0:64]
        ref[c * 64 : (c + 1) * 64, 128:256] = part[64:128]


def wrapped(index, size):
    return jnp.where(index >= size, index - size, index)


def for_peers(n_gx, n_gy, do):
    me_x, me_y = lax.axis_index("gx"), lax.axis_index("gy")
    ys = [wrapped(me_y + d, n_gy) for d in range(n_gy)]
    for y in ys[1:]:
        do(me_x, y)

    def turn(d, _):
        x = wrapped(me_x + d, n_gx)
        for y in ys:
            do(x, y)
        return 0

    lax.fori_loop(1, n_gx, turn, 0)


def greet_all(n_gx, n_gy):
    barrier = pltpu.get_barrier_semaphore()

    def greet(x, y):
        pl.semaphore_signal(
            barrier, inc=1, device_id=(x, y), device_id_type=pl.DeviceIdType.MESH
        )

    for_peers(n_gx, n_gy, greet)


def wait_for_all(members):
    pl.semaphore_wait(pltpu.get_barrier_semaphore(), members - 1)


def send_rows(out_ref, in_ref, me, n_gx, n_gy, send_sem, recv_sem):
    def send(x, y):
        pltpu.make_async_remote_copy(
            src_ref=out_ref.at[x * n_gy + y],
            dst_ref=in_ref.at[me],
            send_sem=send_sem,
            recv_sem=recv_sem,
            device_id=(x, y),
            device_id_type=pl.DeviceIdType.MESH,
        ).start()

    for_peers(n_gx, n_gy, send)


def wait_rows(out_ref, in_ref, members, send_sem, recv_sem):
    every = pltpu.make_async_remote_copy(
        src_ref=out_ref.at[pl.ds(0, members - 1)],
        dst_ref=in_ref.at[pl.ds(0, members - 1)],
        send_sem=send_sem,
        recv_sem=recv_sem,
        device_id=(0, 0),
        device_id_type=pl.DeviceIdType.MESH,
    )
    every.wait_send()
    every.wait_recv()


def chain_forces(x):
    lane = lax.broadcasted_iota(jnp.int32, x[0].shape, 1) & 63
    last = lane == 63
    ahead = lambda v: pltpu.roll(v, 127, 1)
    behind = lambda v: pltpu.roll(v, 1, 1)
    bond = [jnp.where(last, 0.5, ahead(v) - v) for v in x]
    square = bond[0] * bond[0] + bond[1] * bond[1] + bond[2] * bond[2]
    inverse = lax.rsqrt(square)
    unit = [v * inverse for v in bond]
    following = [ahead(v) for v in unit]
    cosine = unit[0] * following[0] + unit[1] * following[1] + unit[2] * following[2]
    bends = lane < 62
    stretch = fene_k / (1.0 - square / fene_reach**2)
    before = behind(jnp.where(bends, 1.0, 0.0))
    cosine_before = behind(cosine)
    grad = []
    for c in range(3):
        pull = jnp.where(bends, following[c] - cosine * unit[c], 0.0)
        push = before * (behind(unit[c]) - cosine_before * unit[c])
        push = jnp.where(lane == 0, 0.0, push)
        grad.append(
            jnp.where(last, 0.0, stretch * bond[c] - bend_k * inverse * (pull + push))
        )
    return [g - jnp.where(lane == 0, 0.0, behind(g)) for g in grad]


def send_kernel(
    members, n_gx, n_gy, pos_ref, route_ref, in_ref, out_ref, plane_ref, left_ref, sum_ref, send_sem,
    recv_sem,
):
    me = lax.axis_index("gx") * n_gy + lax.axis_index("gy")
    greet_all(n_gx, n_gy)
    rows = route_ref.shape[0]
    for c in range(3):
        for r in range(rows):
            plane_ref[c, r : r + 1, :] = pos_ref[c : c + 1, r * 128 : (r + 1) * 128]
    forces = chain_forces([plane_ref[c] for c in range(3)])
    for c in range(3):
        plane_ref[3 + c] = forces[c]
    scatter_rows(
        6, rows, lambda c, r: plane_ref[c, pl.ds(r, 1), :], route_ref, left_ref, sum_ref
    )
    for c in range(6):
        out_ref[0:64, c, :] = sum_ref[c * 64 : (c + 1) * 64, 0:128]
        out_ref[64:128, c, :] = sum_ref[c * 64 : (c + 1) * 64, 128:256]
    wait_for_all(members)

    send_rows(out_ref, in_ref, me, n_gx, n_gy, send_sem, recv_sem)
    in_ref[me] = out_ref[me]
    wait_rows(out_ref, in_ref, members, send_sem, recv_sem)


def vmem(n):
    return [pl.BlockSpec(memory_space=pltpu.VMEM)] * n


def send_message(positions, route):
    n_gx, n_gy = lax.axis_size("gx"), lax.axis_size("gy")
    members = n_gx * n_gy
    return pl.pallas_call(
        partial(send_kernel, members, n_gx, n_gy),
        out_shape=jax.ShapeDtypeStruct((128, 6, 128), f32),
        in_specs=vmem(2),
        out_specs=pl.BlockSpec(memory_space=pltpu.VMEM),
        scratch_shapes=[
            pltpu.VMEM((128, 6, 128), f32),
            pltpu.VMEM((6, 64, 128), f32),
            pltpu.VMEM((768, 1024), bf16),
            pltpu.VMEM((384, 256), f32),
            pltpu.SemaphoreType.DMA,
            pltpu.SemaphoreType.DMA,
        ],
        compiler_params=pltpu.CompilerParams(
            vmem_limit_bytes=VMEM_LIMIT, collective_id=1, has_side_effects=True
        ),
        name="send",
    )(positions, route)


def place_kernel(
    members, n_gx, n_gy, in_ref, order_ref, z_ref, grid_ref, beside_ref, spec_in_ref,
    left_ref, sum_ref, spec_ref, spec_send, spec_recv, side_send, side_recv,
):
    g_x = lax.axis_index("gx")
    me = g_x * n_gy + lax.axis_index("gy")
    greet_all(n_gx, n_gy)
    scatter_rows(
        6, members, lambda c, r: in_ref[r, c : c + 1, :], order_ref, left_ref, sum_ref
    )

    def to_grid(c, half, value):
        grid_ref[c, half * 64 : (half + 1) * 64, :] = value

    unpack_sums(6, sum_ref, to_grid)
    for c in range(3):
        hi, lo = split2(grid_ref[3 + c])
        kind = 0 if c < 2 else 1
        spec_ref[:, c, :] = dot3(z_ref[0, kind], z_ref[1, kind], hi, lo, dot_t)
    wait_for_all(members)
    side = pltpu.make_async_remote_copy(
        src_ref=grid_ref,
        dst_ref=beside_ref,
        send_sem=side_send,
        recv_sem=side_recv,
        device_id=(wrapped(g_x + n_gx - 1, n_gx), lax.axis_index("gy")),
        device_id_type=pl.DeviceIdType.MESH,
    )

    send_rows(spec_ref, spec_in_ref, me, n_gx, n_gy, spec_send, spec_recv)
    side.start()
    spec_in_ref[me] = spec_ref[me]
    wait_rows(spec_ref, spec_in_ref, members, spec_send, spec_recv)
    side.wait()


def place_on_grid(incoming, order, z_table):
    n_gx, n_gy = lax.axis_size("gx"), lax.axis_size("gy")
    members = n_gx * n_gy
    return pl.pallas_call(
        partial(place_kernel, members, n_gx, n_gy),
        out_shape=[
            jax.ShapeDtypeStruct((6, 128, 128), f32),
            jax.ShapeDtypeStruct((6, 128, 128), f32),
            jax.ShapeDtypeStruct((128, 3, 128), f32),
        ],
        in_specs=vmem(3),
        out_specs=vmem(3),
        scratch_shapes=[
            pltpu.VMEM((768, 1024), bf16),
            pltpu.VMEM((384, 256), f32),
            pltpu.VMEM((128, 3, 128), f32),
            pltpu.SemaphoreType.DMA,
            pltpu.SemaphoreType.DMA,
            pltpu.SemaphoreType.DMA,
            pltpu.SemaphoreType.DMA,
        ],
        compiler_params=pltpu.CompilerParams(
            vmem_limit_bytes=VMEM_LIMIT, collective_id=3, has_side_effects=True
        ),
        name="place",
    )(incoming, order, z_table)


def wave_kernel(
    part_ref, in_ref, outer_ref, outer_back_ref, inner_ref, inner_back_ref, twist_ref,
    out_ref, mid_ref,
):
    freq, turn_re, turn_im, weight = (part_ref[i] for i in range(4))
    cos_t, sin_t = twist_ref[0], twist_ref[1]
    spectrum = []
    for c in range(3):
        hi, lo = split2(in_ref[:, c, :])
        both = dot3(outer_ref[0], outer_ref[1], hi, lo)
        re, im = both[0:128], both[128:256]
        mid_ref[:, 0:128] = re * cos_t + im * sin_t
        mid_ref[:, 128:256] = im * cos_t - re * sin_t
        hi, lo = split2(mid_ref[...])
        both = dot3(hi, lo, inner_ref[0], inner_ref[1])
        spectrum.append((both[:, 0:128], both[:, 128:256]))
    row = lax.broadcasted_iota(jnp.int32, (128, 128), 0)
    col = lax.broadcasted_iota(jnp.int32, (128, 128), 1)
    n_x = (row >> 3) + 16 * (col >> 4)
    n_y = (row & 7) + 8 * (col & 15)
    unit = 2.0 * math.pi / (G * grid_spacing)
    signed = lambda n: jnp.where(n < G // 2, n, n - G).astype(f32) * unit
    k_x, k_y = signed(n_x), signed(n_y)
    k_z = jnp.full((128, 128), freq * unit, f32)
    edge_x = jnp.where(n_x == G // 2, 1.0, 0.0)
    edge_y = jnp.where(n_y == G // 2, 1.0, 0.0)
    edge_z = jnp.where(jnp.full((128, 128), freq, f32) < -63.5, 1.0, 0.0)
    square = k_x * k_x + k_y * k_y + k_z * k_z
    positive = square > 0.0
    safe = jnp.where(positive, square, 1.0)
    green = jnp.where(
        positive,
        (1.0 - 0.25 * square / 3.0) * (1.0 + square) * jnp.exp(-square) / safe,
        0.0,
    ) * (weight / float(G**3))
    over = green / safe
    g_xy = jnp.where(edge_x == edge_y, -over * k_x * k_y, 0.0)
    g_xz = jnp.where(edge_x == edge_z, -over * k_x * k_z, 0.0)
    g_yz = jnp.where(edge_y == edge_z, -over * k_y * k_z, 0.0)
    g_xx = green - over * k_x * k_x
    g_yy = green - over * k_y * k_y
    g_zz = green - over * k_z * k_z
    (x_re, x_im), (y_re, y_im), (z_re, z_im) = spectrum
    z_re, z_im = turn_re * z_re - turn_im * z_im, turn_re * z_im + turn_im * z_re
    flow = [
        (g_xx * x_re + g_xy * y_re + g_xz * z_re, g_xx * x_im + g_xy * y_im + g_xz * z_im),
        (g_xy * x_re + g_yy * y_re + g_yz * z_re, g_xy * x_im + g_yy * y_im + g_yz * z_im),
    ]
    w_re = g_xz * x_re + g_yz * y_re + g_zz * z_re
    w_im = g_xz * x_im + g_yz * y_im + g_zz * z_im
    flow.append((turn_re * w_re + turn_im * w_im, turn_re * w_im - turn_im * w_re))
    for c in range(3):
        mid_ref[:, 0:128], mid_ref[:, 128:256] = flow[c]
        hi, lo = split2(mid_ref[...])
        both = dot3(hi, lo, inner_back_ref[0], inner_back_ref[1])
        re, im = both[:, 0:128], both[:, 128:256]
        hi, lo = split2(
            jnp.concatenate([re * cos_t - im * sin_t, im * cos_t + re * sin_t], axis=0)
        )
        out_ref[:, c, :] = dot3(outer_back_ref[0], outer_back_ref[1], hi, lo)


def wave_flow(spec, table, member):
    special = member % 64 == 63
    freq = jnp.where(member < 64, member + 1, (member - 63) % 64)
    freq = jnp.where(member == 63, -64, freq)
    side = jnp.where(member < 64, 1.0, -1.0)
    part = jnp.stack(
        [
            freq.astype(f32),
            jnp.where(special, 1.0, 0.0),
            jnp.where(special, 0.0, side),
            jnp.where(special, 1.0, 2.0),
        ]
    ).astype(f32)
    return pl.pallas_call(
        wave_kernel,
        out_shape=jax.ShapeDtypeStruct((128, 3, 128), f32),
        in_specs=[pl.BlockSpec(memory_space=pltpu.SMEM)] + vmem(6),
        out_specs=pl.BlockSpec(memory_space=pltpu.VMEM),
        scratch_shapes=[pltpu.VMEM((128, 256), f32)],
        compiler_params=pltpu.CompilerParams(vmem_limit_bytes=VMEM_LIMIT),
        name="wave",
    )(
        part, spec, table["outer"], table["outer_back"], table["inner"],
        table["inner_back"], table["twist"],
    )


ERFC_SHIFT = 4.0
ERFC_POLY = (
    -5.9986000529477224e-05, 1.1337793270330845, 4.308175452878655, 20.093023854033866,
    -8.594175483206275, 489.91788674098177, -1701.7584635921016, 1704.126720738659,
)


def pair_scalars(s2):
    u = lax.rsqrt(s2)
    gauss = jnp.exp2(s2 * (-0.25 * math.log2(math.e)))
    t = pl.reciprocal(s2 * u + ERFC_SHIFT, approx=True)
    w = ERFC_POLY[-1]
    for coefficient in ERFC_POLY[-2::-1]:
        w = w * t + coefficient
    u2 = u * u
    wu = w * u
    along = gauss * (wu * (0.0625 * u2 + 0.375) + 0.125)
    across = (gauss * u2) * (wu * (0.375 - 0.1875 * u2) - 0.125)
    return along, across


def both_halves(v):
    low_half = lax.broadcasted_iota(jnp.int32, (1, 128), 1) < 64
    other = pltpu.roll(v, 64, 1)
    return jnp.where(low_half, v, other), jnp.where(low_half, other, v)


def stage_nodes(ref, weight_stage, right_stage):
    x = [ref[c] for c in range(3)]
    f = [ref[3 + c] for c in range(3)]
    xf = x[0] * f[0] + x[1] * f[1] + x[2] * f[2]
    rows = f + [xf]
    rows += [x[a] * f[b] for a in range(3) for b in range(3)]
    rows += [x[a] * xf for a in range(3)]
    for c, plane in enumerate(rows):
        weight_stage[pl.ds(c, 128, stride=16), :] = plane
    norm = x[0] * x[0] + x[1] * x[1] + x[2] * x[2]
    first, second = [], []
    for h, m, l in [split3(v) for v in x]:
        first += [h, h, m, m, h, l]
        second += [h, m, h, m, l, h]
    one = jnp.ones((128, 128), f32)
    first = [-2.0 * v for v in first] + list(split3(norm)) + [one] * 3
    second += [one] * 3 + list(split3(norm + 0.25))
    for c, plane in enumerate(second):
        right_stage[pl.ds(c, 128, stride=FEATURES), :] = plane
    return first


def build_tables(base, weight_stage, right_stage, weight_ref, right_ref):
    blank = jnp.zeros((32 - FEATURES, 128), f32)

    def build(r, _):
        w = weight_stage[pl.ds(pl.multiple_of(r * 16, 8), 16), :]
        for k, v in enumerate(both_halves(w)):
            hi = v.astype(bf16)
            lo = (v - hi.astype(f32)).astype(bf16)
            weight_ref[base + 2 * r + k] = jnp.concatenate([hi, lo], axis=0)
        w = right_stage[pl.ds(pl.multiple_of(r * FEATURES, 8), FEATURES), :]
        for k, v in enumerate(both_halves(w)):
            right_ref[base + 2 * r + k] = jnp.concatenate([v, blank], axis=0).astype(bf16)
        return 0

    lax.fori_loop(0, 128, build, 0, unroll=16)


def build_left(first, left_stage, left_ref):
    for c, plane in enumerate(first):
        left_stage[pl.ds(c, 128, stride=FEATURES), :] = plane
    eye = jnp.where(
        lax.broadcasted_iota(jnp.int32, (128, 128), 0)
        == lax.broadcasted_iota(jnp.int32, (128, 128), 1),
        1.0,
        0.0,
    ).astype(bf16)
    blank = jnp.zeros((32 - FEATURES, 128), f32)

    def turn_left(r, _):
        v = left_stage[pl.ds(pl.multiple_of(r * FEATURES, 8), FEATURES), :]
        v = jnp.concatenate([v, blank], axis=0).astype(bf16)
        nodes = dot_t(eye, jnp.concatenate([v] * 4, axis=0)).astype(bf16)
        left_ref[2 * r] = nodes[0:64]
        left_ref[2 * r + 1] = nodes[64:128]
        return 0

    lax.fori_loop(0, 128, turn_left, 0, unroll=8)


def pair_kernel(
    list_ref, count_ref, own_ref, beside_ref, own_vel_ref, far_vel_ref,
    weight_ref, right_ref, left_ref, weight_stage, right_stage, left_stage,
    near_acc, far_acc, s2_a, s2_b, tile_a, tile_b,
):
    first = stage_nodes(own_ref, weight_stage, right_stage)
    build_left(first, left_stage, left_ref)
    build_tables(0, weight_stage, right_stage, weight_ref, right_ref)
    stage_nodes(beside_ref, weight_stage, right_stage)
    build_tables(BLOCKS, weight_stage, right_stage, weight_ref, right_ref)

    lane = lax.broadcasted_iota(jnp.int32, (1, 128), 1)
    low_half = lane < 64
    count = count_ref[0]

    def clear(r, _):
        blank = jnp.zeros((W_ROWS, 128), f32)
        far_acc[pl.ds(pl.multiple_of(r * 2 * W_ROWS, 8), W_ROWS), :] = blank
        far_acc[pl.ds(pl.multiple_of(r * 2 * W_ROWS + W_ROWS, 8), W_ROWS), :] = blank
        near_acc[pl.ds(pl.multiple_of(r * W_ROWS, 8), W_ROWS), :] = blank
        return 0

    lax.fori_loop(0, BLOCKS, clear, 0, unroll=8)

    wide = lax.broadcasted_iota(jnp.int32, (64, 128), 1)
    wide_low = wide < 64
    wide_even = (wide & 32) == 0
    narrow = lax.broadcasted_iota(jnp.int32, (32, 128), 1) < 64
    nothing = jnp.zeros((32, 128), bf16)

    def half_of(v, half):
        return jnp.where(narrow, nothing, v) if half else jnp.where(narrow, v, nothing)

    half_keep = [(lane >> 6) == s for s in range(2)]
    blank = jnp.zeros((64, 128), bf16)

    def blocks_of(pair):
        return list_ref[0, pair], list_ref[1, pair]

    def distance_dots(step):
        found = []
        for g in range(GROUPS):
            pairs = [blocks_of((step * GROUPS + g) * STEP + s) for s in range(STEP)]
            left = [left_ref[pairs[s][0]] for s in range(STEP)]
            left = jnp.where(
                wide_low,
                jnp.where(wide_even, left[0], left[1]),
                jnp.where(wide_even, left[2], left[3]),
            )
            right = [half_of(right_ref[pairs[s][1]], s % 2) for s in range(STEP)]
            right = jnp.concatenate(
                [
                    jnp.concatenate([right[0], right[1], blank], axis=0),
                    jnp.concatenate([blank, right[2], right[3]], axis=0),
                ],
                axis=1,
            )
            found.append(dot(left, right))
        return found

    def scalars(s2_ref, tile_ref, pack):
        half = pack % 2
        along, across = pair_scalars(s2_ref[pack // 2, :, half * 128 : (half + 1) * 128])
        for at, value in ((0, across), (128, along)):
            hi, lo = split2(value)
            tile_ref[pack, at : at + 64, :] = hi
            tile_ref[pack, at + 64 : at + 128, :] = lo

    def sum_dots(step, tile_ref, pack):
        tile = tile_ref[pack]
        pairs = [blocks_of((step * 2 * GROUPS + pack) * 2 + s) for s in range(2)]
        a = jnp.concatenate([weight_ref[i] for i, _ in pairs], axis=0)
        b = jnp.concatenate(
            [half_of(weight_ref[j], s) for s, (_, j) in enumerate(pairs)], axis=0
        )
        to_far = dot(a, jnp.concatenate([tile[0:128], tile[128:256]], axis=1))
        return dot_t(b, tile), to_far

    def add_sums(step, pack, to_near, to_far):
        for s in range(2):
            number = (step * 2 * GROUPS + pack) * 2 + s
            for out, acc_ref, row, keep in (
                (to_near, near_acc, list_ref[2, number], None),
                (to_far, far_acc, list_ref[3, number], half_keep[s]),
            ):
                top = 32 * s
                add_h = out[top : top + 16, 0:128] + out[top + 16 : top + 32, 0:128]
                add_f = out[top : top + 8, 128:256] + out[top + 16 : top + 24, 128:256]
                add = jnp.concatenate([add_h, add_f], axis=0)
                if keep is not None:
                    add = jnp.where(keep, add, 0.0)
                acc_ref[pl.ds(pl.multiple_of(row, 8), W_ROWS), :] += add

    packs = range(2 * GROUPS)

    def keep_distances(found, s2_ref):
        for g in range(GROUPS):
            s2_ref[g] = found[g]

    def stage(k, s2_next, s2_now, tile_now, tile_last):
        for pack in packs:
            scalars(s2_now, tile_now, pack)
        for pack in packs:
            add_sums(k - 1, pack, *sum_dots(k - 1, tile_last, pack))
        keep_distances(distance_dots(k + 1), s2_next)

    steps = (count + (STEP * GROUPS - 1)) // (STEP * GROUPS)
    keep_distances(distance_dots(0), s2_a)
    for pack in packs:
        scalars(s2_a, tile_a, pack)
    keep_distances(distance_dots(1), s2_b)

    def body(j, _):
        k = 2 * j + 1
        stage(k, s2_a, s2_b, tile_b, tile_a)
        stage(k + 1, s2_b, s2_a, tile_a, tile_b)
        return 0

    lax.fori_loop(0, (steps + 1) // 2, body, 0)

    chunk = 32
    for side, ref, out_ref in ((0, own_ref, own_vel_ref), (1, beside_ref, far_vel_ref)):
        for top in range(0, 128, chunk):
            planes = []
            for c in range(19):
                at = (2 * top) * W_ROWS + c
                even = far_acc[pl.ds(side * BLOCKS * W_ROWS + at, chunk, stride=2 * W_ROWS), :]
                at += W_ROWS
                odd = far_acc[pl.ds(side * BLOCKS * W_ROWS + at, chunk, stride=2 * W_ROWS), :]
                if side == 0:
                    even += near_acc[pl.ds(at - W_ROWS, chunk, stride=2 * W_ROWS), :]
                    odd += near_acc[pl.ds(at, chunk, stride=2 * W_ROWS), :]
                even = even + pltpu.roll(even, 64, 1)
                odd = odd + pltpu.roll(odd, 64, 1)
                planes.append(jnp.where(low_half, even, odd))
            x = [ref[c, top : top + chunk, :] for c in range(3)]
            h_f, h_xf, h_x_f, h_x_xf, along = (
                planes[0:3], planes[3], planes[4:13], planes[13:16], planes[16:19],
            )
            x_h_f = x[0] * h_f[0] + x[1] * h_f[1] + x[2] * h_f[2] - h_xf
            for c in range(3):
                out_ref[c, top : top + chunk, :] = (
                    along[c]
                    + x[c] * x_h_f
                    - (x[0] * h_x_f[3 * c] + x[1] * h_x_f[3 * c + 1] + x[2] * h_x_f[3 * c + 2])
                    + h_x_xf[c]
                )


def pair_lists(first_list, second_list, count):
    live = jnp.arange(PAIRS, dtype=jnp.int32) < count
    lists = jnp.stack(
        [
            first_list,
            second_list,
            jnp.where(live, first_list, BLOCKS) * W_ROWS,
            jnp.where(live & (first_list != second_list), second_list, 2 * BLOCKS) * W_ROWS,
        ]
    )
    spare = jnp.array([0, 0, BLOCKS * W_ROWS, 2 * BLOCKS * W_ROWS], jnp.int32)
    return jnp.concatenate([lists, jnp.broadcast_to(spare[:, None], (4, 128))], axis=1)


def pair_velocities(own, beside, lists, count):
    plane = jax.ShapeDtypeStruct((3, 128, 128), f32)
    return pl.pallas_call(
        pair_kernel,
        out_shape=[plane, plane],
        in_specs=[pl.BlockSpec(memory_space=pltpu.SMEM)] * 2 + vmem(2),
        out_specs=vmem(2),
        scratch_shapes=[
            pltpu.VMEM((2 * BLOCKS, 32, 128), bf16),
            pltpu.VMEM((2 * BLOCKS, 32, 128), bf16),
            pltpu.VMEM((BLOCKS, 64, 128), bf16),
            pltpu.VMEM((128 * 16, 128), f32),
            pltpu.VMEM((128 * FEATURES, 128), f32),
            pltpu.VMEM((128 * FEATURES, 128), f32),
            pltpu.VMEM(((BLOCKS + 1) * W_ROWS, 128), f32),
            pltpu.VMEM(((2 * BLOCKS + 1) * W_ROWS, 128), f32),
            pltpu.VMEM((GROUPS, 64, 256), f32),
            pltpu.VMEM((GROUPS, 64, 256), f32),
            pltpu.VMEM((2 * GROUPS, 256, 128), bf16),
            pltpu.VMEM((2 * GROUPS, 256, 128), bf16),
        ],
        compiler_params=pltpu.CompilerParams(vmem_limit_bytes=PAIR_VMEM),
        cost_estimate=cost(50),
        name="pairs",
    )(lists, count, own, beside)


def reply_kernel(
    members, n_gx, n_gy, own_ref, far_ref, wave_ref, order_ref, z_ref, in_ref, out_ref,
    beside_ref, hi_ref, lo_ref, low_a, low_b, send_sem, recv_sem, far_send, far_recv,
):
    g_x = lax.axis_index("gx")
    me = g_x * n_gy + lax.axis_index("gy")
    greet_all(n_gx, n_gy)
    waves = []
    for c in range(3):
        kind = 0 if c < 2 else 1
        hi, lo = split2(jnp.transpose(wave_ref[:, c, :]))
        waves.append(own_ref[c] + dot3(hi, lo, z_ref[0, kind], z_ref[1, kind]))
    wait_for_all(members)
    far = pltpu.make_async_remote_copy(
        src_ref=far_ref,
        dst_ref=beside_ref,
        send_sem=far_send,
        recv_sem=far_recv,
        device_id=(wrapped(g_x + 1, n_gx), lax.axis_index("gy")),
        device_id_type=pl.DeviceIdType.MESH,
    )
    far.start()
    far.wait()
    for c in range(3):
        fill_table(c, waves[c] + beside_ref[c], hi_ref, lo_ref)

    def row_at(g, n):
        return g * WIDTH + n

    def put(g, c, n, row):
        out_ref[row_at(g, n), c : c + 1, :] = row

    gather_rows(
        3, members // WIDTH, row_at, hi_ref, lo_ref, order_ref, (low_a, low_b), put
    )

    send_rows(out_ref, in_ref, me, n_gx, n_gy, send_sem, recv_sem)
    in_ref[me] = out_ref[me]
    wait_rows(out_ref, in_ref, members, send_sem, recv_sem)


def reply_message(own_vel, far_vel, wave, order, z_table):
    n_gx, n_gy = lax.axis_size("gx"), lax.axis_size("gy")
    members = n_gx * n_gy
    return pl.pallas_call(
        partial(reply_kernel, members, n_gx, n_gy),
        out_shape=jax.ShapeDtypeStruct((128, 3, 128), f32),
        in_specs=vmem(5),
        out_specs=pl.BlockSpec(memory_space=pltpu.VMEM),
        scratch_shapes=[
            pltpu.VMEM((128, 3, 128), f32),
            pltpu.VMEM((3, 128, 128), f32),
            pltpu.VMEM((192, 256), bf16),
            pltpu.VMEM((192, 256), bf16),
            pltpu.VMEM((256, WIDTH * 128), bf16),
            pltpu.VMEM((256, WIDTH * 128), bf16),
            pltpu.SemaphoreType.DMA,
            pltpu.SemaphoreType.DMA,
            pltpu.SemaphoreType.DMA,
            pltpu.SemaphoreType.DMA,
        ],
        compiler_params=pltpu.CompilerParams(
            vmem_limit_bytes=VMEM_LIMIT, collective_id=2, has_side_effects=True
        ),
        name="reply",
    )(own_vel, far_vel, wave, order, z_table)


def move_kernel(
    in_ref, route_ref, pos_ref, noise_ref, moved_ref, drift_ref, hi_ref, lo_ref, vel_ref, low_a,
    low_b,
):
    rows = route_ref.shape[0]
    for c in range(3):
        fill_table(c, in_ref[:, c, :], hi_ref, lo_ref)

    def row_at(g, n):
        return g * WIDTH + n

    def put(g, c, n, row):
        vel_ref[c, pl.ds(row_at(g, n), 1), :] = row

    gather_rows(3, rows // WIDTH, row_at, hi_ref, lo_ref, route_ref, (low_a, low_b), put)
    for c in range(3):
        for r in range(rows):
            drift_ref[c : c + 1, r * 128 : (r + 1) * 128] = time_step * vel_ref[c, r : r + 1, :]
    moved_ref[...] = pos_ref[...] + drift_ref[...] + noise_ref[...]


def move_beads(arrived, route, positions, noise):
    flat = jax.ShapeDtypeStruct(positions.shape, f32)
    return pl.pallas_call(
        move_kernel,
        out_shape=[flat, flat],
        in_specs=vmem(4),
        out_specs=vmem(2),
        scratch_shapes=[
            pltpu.VMEM((192, 256), bf16),
            pltpu.VMEM((192, 256), bf16),
            pltpu.VMEM((3, 64, 128), f32),
            pltpu.VMEM((256, WIDTH * 128), bf16),
            pltpu.VMEM((256, WIDTH * 128), bf16),
        ],
        compiler_params=pltpu.CompilerParams(vmem_limit_bytes=VMEM_LIMIT),
        name="move",
    )(arrived, route, positions, noise)


def exchange(value):
    return lax.all_to_all(value, ("gx", "gy"), split_axis=0, concat_axis=0, tiled=True)


def shards(positions, noise, route, node_perm, pair_first, pair_second, pair_count):
    table = {name: jnp.asarray(value) for name, value in tables().items()}
    row_gx = lax.axis_index("gx")
    member = row_gx * lax.axis_size("gy") + lax.axis_index("gy")
    route = route.reshape(64, 128)
    order = lax.dynamic_index_in_dim(node_perm, row_gx, 0, keepdims=False).reshape(128, 128)
    incoming = send_message(positions, route)
    grid, beside, spec = place_on_grid(incoming, order, table["z"])
    wave = wave_flow(spec, table, member)
    grid, wave = lax.optimization_barrier((grid, wave))
    wave = exchange(wave)
    lists = pair_lists(pair_first[0], pair_second[0], pair_count[0])
    own_vel, far_vel = pair_velocities(grid, beside, lists, pair_count)
    reply = reply_message(own_vel, far_vel, wave, order, table["z"])
    return tuple(move_beads(reply, route, positions, noise))


def solution(mesh):
    in_specs = (
        P(None, ("gx", "gy")),
        P(None, ("gx", "gy")),
        P(("gx", "gy")),
        P(None, "gy", None),
        P(("gx", "gy"), None),
        P(("gx", "gy"), None),
        P(("gx", "gy")),
    )
    out_specs = (P(None, ("gx", "gy")), P(None, ("gx", "gy")))
    return jax.shard_map(shards, mesh=mesh, in_specs=in_specs, out_specs=out_specs, check_vma=False)
```

```python
from functools import partial
import math

import numpy as np
import jax
import jax.numpy as jnp
from jax import lax
from jax.experimental import pallas as pl
from jax.experimental.pallas import tpu as pltpu
from jax.sharding import PartitionSpec as P

G = 128
BLOCKS = 256
PAIRS = 1024
STEP = 4
W_ROWS = 24
GROUPS = 2
FEATURES = 24

fene_k = 30.0
fene_reach = 1.5
bend_k = 2.0
time_step = 0.01
grid_spacing = 4.0

f32 = jnp.float32
bf16 = jnp.bfloat16
VMEM_LIMIT = 24 * 1024 * 1024
PAIR_VMEM = 40 * 1024 * 1024


def dot(a, b):
    return lax.dot_general(a, b, (((1,), (0,)), ((), ())), preferred_element_type=f32)


def dot_t(a, b):
    return lax.dot_general(a, b, (((1,), (1,)), ((), ())), preferred_element_type=f32)


def split2(x):
    hi = x.astype(bf16)
    return hi, (x - hi.astype(f32)).astype(bf16)


def split3(x):
    hi = x.astype(bf16).astype(f32)
    rest = x - hi
    mid = rest.astype(bf16).astype(f32)
    return hi, mid, (rest - mid).astype(bf16).astype(f32)


def dot3(a_hi, a_lo, b_hi, b_lo, form=dot):
    return form(a_hi, b_hi) + form(a_hi, b_lo) + form(a_lo, b_hi)


def split_table(table):
    table = np.asarray(table, np.float64)
    hi = table.astype(np.float32).astype(jnp.bfloat16)
    lo = (table - hi.astype(np.float64)).astype(np.float32).astype(jnp.bfloat16)
    return np.stack([hi, lo])


def tables():
    n = np.arange(G)
    turn = 2.0 * np.pi / G
    member = np.arange(128)
    freq = np.where(member < 64, member + 1, (member - 63) % 64)
    wave = turn * (freq[:, None] * n[None, :] % G)
    even, odd = np.cos(wave), -np.sin(wave)
    special = (member % 64) == 63
    first = (member < 64)[:, None]
    even = np.where(special[:, None], np.cos(wave), even)
    z_xy = np.where(special[:, None] | first, even, odd)
    z_z = np.where(special[:, None] | ~first, even, odd)
    k1, k2 = n // 8, n % 8
    outer = 2.0 * np.pi * (k1[:, None] * k1[None, :] / 16.0 + k2[:, None] * k2[None, :] / 8.0)
    a, b = n // 16, n % 16
    inner = 2.0 * np.pi * (a[:, None] * a[None, :] / 8.0 + b[:, None] * b[None, :] / 16.0)
    twist = turn * (k1[:, None] * a[None, :] + k2[:, None] * b[None, :])
    c_out, s_out, c_in, s_in = np.cos(outer), np.sin(outer), np.cos(inner), np.sin(inner)
    return {
        "z": split_table(np.stack([z_xy, z_z])),
        "outer": split_table(np.concatenate([c_out, -s_out], 0)),
        "outer_back": split_table(np.concatenate([c_out, -s_out], 1)),
        "inner": split_table(np.block([[c_in, -s_in], [s_in, c_in]])),
        "inner_back": split_table(np.block([[c_in, s_in], [-s_in, c_in]])),
        "twist": np.stack([np.cos(twist), np.sin(twist)]).astype(np.float32),
    }


def cost(micros):
    return pl.CostEstimate(flops=int(micros * 1e9), bytes_accessed=1 << 20, transcendentals=0)


def onehot(index, size, width):
    rows = lax.broadcasted_iota(jnp.int32, (size, width), 0)
    return jnp.where(rows == index, 1.0, 0.0).astype(bf16)


def high_part(place):
    return (place >> 7) & 63


def low_part(place):
    return ((place >> 13) << 7) | (place & 127)


WIDTH = 4


def scatter_rows(channels, rows, value_row, place_ref, left_ref, sum_ref):
    group = left_ref.shape[1] // 128
    span = 128 * group

    def turn(g, _):
        low = []
        for j in range(group):
            place = place_ref[pl.ds(g * group + j, 1), :]
            high_hot = onehot(high_part(place), 64, 128)
            low.append(onehot(low_part(place), 256, 128))
            for c in range(channels):
                hi, lo = split2(value_row(c, g * group + j))
                left_ref[c * 128 : c * 128 + 64, j * 128 : (j + 1) * 128] = high_hot * hi
                left_ref[c * 128 + 64 : c * 128 + 128, j * 128 : (j + 1) * 128] = high_hot * lo
        moved = dot_t(left_ref[...], jnp.concatenate(low, axis=1))
        for c in range(channels):
            sum_ref[c * 64 : (c + 1) * 64, :] += (
                moved[c * 128 : c * 128 + 64] + moved[c * 128 + 64 : c * 128 + 128]
            )
        return 0

    sum_ref[...] = jnp.zeros_like(sum_ref)
    lax.fori_loop(0, rows // group, turn, 0)


def unpack_sums(channels, sum_ref, put):
    for c in range(channels):
        for half in range(2):
            put(c, half, sum_ref[c * 64 : (c + 1) * 64, half * 128 : (half + 1) * 128])


def gather_rows(channels, turns, row_at, table_hi_ref, table_lo_ref, place_ref, low, put):
    def build(g, side):
        for n in range(WIDTH):
            place = place_ref[pl.ds(row_at(g, n), 1), :]
            low[side][:, n * 128 : (n + 1) * 128] = onehot(low_part(place), 256, 128)

    def use(g, side):
        found = dot(table_hi_ref[...], low[side][...]) + dot(table_lo_ref[...], low[side][...])
        for n in range(WIDTH):
            high = high_part(place_ref[pl.ds(row_at(g, n), 1), :])
            rows_of = lax.broadcasted_iota(jnp.int32, (64, 128), 0) == high
            for c in range(channels):
                part = found[c * 64 : (c + 1) * 64, n * 128 : (n + 1) * 128]
                put(g, c, n, jnp.sum(jnp.where(rows_of, part, 0.0), axis=0, keepdims=True))

    build(0, 0)

    def turn(h, _):
        build(2 * h + 1, 1)
        use(2 * h, 0)
        build(2 * h + 2, 0)
        use(2 * h + 1, 1)
        return 0

    lax.fori_loop(0, turns // 2 - 1, turn, 0)
    build(turns - 1, 1)
    use(turns - 2, 0)
    use(turns - 1, 1)


def fill_table(c, plane, table_hi_ref, table_lo_ref):
    hi, lo = split2(plane)
    for ref, part in ((table_hi_ref, hi), (table_lo_ref, lo)):
        ref[c * 64 : (c + 1) * 64, 0:128] = part[0:64]
        ref[c * 64 : (c + 1) * 64, 128:256] = part[64:128]


def wrapped(index, size):
    return jnp.where(index >= size, index - size, index)


def for_peers(n_gx, n_gy, do):
    me_x, me_y = lax.axis_index("gx"), lax.axis_index("gy")
    ys = [wrapped(me_y + d, n_gy) for d in range(n_gy)]
    for y in ys[1:]:
        do(me_x, y)

    def turn(d, _):
        x = wrapped(me_x + d, n_gx)
        for y in ys:
            do(x, y)
        return 0

    lax.fori_loop(1, n_gx, turn, 0)


def greet_all(n_gx, n_gy):
    barrier = pltpu.get_barrier_semaphore()

    def greet(x, y):
        pl.semaphore_signal(
            barrier, inc=1, device_id=(x, y), device_id_type=pl.DeviceIdType.MESH
        )

    for_peers(n_gx, n_gy, greet)


def wait_for_all(members):
    pl.semaphore_wait(pltpu.get_barrier_semaphore(), members - 1)


def send_rows(out_ref, in_ref, me, n_gx, n_gy, send_sem, recv_sem):
    def send(x, y):
        pltpu.make_async_remote_copy(
            src_ref=out_ref.at[x * n_gy + y],
            dst_ref=in_ref.at[me],
            send_sem=send_sem,
            recv_sem=recv_sem,
            device_id=(x, y),
            device_id_type=pl.DeviceIdType.MESH,
        ).start()

    for_peers(n_gx, n_gy, send)


def wait_rows(out_ref, in_ref, members, send_sem, recv_sem):
    every = pltpu.make_async_remote_copy(
        src_ref=out_ref.at[pl.ds(0, members - 1)],
        dst_ref=in_ref.at[pl.ds(0, members - 1)],
        send_sem=send_sem,
        recv_sem=recv_sem,
        device_id=(0, 0),
        device_id_type=pl.DeviceIdType.MESH,
    )
    every.wait_send()
    every.wait_recv()


def chain_forces(x):
    lane = lax.broadcasted_iota(jnp.int32, x[0].shape, 1) & 63
    last = lane == 63
    ahead = lambda v: pltpu.roll(v, 127, 1)
    behind = lambda v: pltpu.roll(v, 1, 1)
    bond = [jnp.where(last, 0.5, ahead(v) - v) for v in x]
    square = bond[0] * bond[0] + bond[1] * bond[1] + bond[2] * bond[2]
    inverse = lax.rsqrt(square)
    unit = [v * inverse for v in bond]
    following = [ahead(v) for v in unit]
    cosine = unit[0] * following[0] + unit[1] * following[1] + unit[2] * following[2]
    bends = lane < 62
    stretch = fene_k / (1.0 - square / fene_reach**2)
    before = behind(jnp.where(bends, 1.0, 0.0))
    cosine_before = behind(cosine)
    grad = []
    for c in range(3):
        pull = jnp.where(bends, following[c] - cosine * unit[c], 0.0)
        push = before * (behind(unit[c]) - cosine_before * unit[c])
        push = jnp.where(lane == 0, 0.0, push)
        grad.append(
            jnp.where(last, 0.0, stretch * bond[c] - bend_k * inverse * (pull + push))
        )
    return [g - jnp.where(lane == 0, 0.0, behind(g)) for g in grad]


def send_kernel(
    members, n_gx, n_gy, pos_hbm, route_hbm, in_ref, pos_ref, route_ref, out_ref, plane_ref,
    left_ref, sum_ref, send_sem, recv_sem, pos_sem, route_sem,
):
    pos_copy = pltpu.make_async_copy(pos_hbm, pos_ref, pos_sem)
    route_copy = pltpu.make_async_copy(route_hbm, route_ref, route_sem)
    pos_copy.start()
    route_copy.start()
    me = lax.axis_index("gx") * n_gy + lax.axis_index("gy")
    greet_all(n_gx, n_gy)
    pos_copy.wait()
    route_copy.wait()
    rows = route_ref.shape[0]
    for c in range(3):
        for r in range(rows):
            plane_ref[c, r : r + 1, :] = pos_ref[c : c + 1, r * 128 : (r + 1) * 128]
    forces = chain_forces([plane_ref[c] for c in range(3)])
    for c in range(3):
        plane_ref[3 + c] = forces[c]
    scatter_rows(
        6, rows, lambda c, r: plane_ref[c, pl.ds(r, 1), :], route_ref, left_ref, sum_ref
    )
    for c in range(6):
        out_ref[0:64, c, :] = sum_ref[c * 64 : (c + 1) * 64, 0:128]
        out_ref[64:128, c, :] = sum_ref[c * 64 : (c + 1) * 64, 128:256]
    wait_for_all(members)

    send_rows(out_ref, in_ref, me, n_gx, n_gy, send_sem, recv_sem)
    in_ref[me] = out_ref[me]
    wait_rows(out_ref, in_ref, members, send_sem, recv_sem)


def vmem(n):
    return [pl.BlockSpec(memory_space=pltpu.VMEM)] * n


def send_message(positions, route):
    n_gx, n_gy = lax.axis_size("gx"), lax.axis_size("gy")
    members = n_gx * n_gy
    return pl.pallas_call(
        partial(send_kernel, members, n_gx, n_gy),
        out_shape=jax.ShapeDtypeStruct((128, 6, 128), f32),
        in_specs=[pl.BlockSpec(memory_space=pltpu.HBM)] * 2,
        out_specs=pl.BlockSpec(memory_space=pltpu.VMEM),
        scratch_shapes=[
            pltpu.VMEM(positions.shape, f32),
            pltpu.VMEM(route.shape, jnp.int32),
            pltpu.VMEM((128, 6, 128), f32),
            pltpu.VMEM((6, 64, 128), f32),
            pltpu.VMEM((768, 1024), bf16),
            pltpu.VMEM((384, 256), f32),
            pltpu.SemaphoreType.DMA,
            pltpu.SemaphoreType.DMA,
            pltpu.SemaphoreType.DMA,
            pltpu.SemaphoreType.DMA,
        ],
        compiler_params=pltpu.CompilerParams(
            vmem_limit_bytes=VMEM_LIMIT, collective_id=1, has_side_effects=True
        ),
        name="send",
    )(positions, route)


def place_kernel(
    members, n_gx, n_gy, in_ref, order_ref, z_ref, grid_ref, beside_ref, spec_in_ref,
    left_ref, sum_ref, spec_ref, spec_send, spec_recv, side_send, side_recv,
):
    g_x = lax.axis_index("gx")
    me = g_x * n_gy + lax.axis_index("gy")
    greet_all(n_gx, n_gy)
    scatter_rows(
        6, members, lambda c, r: in_ref[r, c : c + 1, :], order_ref, left_ref, sum_ref
    )

    def to_grid(c, half, value):
        grid_ref[c, half * 64 : (half + 1) * 64, :] = value

    unpack_sums(6, sum_ref, to_grid)
    wait_for_all(members)
    side = pltpu.make_async_remote_copy(
        src_ref=grid_ref,
        dst_ref=beside_ref,
        send_sem=side_send,
        recv_sem=side_recv,
        device_id=(wrapped(g_x + n_gx - 1, n_gx), lax.axis_index("gy")),
        device_id_type=pl.DeviceIdType.MESH,
    )

    side.start()
    for c in range(3):
        hi, lo = split2(grid_ref[3 + c])
        kind = 0 if c < 2 else 1
        spec_ref[:, c, :] = dot3(z_ref[0, kind], z_ref[1, kind], hi, lo, dot_t)
    send_rows(spec_ref, spec_in_ref, me, n_gx, n_gy, spec_send, spec_recv)
    spec_in_ref[me] = spec_ref[me]
    wait_rows(spec_ref, spec_in_ref, members, spec_send, spec_recv)
    side.wait()


def place_on_grid(incoming, order, z_table):
    n_gx, n_gy = lax.axis_size("gx"), lax.axis_size("gy")
    members = n_gx * n_gy
    return pl.pallas_call(
        partial(place_kernel, members, n_gx, n_gy),
        out_shape=[
            jax.ShapeDtypeStruct((6, 128, 128), f32),
            jax.ShapeDtypeStruct((6, 128, 128), f32),
            jax.ShapeDtypeStruct((128, 3, 128), f32),
        ],
        in_specs=vmem(3),
        out_specs=vmem(3),
        scratch_shapes=[
            pltpu.VMEM((768, 1024), bf16),
            pltpu.VMEM((384, 256), f32),
            pltpu.VMEM((128, 3, 128), f32),
            pltpu.SemaphoreType.DMA,
            pltpu.SemaphoreType.DMA,
            pltpu.SemaphoreType.DMA,
            pltpu.SemaphoreType.DMA,
        ],
        compiler_params=pltpu.CompilerParams(
            vmem_limit_bytes=VMEM_LIMIT, collective_id=3, has_side_effects=True
        ),
        name="place",
    )(incoming, order, z_table)


def wave_kernel(
    part_ref, in_ref, outer_ref, outer_back_ref, inner_ref, inner_back_ref, twist_ref,
    out_ref, mid_ref,
):
    freq, turn_re, turn_im, weight = (part_ref[i] for i in range(4))
    cos_t, sin_t = twist_ref[0], twist_ref[1]
    spectrum = []
    for c in range(3):
        hi, lo = split2(in_ref[:, c, :])
        both = dot3(outer_ref[0], outer_ref[1], hi, lo)
        re, im = both[0:128], both[128:256]
        mid_ref[:, 0:128] = re * cos_t + im * sin_t
        mid_ref[:, 128:256] = im * cos_t - re * sin_t
        hi, lo = split2(mid_ref[...])
        both = dot3(hi, lo, inner_ref[0], inner_ref[1])
        spectrum.append((both[:, 0:128], both[:, 128:256]))
    row = lax.broadcasted_iota(jnp.int32, (128, 128), 0)
    col = lax.broadcasted_iota(jnp.int32, (128, 128), 1)
    n_x = (row >> 3) + 16 * (col >> 4)
    n_y = (row & 7) + 8 * (col & 15)
    unit = 2.0 * math.pi / (G * grid_spacing)
    signed = lambda n: jnp.where(n < G // 2, n, n - G).astype(f32) * unit
    k_x, k_y = signed(n_x), signed(n_y)
    k_z = jnp.full((128, 128), freq * unit, f32)
    edge_x = jnp.where(n_x == G // 2, 1.0, 0.0)
    edge_y = jnp.where(n_y == G // 2, 1.0, 0.0)
    edge_z = jnp.where(jnp.full((128, 128), freq, f32) < -63.5, 1.0, 0.0)
    square = k_x * k_x + k_y * k_y + k_z * k_z
    positive = square > 0.0
    safe = jnp.where(positive, square, 1.0)
    green = jnp.where(
        positive,
        (1.0 - 0.25 * square / 3.0) * (1.0 + square) * jnp.exp(-square) / safe,
        0.0,
    ) * (weight / float(G**3))
    over = green / safe
    g_xy = jnp.where(edge_x == edge_y, -over * k_x * k_y, 0.0)
    g_xz = jnp.where(edge_x == edge_z, -over * k_x * k_z, 0.0)
    g_yz = jnp.where(edge_y == edge_z, -over * k_y * k_z, 0.0)
    g_xx = green - over * k_x * k_x
    g_yy = green - over * k_y * k_y
    g_zz = green - over * k_z * k_z
    (x_re, x_im), (y_re, y_im), (z_re, z_im) = spectrum
    z_re, z_im = turn_re * z_re - turn_im * z_im, turn_re * z_im + turn_im * z_re
    flow = [
        (g_xx * x_re + g_xy * y_re + g_xz * z_re, g_xx * x_im + g_xy * y_im + g_xz * z_im),
        (g_xy * x_re + g_yy * y_re + g_yz * z_re, g_xy * x_im + g_yy * y_im + g_yz * z_im),
    ]
    w_re = g_xz * x_re + g_yz * y_re + g_zz * z_re
    w_im = g_xz * x_im + g_yz * y_im + g_zz * z_im
    flow.append((turn_re * w_re + turn_im * w_im, turn_re * w_im - turn_im * w_re))
    for c in range(3):
        mid_ref[:, 0:128], mid_ref[:, 128:256] = flow[c]
        hi, lo = split2(mid_ref[...])
        both = dot3(hi, lo, inner_back_ref[0], inner_back_ref[1])
        re, im = both[:, 0:128], both[:, 128:256]
        hi, lo = split2(
            jnp.concatenate([re * cos_t - im * sin_t, im * cos_t + re * sin_t], axis=0)
        )
        out_ref[:, c, :] = dot3(outer_back_ref[0], outer_back_ref[1], hi, lo)


def wave_flow(spec, table, member):
    special = member % 64 == 63
    freq = jnp.where(member < 64, member + 1, (member - 63) % 64)
    freq = jnp.where(member == 63, -64, freq)
    side = jnp.where(member < 64, 1.0, -1.0)
    part = jnp.stack(
        [
            freq.astype(f32),
            jnp.where(special, 1.0, 0.0),
            jnp.where(special, 0.0, side),
            jnp.where(special, 1.0, 2.0),
        ]
    ).astype(f32)
    return pl.pallas_call(
        wave_kernel,
        out_shape=jax.ShapeDtypeStruct((128, 3, 128), f32),
        in_specs=[pl.BlockSpec(memory_space=pltpu.SMEM)] + vmem(6),
        out_specs=pl.BlockSpec(memory_space=pltpu.VMEM),
        scratch_shapes=[pltpu.VMEM((128, 256), f32)],
        compiler_params=pltpu.CompilerParams(vmem_limit_bytes=VMEM_LIMIT),
        name="wave",
    )(
        part, spec, table["outer"], table["outer_back"], table["inner"],
        table["inner_back"], table["twist"],
    )


ERFC_SHIFT = 4.0
ERFC_POLY = (
    -5.9986000529477224e-05, 1.1337793270330845, 4.308175452878655, 20.093023854033866,
    -8.594175483206275, 489.91788674098177, -1701.7584635921016, 1704.126720738659,
)


def pair_scalars(s2):
    u = lax.rsqrt(s2)
    gauss = jnp.exp2(s2 * (-0.25 * math.log2(math.e)))
    t = pl.reciprocal(s2 * u + ERFC_SHIFT, approx=True)
    w = ERFC_POLY[-1]
    for coefficient in ERFC_POLY[-2::-1]:
        w = w * t + coefficient
    u2 = u * u
    wu = w * u
    along = gauss * (wu * (0.0625 * u2 + 0.375) + 0.125)
    across = (gauss * u2) * (wu * (0.375 - 0.1875 * u2) - 0.125)
    return along, across


def both_halves(v):
    low_half = lax.broadcasted_iota(jnp.int32, (1, 128), 1) < 64
    other = pltpu.roll(v, 64, 1)
    return jnp.where(low_half, v, other), jnp.where(low_half, other, v)


def stage_nodes(ref, weight_stage, right_stage):
    x = [ref[c] for c in range(3)]
    f = [ref[3 + c] for c in range(3)]
    xf = x[0] * f[0] + x[1] * f[1] + x[2] * f[2]
    rows = f + [xf]
    rows += [x[a] * f[b] for a in range(3) for b in range(3)]
    rows += [x[a] * xf for a in range(3)]
    for c, plane in enumerate(rows):
        weight_stage[pl.ds(c, 128, stride=16), :] = plane
    norm = x[0] * x[0] + x[1] * x[1] + x[2] * x[2]
    first, second = [], []
    for h, m, l in [split3(v) for v in x]:
        first += [h, h, m, m, h, l]
        second += [h, m, h, m, l, h]
    one = jnp.ones((128, 128), f32)
    first = [-2.0 * v for v in first] + list(split3(norm)) + [one] * 3
    second += [one] * 3 + list(split3(norm + 0.25))
    for c, plane in enumerate(second):
        right_stage[pl.ds(c, 128, stride=FEATURES), :] = plane
    return first


def build_tables(base, weight_stage, right_stage, weight_ref, right_ref):
    blank = jnp.zeros((32 - FEATURES, 128), f32)

    def build(r, _):
        w = weight_stage[pl.ds(pl.multiple_of(r * 16, 8), 16), :]
        for k, v in enumerate(both_halves(w)):
            hi = v.astype(bf16)
            lo = (v - hi.astype(f32)).astype(bf16)
            weight_ref[base + 2 * r + k] = jnp.concatenate([hi, lo], axis=0)
        w = right_stage[pl.ds(pl.multiple_of(r * FEATURES, 8), FEATURES), :]
        for k, v in enumerate(both_halves(w)):
            right_ref[base + 2 * r + k] = jnp.concatenate([v, blank], axis=0).astype(bf16)
        return 0

    lax.fori_loop(0, 128, build, 0, unroll=16)


def build_left(first, left_stage, left_ref):
    for c, plane in enumerate(first):
        left_stage[pl.ds(c, 128, stride=FEATURES), :] = plane
    eye = jnp.where(
        lax.broadcasted_iota(jnp.int32, (128, 128), 0)
        == lax.broadcasted_iota(jnp.int32, (128, 128), 1),
        1.0,
        0.0,
    ).astype(bf16)
    blank = jnp.zeros((32 - FEATURES, 128), f32)

    def turn_left(r, _):
        v = left_stage[pl.ds(pl.multiple_of(r * FEATURES, 8), FEATURES), :]
        v = jnp.concatenate([v, blank], axis=0).astype(bf16)
        nodes = dot_t(eye, jnp.concatenate([v] * 4, axis=0)).astype(bf16)
        left_ref[2 * r] = nodes[0:64]
        left_ref[2 * r + 1] = nodes[64:128]
        return 0

    lax.fori_loop(0, 128, turn_left, 0, unroll=8)


def pair_kernel(
    list_ref, count_ref, own_ref, beside_ref, own_vel_ref, far_vel_ref,
    weight_ref, right_ref, left_ref, weight_stage, right_stage, left_stage,
    near_acc, far_acc, s2_a, s2_b, tile_a, tile_b,
):
    first = stage_nodes(own_ref, weight_stage, right_stage)
    build_left(first, left_stage, left_ref)
    build_tables(0, weight_stage, right_stage, weight_ref, right_ref)
    stage_nodes(beside_ref, weight_stage, right_stage)
    build_tables(BLOCKS, weight_stage, right_stage, weight_ref, right_ref)

    lane = lax.broadcasted_iota(jnp.int32, (1, 128), 1)
    low_half = lane < 64
    count = count_ref[0]

    def clear(r, _):
        blank = jnp.zeros((W_ROWS, 128), f32)
        far_acc[pl.ds(pl.multiple_of(r * 2 * W_ROWS, 8), W_ROWS), :] = blank
        far_acc[pl.ds(pl.multiple_of(r * 2 * W_ROWS + W_ROWS, 8), W_ROWS), :] = blank
        near_acc[pl.ds(pl.multiple_of(r * W_ROWS, 8), W_ROWS), :] = blank
        return 0

    lax.fori_loop(0, BLOCKS, clear, 0, unroll=8)

    wide = lax.broadcasted_iota(jnp.int32, (64, 128), 1)
    wide_low = wide < 64
    wide_even = (wide & 32) == 0
    narrow = lax.broadcasted_iota(jnp.int32, (32, 128), 1) < 64
    nothing = jnp.zeros((32, 128), bf16)

    def half_of(v, half):
        return jnp.where(narrow, nothing, v) if half else jnp.where(narrow, v, nothing)

    half_keep = [(lane >> 6) == s for s in range(2)]
    blank = jnp.zeros((64, 128), bf16)

    def blocks_of(pair):
        return list_ref[0, pair], list_ref[1, pair]

    def distance_dots(step):
        found = []
        for g in range(GROUPS):
            pairs = [blocks_of((step * GROUPS + g) * STEP + s) for s in range(STEP)]
            left = [left_ref[pairs[s][0]] for s in range(STEP)]
            left = jnp.where(
                wide_low,
                jnp.where(wide_even, left[0], left[1]),
                jnp.where(wide_even, left[2], left[3]),
            )
            right = [half_of(right_ref[pairs[s][1]], s % 2) for s in range(STEP)]
            right = jnp.concatenate(
                [
                    jnp.concatenate([right[0], right[1], blank], axis=0),
                    jnp.concatenate([blank, right[2], right[3]], axis=0),
                ],
                axis=1,
            )
            found.append(dot(left, right))
        return found

    def scalars(s2_ref, tile_ref, pack):
        lanes = slice(pack % 2 * 128, (pack % 2 + 1) * 128)
        along, across = pair_scalars(s2_ref[pack // 2, :, lanes])
        for at, value in ((0, across), (128, along)):
            hi, lo = split2(value)
            tile_ref[pack // 2, at : at + 64, lanes] = hi
            tile_ref[pack // 2, at + 64 : at + 128, lanes] = lo

    def add_to(acc_ref, row, out, top, keep):
        add_h = out[top : top + 16, 0:128] + out[top + 16 : top + 32, 0:128]
        add_f = out[top : top + 8, 128:256] + out[top + 16 : top + 24, 128:256]
        add = jnp.concatenate([add_h, add_f], axis=0)
        if keep is not None:
            add = jnp.where(keep, add, 0.0)
        acc_ref[pl.ds(pl.multiple_of(row, 8), W_ROWS), :] += add

    def sums(step, tile_ref, g):
        numbers = [(step * GROUPS + g) * STEP + s for s in range(STEP)]
        pairs = [blocks_of(n) for n in numbers]
        near = []
        for s, (_, j) in enumerate(pairs):
            part = half_of(weight_ref[j], s % 2)
            near.append(jnp.concatenate([nothing, part] if s // 2 else [part, nothing], axis=1))
        to_near = dot_t(jnp.concatenate(near, axis=0), tile_ref[g])
        for half in range(2):
            lanes = slice(half * 128, (half + 1) * 128)
            a = jnp.concatenate([weight_ref[pairs[2 * half + s][0]] for s in range(2)], axis=0)
            tile = jnp.concatenate([tile_ref[g, 0:128, lanes], tile_ref[g, 128:256, lanes]], axis=1)
            to_far = dot(a, tile)
            for s in range(2):
                add_to(far_acc, list_ref[3, numbers[2 * half + s]], to_far, 32 * s, half_keep[s])
        for s in range(STEP):
            add_to(near_acc, list_ref[2, numbers[s]], to_near, 32 * s, None)

    packs = range(2 * GROUPS)

    def keep_distances(found, s2_ref):
        for g in range(GROUPS):
            s2_ref[g] = found[g]

    def stage(k, s2_next, s2_now, tile_now, tile_last):
        for pack in packs:
            scalars(s2_now, tile_now, pack)
        for g in range(GROUPS):
            sums(k - 1, tile_last, g)
        keep_distances(distance_dots(k + 1), s2_next)

    steps = (count + (STEP * GROUPS - 1)) // (STEP * GROUPS)
    keep_distances(distance_dots(0), s2_a)
    for pack in packs:
        scalars(s2_a, tile_a, pack)
    keep_distances(distance_dots(1), s2_b)

    def body(j, _):
        k = 2 * j + 1
        stage(k, s2_a, s2_b, tile_b, tile_a)
        stage(k + 1, s2_b, s2_a, tile_a, tile_b)
        return 0

    lax.fori_loop(0, (steps + 1) // 2, body, 0)

    chunk = 32
    for side, ref, out_ref in ((0, own_ref, own_vel_ref), (1, beside_ref, far_vel_ref)):
        for top in range(0, 128, chunk):
            planes = []
            for c in range(19):
                at = (2 * top) * W_ROWS + c
                even = far_acc[pl.ds(side * BLOCKS * W_ROWS + at, chunk, stride=2 * W_ROWS), :]
                at += W_ROWS
                odd = far_acc[pl.ds(side * BLOCKS * W_ROWS + at, chunk, stride=2 * W_ROWS), :]
                if side == 0:
                    even += near_acc[pl.ds(at - W_ROWS, chunk, stride=2 * W_ROWS), :]
                    odd += near_acc[pl.ds(at, chunk, stride=2 * W_ROWS), :]
                even = even + pltpu.roll(even, 64, 1)
                odd = odd + pltpu.roll(odd, 64, 1)
                planes.append(jnp.where(low_half, even, odd))
            x = [ref[c, top : top + chunk, :] for c in range(3)]
            h_f, h_xf, h_x_f, h_x_xf, along = (
                planes[0:3], planes[3], planes[4:13], planes[13:16], planes[16:19],
            )
            x_h_f = x[0] * h_f[0] + x[1] * h_f[1] + x[2] * h_f[2] - h_xf
            for c in range(3):
                out_ref[c, top : top + chunk, :] = (
                    along[c]
                    + x[c] * x_h_f
                    - (x[0] * h_x_f[3 * c] + x[1] * h_x_f[3 * c + 1] + x[2] * h_x_f[3 * c + 2])
                    + h_x_xf[c]
                )


def pair_lists(first_list, second_list, count):
    live = jnp.arange(PAIRS, dtype=jnp.int32) < count
    lists = jnp.stack(
        [
            first_list,
            second_list,
            jnp.where(live, first_list, BLOCKS) * W_ROWS,
            jnp.where(live & (first_list != second_list), second_list, 2 * BLOCKS) * W_ROWS,
        ]
    )
    spare = jnp.array([0, 0, BLOCKS * W_ROWS, 2 * BLOCKS * W_ROWS], jnp.int32)
    return jnp.concatenate([lists, jnp.broadcast_to(spare[:, None], (4, 128))], axis=1)


def pair_velocities(own, beside, lists, count):
    plane = jax.ShapeDtypeStruct((3, 128, 128), f32)
    return pl.pallas_call(
        pair_kernel,
        out_shape=[plane, plane],
        in_specs=[pl.BlockSpec(memory_space=pltpu.SMEM)] * 2 + vmem(2),
        out_specs=vmem(2),
        scratch_shapes=[
            pltpu.VMEM((2 * BLOCKS, 32, 128), bf16),
            pltpu.VMEM((2 * BLOCKS, 32, 128), bf16),
            pltpu.VMEM((BLOCKS, 64, 128), bf16),
            pltpu.VMEM((128 * 16, 128), f32),
            pltpu.VMEM((128 * FEATURES, 128), f32),
            pltpu.VMEM((128 * FEATURES, 128), f32),
            pltpu.VMEM(((BLOCKS + 1) * W_ROWS, 128), f32),
            pltpu.VMEM(((2 * BLOCKS + 1) * W_ROWS, 128), f32),
            pltpu.VMEM((GROUPS, 64, 256), f32),
            pltpu.VMEM((GROUPS, 64, 256), f32),
            pltpu.VMEM((GROUPS, 256, 256), bf16),
            pltpu.VMEM((GROUPS, 256, 256), bf16),
        ],
        compiler_params=pltpu.CompilerParams(vmem_limit_bytes=PAIR_VMEM),
        cost_estimate=cost(50),
        name="pairs",
    )(lists, count, own, beside)


def reply_kernel(
    members, n_gx, n_gy, own_ref, far_ref, flow_ref, order_ref, z_ref, in_ref, out_ref,
    wave_ref, beside_ref, hi_ref, lo_ref, low_a, low_b, send_sem, recv_sem, far_send, far_recv,
    wave_send, wave_recv,
):
    g_x = lax.axis_index("gx")
    me = g_x * n_gy + lax.axis_index("gy")
    greet_all(n_gx, n_gy)
    wait_for_all(members)
    far = pltpu.make_async_remote_copy(
        src_ref=far_ref,
        dst_ref=beside_ref,
        send_sem=far_send,
        recv_sem=far_recv,
        device_id=(wrapped(g_x + 1, n_gx), lax.axis_index("gy")),
        device_id_type=pl.DeviceIdType.MESH,
    )
    far.start()
    send_rows(flow_ref, wave_ref, me, n_gx, n_gy, wave_send, wave_recv)
    wave_ref[me] = flow_ref[me]
    far.wait()
    wait_rows(flow_ref, wave_ref, members, wave_send, wave_recv)
    for c in range(3):
        kind = 0 if c < 2 else 1
        hi, lo = split2(jnp.transpose(wave_ref[:, c, :]))
        wave = dot3(hi, lo, z_ref[0, kind], z_ref[1, kind])
        fill_table(c, own_ref[c] + beside_ref[c] + wave, hi_ref, lo_ref)

    def row_at(g, n):
        return g * WIDTH + n

    def put(g, c, n, row):
        out_ref[row_at(g, n), c : c + 1, :] = row

    gather_rows(
        3, members // WIDTH, row_at, hi_ref, lo_ref, order_ref, (low_a, low_b), put
    )

    send_rows(out_ref, in_ref, me, n_gx, n_gy, send_sem, recv_sem)
    in_ref[me] = out_ref[me]
    wait_rows(out_ref, in_ref, members, send_sem, recv_sem)


def reply_message(own_vel, far_vel, wave, order, z_table):
    n_gx, n_gy = lax.axis_size("gx"), lax.axis_size("gy")
    members = n_gx * n_gy
    return pl.pallas_call(
        partial(reply_kernel, members, n_gx, n_gy),
        out_shape=jax.ShapeDtypeStruct((128, 3, 128), f32),
        in_specs=vmem(5),
        out_specs=pl.BlockSpec(memory_space=pltpu.VMEM),
        scratch_shapes=[
            pltpu.VMEM((128, 3, 128), f32),
            pltpu.VMEM((128, 3, 128), f32),
            pltpu.VMEM((3, 128, 128), f32),
            pltpu.VMEM((192, 256), bf16),
            pltpu.VMEM((192, 256), bf16),
            pltpu.VMEM((256, WIDTH * 128), bf16),
            pltpu.VMEM((256, WIDTH * 128), bf16),
            pltpu.SemaphoreType.DMA,
            pltpu.SemaphoreType.DMA,
            pltpu.SemaphoreType.DMA,
            pltpu.SemaphoreType.DMA,
            pltpu.SemaphoreType.DMA,
            pltpu.SemaphoreType.DMA,
        ],
        compiler_params=pltpu.CompilerParams(
            vmem_limit_bytes=VMEM_LIMIT, collective_id=2, has_side_effects=True
        ),
        name="reply",
    )(own_vel, far_vel, wave, order, z_table)


def move_kernel(
    in_ref, route_ref, pos_ref, noise_ref, moved_ref, drift_ref, hi_ref, lo_ref, vel_ref, low_a,
    low_b,
):
    rows = route_ref.shape[0]
    for c in range(3):
        fill_table(c, in_ref[:, c, :], hi_ref, lo_ref)

    def row_at(g, n):
        return g * WIDTH + n

    def put(g, c, n, row):
        vel_ref[c, pl.ds(row_at(g, n), 1), :] = row

    gather_rows(3, rows // WIDTH, row_at, hi_ref, lo_ref, route_ref, (low_a, low_b), put)
    for c in range(3):
        for r in range(rows):
            drift_ref[c : c + 1, r * 128 : (r + 1) * 128] = time_step * vel_ref[c, r : r + 1, :]
    moved_ref[...] = pos_ref[...] + drift_ref[...] + noise_ref[...]


def move_beads(arrived, route, positions, noise):
    flat = jax.ShapeDtypeStruct(positions.shape, f32)
    return pl.pallas_call(
        move_kernel,
        out_shape=[flat, flat],
        in_specs=vmem(4),
        out_specs=vmem(2),
        scratch_shapes=[
            pltpu.VMEM((192, 256), bf16),
            pltpu.VMEM((192, 256), bf16),
            pltpu.VMEM((3, 64, 128), f32),
            pltpu.VMEM((256, WIDTH * 128), bf16),
            pltpu.VMEM((256, WIDTH * 128), bf16),
        ],
        compiler_params=pltpu.CompilerParams(vmem_limit_bytes=VMEM_LIMIT),
        name="move",
    )(arrived, route, positions, noise)


def shards(positions, noise, route, node_perm, pair_first, pair_second, pair_count):
    table = {name: jnp.asarray(value) for name, value in tables().items()}
    row_gx = lax.axis_index("gx")
    member = row_gx * lax.axis_size("gy") + lax.axis_index("gy")
    route = route.reshape(64, 128)
    order = lax.dynamic_index_in_dim(node_perm, row_gx, 0, keepdims=False).reshape(128, 128)
    incoming = send_message(positions, route)
    grid, beside, spec = place_on_grid(incoming, order, table["z"])
    wave = wave_flow(spec, table, member)
    grid, wave = lax.optimization_barrier((grid, wave))
    lists = pair_lists(pair_first[0], pair_second[0], pair_count[0])
    own_vel, far_vel = pair_velocities(grid, beside, lists, pair_count)
    reply = reply_message(own_vel, far_vel, wave, order, table["z"])
    return tuple(move_beads(reply, route, positions, noise))


def solution(mesh):
    in_specs = (
        P(None, ("gx", "gy")),
        P(None, ("gx", "gy")),
        P(("gx", "gy")),
        P(None, "gy", None),
        P(("gx", "gy"), None),
        P(("gx", "gy"), None),
        P(("gx", "gy")),
    )
    out_specs = (P(None, ("gx", "gy")), P(None, ("gx", "gy")))
    return jax.shard_map(shards, mesh=mesh, in_specs=in_specs, out_specs=out_specs, check_vma=False)
```

```python
from functools import partial
import math

import numpy as np
import jax
import jax.numpy as jnp
from jax import lax
from jax.experimental import pallas as pl
from jax.experimental.pallas import tpu as pltpu
from jax.sharding import PartitionSpec as P

G = 128
BLOCKS = 256
PAIRS = 1024
STEP = 4
W_ROWS = 24
GROUPS = 2
FEATURES = 24

fene_k = 30.0
fene_reach = 1.5
bend_k = 2.0
time_step = 0.01
grid_spacing = 4.0

f32 = jnp.float32
bf16 = jnp.bfloat16
VMEM_LIMIT = 24 * 1024 * 1024
PAIR_VMEM = 40 * 1024 * 1024


def dot(a, b):
    return lax.dot_general(a, b, (((1,), (0,)), ((), ())), preferred_element_type=f32)


def dot_t(a, b):
    return lax.dot_general(a, b, (((1,), (1,)), ((), ())), preferred_element_type=f32)


def split2(x):
    hi = x.astype(bf16)
    return hi, (x - hi.astype(f32)).astype(bf16)


def split3(x):
    hi = x.astype(bf16).astype(f32)
    rest = x - hi
    mid = rest.astype(bf16).astype(f32)
    return hi, mid, (rest - mid).astype(bf16).astype(f32)


def dot3(a_hi, a_lo, b_hi, b_lo, form=dot):
    return form(a_hi, b_hi) + form(a_hi, b_lo) + form(a_lo, b_hi)


def split_table(table):
    table = np.asarray(table, np.float64)
    hi = table.astype(np.float32).astype(jnp.bfloat16)
    lo = (table - hi.astype(np.float64)).astype(np.float32).astype(jnp.bfloat16)
    return np.stack([hi, lo])


def tables():
    n = np.arange(G)
    turn = 2.0 * np.pi / G
    member = np.arange(128)
    freq = np.where(member < 64, member + 1, (member - 63) % 64)
    wave = turn * (freq[:, None] * n[None, :] % G)
    even, odd = np.cos(wave), -np.sin(wave)
    special = (member % 64) == 63
    first = (member < 64)[:, None]
    even = np.where(special[:, None], np.cos(wave), even)
    z_xy = np.where(special[:, None] | first, even, odd)
    z_z = np.where(special[:, None] | ~first, even, odd)
    k1, k2 = n // 8, n % 8
    outer = 2.0 * np.pi * (k1[:, None] * k1[None, :] / 16.0 + k2[:, None] * k2[None, :] / 8.0)
    a, b = n // 16, n % 16
    inner = 2.0 * np.pi * (a[:, None] * a[None, :] / 8.0 + b[:, None] * b[None, :] / 16.0)
    twist = turn * (k1[:, None] * a[None, :] + k2[:, None] * b[None, :])
    c_out, s_out, c_in, s_in = np.cos(outer), np.sin(outer), np.cos(inner), np.sin(inner)
    return {
        "z": split_table(np.stack([z_xy, z_z])),
        "outer": split_table(np.concatenate([c_out, -s_out], 0)),
        "outer_back": split_table(np.concatenate([c_out, -s_out], 1)),
        "inner": split_table(np.block([[c_in, -s_in], [s_in, c_in]])),
        "inner_back": split_table(np.block([[c_in, s_in], [-s_in, c_in]])),
        "twist": np.stack([np.cos(twist), np.sin(twist)]).astype(np.float32),
    }


def cost(micros):
    return pl.CostEstimate(flops=int(micros * 1e9), bytes_accessed=1 << 20, transcendentals=0)


def onehot(index, size, width):
    rows = lax.broadcasted_iota(jnp.int32, (size, width), 0)
    return jnp.where(rows == index, 1.0, 0.0).astype(bf16)


def high_part(place):
    return (place >> 7) & 63


def low_part(place):
    return ((place >> 13) << 7) | (place & 127)


WIDTH = 4


def scatter_rows(channels, rows, value_row, place_ref, left_ref, sum_ref):
    group = left_ref.shape[1] // 128
    span = 128 * group

    def turn(g, _):
        low = []
        for j in range(group):
            place = place_ref[pl.ds(g * group + j, 1), :]
            high_hot = onehot(high_part(place), 64, 128)
            low.append(onehot(low_part(place), 256, 128))
            for c in range(channels):
                hi, lo = split2(value_row(c, g * group + j))
                left_ref[c * 128 : c * 128 + 64, j * 128 : (j + 1) * 128] = high_hot * hi
                left_ref[c * 128 + 64 : c * 128 + 128, j * 128 : (j + 1) * 128] = high_hot * lo
        moved = dot_t(left_ref[...], jnp.concatenate(low, axis=1))
        for c in range(channels):
            sum_ref[c * 64 : (c + 1) * 64, :] += (
                moved[c * 128 : c * 128 + 64] + moved[c * 128 + 64 : c * 128 + 128]
            )
        return 0

    sum_ref[...] = jnp.zeros_like(sum_ref)
    lax.fori_loop(0, rows // group, turn, 0)


def unpack_sums(channels, sum_ref, put):
    for c in range(channels):
        for half in range(2):
            put(c, half, sum_ref[c * 64 : (c + 1) * 64, half * 128 : (half + 1) * 128])


def gather_rows(channels, turns, row_at, table_hi_ref, table_lo_ref, place_ref, low, put):
    def build(g, side):
        for n in range(WIDTH):
            place = place_ref[pl.ds(row_at(g, n), 1), :]
            low[side][:, n * 128 : (n + 1) * 128] = onehot(low_part(place), 256, 128)

    def use(g, side):
        found = dot(table_hi_ref[...], low[side][...]) + dot(table_lo_ref[...], low[side][...])
        for n in range(WIDTH):
            high = high_part(place_ref[pl.ds(row_at(g, n), 1), :])
            rows_of = lax.broadcasted_iota(jnp.int32, (64, 128), 0) == high
            for c in range(channels):
                part = found[c * 64 : (c + 1) * 64, n * 128 : (n + 1) * 128]
                put(g, c, n, jnp.sum(jnp.where(rows_of, part, 0.0), axis=0, keepdims=True))

    build(0, 0)

    def turn(h, _):
        build(2 * h + 1, 1)
        use(2 * h, 0)
        build(2 * h + 2, 0)
        use(2 * h + 1, 1)
        return 0

    lax.fori_loop(0, turns // 2 - 1, turn, 0)
    build(turns - 1, 1)
    use(turns - 2, 0)
    use(turns - 1, 1)


def fill_table(c, plane, table_hi_ref, table_lo_ref):
    hi, lo = split2(plane)
    for ref, part in ((table_hi_ref, hi), (table_lo_ref, lo)):
        ref[c * 64 : (c + 1) * 64, 0:128] = part[0:64]
        ref[c * 64 : (c + 1) * 64, 128:256] = part[64:128]


def wrapped(index, size):
    return jnp.where(index >= size, index - size, index)


def for_peers(n_gx, n_gy, do):
    me_x, me_y = lax.axis_index("gx"), lax.axis_index("gy")
    ys = [wrapped(me_y + d, n_gy) for d in range(n_gy)]
    for y in ys[1:]:
        do(me_x, y)

    def turn(d, _):
        x = wrapped(me_x + d, n_gx)
        for y in ys:
            do(x, y)
        return 0

    lax.fori_loop(1, n_gx, turn, 0)


def greet_all(n_gx, n_gy):
    barrier = pltpu.get_barrier_semaphore()

    def greet(x, y):
        pl.semaphore_signal(
            barrier, inc=1, device_id=(x, y), device_id_type=pl.DeviceIdType.MESH
        )

    for_peers(n_gx, n_gy, greet)


def wait_for_all(members):
    pl.semaphore_wait(pltpu.get_barrier_semaphore(), members - 1)


def send_rows(out_ref, in_ref, me, n_gx, n_gy, send_sem, recv_sem):
    def send(x, y):
        pltpu.make_async_remote_copy(
            src_ref=out_ref.at[x * n_gy + y],
            dst_ref=in_ref.at[me],
            send_sem=send_sem,
            recv_sem=recv_sem,
            device_id=(x, y),
            device_id_type=pl.DeviceIdType.MESH,
        ).start()

    for_peers(n_gx, n_gy, send)


def wait_rows(out_ref, in_ref, members, send_sem, recv_sem):
    every = pltpu.make_async_remote_copy(
        src_ref=out_ref.at[pl.ds(0, members - 1)],
        dst_ref=in_ref.at[pl.ds(0, members - 1)],
        send_sem=send_sem,
        recv_sem=recv_sem,
        device_id=(0, 0),
        device_id_type=pl.DeviceIdType.MESH,
    )
    every.wait_send()
    every.wait_recv()


def chain_forces(x):
    lane = lax.broadcasted_iota(jnp.int32, x[0].shape, 1) & 63
    last = lane == 63
    ahead = lambda v: pltpu.roll(v, 127, 1)
    behind = lambda v: pltpu.roll(v, 1, 1)
    bond = [jnp.where(last, 0.5, ahead(v) - v) for v in x]
    square = bond[0] * bond[0] + bond[1] * bond[1] + bond[2] * bond[2]
    inverse = lax.rsqrt(square)
    unit = [v * inverse for v in bond]
    following = [ahead(v) for v in unit]
    cosine = unit[0] * following[0] + unit[1] * following[1] + unit[2] * following[2]
    bends = lane < 62
    stretch = fene_k / (1.0 - square / fene_reach**2)
    before = behind(jnp.where(bends, 1.0, 0.0))
    cosine_before = behind(cosine)
    grad = []
    for c in range(3):
        pull = jnp.where(bends, following[c] - cosine * unit[c], 0.0)
        push = before * (behind(unit[c]) - cosine_before * unit[c])
        push = jnp.where(lane == 0, 0.0, push)
        grad.append(
            jnp.where(last, 0.0, stretch * bond[c] - bend_k * inverse * (pull + push))
        )
    return [g - jnp.where(lane == 0, 0.0, behind(g)) for g in grad]


def send_kernel(
    members, n_gx, n_gy, pos_ref, route_ref, in_ref, out_ref, plane_ref, left_ref, sum_ref, send_sem,
    recv_sem,
):
    me = lax.axis_index("gx") * n_gy + lax.axis_index("gy")
    greet_all(n_gx, n_gy)
    rows = route_ref.shape[0]
    for c in range(3):
        for r in range(rows):
            plane_ref[c, r : r + 1, :] = pos_ref[c : c + 1, r * 128 : (r + 1) * 128]
    forces = chain_forces([plane_ref[c] for c in range(3)])
    for c in range(3):
        plane_ref[3 + c] = forces[c]
    scatter_rows(
        6, rows, lambda c, r: plane_ref[c, pl.ds(r, 1), :], route_ref, left_ref, sum_ref
    )
    for c in range(6):
        out_ref[0:64, c, :] = sum_ref[c * 64 : (c + 1) * 64, 0:128]
        out_ref[64:128, c, :] = sum_ref[c * 64 : (c + 1) * 64, 128:256]
    wait_for_all(members)

    send_rows(out_ref, in_ref, me, n_gx, n_gy, send_sem, recv_sem)
    in_ref[me] = out_ref[me]
    wait_rows(out_ref, in_ref, members, send_sem, recv_sem)


def vmem(n):
    return [pl.BlockSpec(memory_space=pltpu.VMEM)] * n


def send_message(positions, route):
    n_gx, n_gy = lax.axis_size("gx"), lax.axis_size("gy")
    members = n_gx * n_gy
    return pl.pallas_call(
        partial(send_kernel, members, n_gx, n_gy),
        out_shape=jax.ShapeDtypeStruct((128, 6, 128), f32),
        in_specs=vmem(2),
        out_specs=pl.BlockSpec(memory_space=pltpu.VMEM),
        scratch_shapes=[
            pltpu.VMEM((128, 6, 128), f32),
            pltpu.VMEM((6, 64, 128), f32),
            pltpu.VMEM((768, 1024), bf16),
            pltpu.VMEM((384, 256), f32),
            pltpu.SemaphoreType.DMA,
            pltpu.SemaphoreType.DMA,
        ],
        compiler_params=pltpu.CompilerParams(
            vmem_limit_bytes=VMEM_LIMIT, collective_id=1, has_side_effects=True
        ),
        name="send",
    )(positions, route)


def place_kernel(
    members, n_gx, n_gy, in_ref, order_ref, z_ref, grid_ref, beside_ref, spec_in_ref,
    left_ref, sum_ref, spec_ref, spec_send, spec_recv, side_send, side_recv,
):
    g_x = lax.axis_index("gx")
    me = g_x * n_gy + lax.axis_index("gy")
    greet_all(n_gx, n_gy)
    scatter_rows(
        6, members, lambda c, r: in_ref[r, c : c + 1, :], order_ref, left_ref, sum_ref
    )

    def to_grid(c, half, value):
        grid_ref[c, half * 64 : (half + 1) * 64, :] = value

    unpack_sums(6, sum_ref, to_grid)
    for c in range(3):
        hi, lo = split2(grid_ref[3 + c])
        kind = 0 if c < 2 else 1
        spec_ref[:, c, :] = dot3(z_ref[0, kind], z_ref[1, kind], hi, lo, dot_t)
    wait_for_all(members)
    side = pltpu.make_async_remote_copy(
        src_ref=grid_ref,
        dst_ref=beside_ref,
        send_sem=side_send,
        recv_sem=side_recv,
        device_id=(wrapped(g_x + n_gx - 1, n_gx), lax.axis_index("gy")),
        device_id_type=pl.DeviceIdType.MESH,
    )

    send_rows(spec_ref, spec_in_ref, me, n_gx, n_gy, spec_send, spec_recv)
    side.start()
    spec_in_ref[me] = spec_ref[me]
    wait_rows(spec_ref, spec_in_ref, members, spec_send, spec_recv)
    side.wait()


def place_on_grid(incoming, order, z_table):
    n_gx, n_gy = lax.axis_size("gx"), lax.axis_size("gy")
    members = n_gx * n_gy
    return pl.pallas_call(
        partial(place_kernel, members, n_gx, n_gy),
        out_shape=[
            jax.ShapeDtypeStruct((6, 128, 128), f32),
            jax.ShapeDtypeStruct((6, 128, 128), f32),
            jax.ShapeDtypeStruct((128, 3, 128), f32),
        ],
        in_specs=vmem(3),
        out_specs=vmem(3),
        scratch_shapes=[
            pltpu.VMEM((768, 1024), bf16),
            pltpu.VMEM((384, 256), f32),
            pltpu.VMEM((128, 3, 128), f32),
            pltpu.SemaphoreType.DMA,
            pltpu.SemaphoreType.DMA,
            pltpu.SemaphoreType.DMA,
            pltpu.SemaphoreType.DMA,
        ],
        compiler_params=pltpu.CompilerParams(
            vmem_limit_bytes=VMEM_LIMIT, collective_id=3, has_side_effects=True
        ),
        name="place",
    )(incoming, order, z_table)


def wave_kernel(
    part_ref, in_ref, outer_ref, outer_back_ref, inner_ref, inner_back_ref, twist_ref,
    out_ref, mid_ref,
):
    freq, turn_re, turn_im, weight = (part_ref[i] for i in range(4))
    cos_t, sin_t = twist_ref[0], twist_ref[1]
    spectrum = []
    for c in range(3):
        hi, lo = split2(in_ref[:, c, :])
        both = dot3(outer_ref[0], outer_ref[1], hi, lo)
        re, im = both[0:128], both[128:256]
        mid_ref[:, 0:128] = re * cos_t + im * sin_t
        mid_ref[:, 128:256] = im * cos_t - re * sin_t
        hi, lo = split2(mid_ref[...])
        both = dot3(hi, lo, inner_ref[0], inner_ref[1])
        spectrum.append((both[:, 0:128], both[:, 128:256]))
    row = lax.broadcasted_iota(jnp.int32, (128, 128), 0)
    col = lax.broadcasted_iota(jnp.int32, (128, 128), 1)
    n_x = (row >> 3) + 16 * (col >> 4)
    n_y = (row & 7) + 8 * (col & 15)
    unit = 2.0 * math.pi / (G * grid_spacing)
    signed = lambda n: jnp.where(n < G // 2, n, n - G).astype(f32) * unit
    k_x, k_y = signed(n_x), signed(n_y)
    k_z = jnp.full((128, 128), freq * unit, f32)
    edge_x = jnp.where(n_x == G // 2, 1.0, 0.0)
    edge_y = jnp.where(n_y == G // 2, 1.0, 0.0)
    edge_z = jnp.where(jnp.full((128, 128), freq, f32) < -63.5, 1.0, 0.0)
    square = k_x * k_x + k_y * k_y + k_z * k_z
    positive = square > 0.0
    safe = jnp.where(positive, square, 1.0)
    green = jnp.where(
        positive,
        (1.0 - 0.25 * square / 3.0) * (1.0 + square) * jnp.exp(-square) / safe,
        0.0,
    ) * (weight / float(G**3))
    over = green / safe
    g_xy = jnp.where(edge_x == edge_y, -over * k_x * k_y, 0.0)
    g_xz = jnp.where(edge_x == edge_z, -over * k_x * k_z, 0.0)
    g_yz = jnp.where(edge_y == edge_z, -over * k_y * k_z, 0.0)
    g_xx = green - over * k_x * k_x
    g_yy = green - over * k_y * k_y
    g_zz = green - over * k_z * k_z
    (x_re, x_im), (y_re, y_im), (z_re, z_im) = spectrum
    z_re, z_im = turn_re * z_re - turn_im * z_im, turn_re * z_im + turn_im * z_re
    flow = [
        (g_xx * x_re + g_xy * y_re + g_xz * z_re, g_xx * x_im + g_xy * y_im + g_xz * z_im),
        (g_xy * x_re + g_yy * y_re + g_yz * z_re, g_xy * x_im + g_yy * y_im + g_yz * z_im),
    ]
    w_re = g_xz * x_re + g_yz * y_re + g_zz * z_re
    w_im = g_xz * x_im + g_yz * y_im + g_zz * z_im
    flow.append((turn_re * w_re + turn_im * w_im, turn_re * w_im - turn_im * w_re))
    for c in range(3):
        mid_ref[:, 0:128], mid_ref[:, 128:256] = flow[c]
        hi, lo = split2(mid_ref[...])
        both = dot3(hi, lo, inner_back_ref[0], inner_back_ref[1])
        re, im = both[:, 0:128], both[:, 128:256]
        hi, lo = split2(
            jnp.concatenate([re * cos_t - im * sin_t, im * cos_t + re * sin_t], axis=0)
        )
        out_ref[:, c, :] = dot3(outer_back_ref[0], outer_back_ref[1], hi, lo)


def wave_flow(spec, table, member):
    special = member % 64 == 63
    freq = jnp.where(member < 64, member + 1, (member - 63) % 64)
    freq = jnp.where(member == 63, -64, freq)
    side = jnp.where(member < 64, 1.0, -1.0)
    part = jnp.stack(
        [
            freq.astype(f32),
            jnp.where(special, 1.0, 0.0),
            jnp.where(special, 0.0, side),
            jnp.where(special, 1.0, 2.0),
        ]
    ).astype(f32)
    return pl.pallas_call(
        wave_kernel,
        out_shape=jax.ShapeDtypeStruct((128, 3, 128), f32),
        in_specs=[pl.BlockSpec(memory_space=pltpu.SMEM)] + vmem(6),
        out_specs=pl.BlockSpec(memory_space=pltpu.VMEM),
        scratch_shapes=[pltpu.VMEM((128, 256), f32)],
        compiler_params=pltpu.CompilerParams(vmem_limit_bytes=VMEM_LIMIT),
        name="wave",
    )(
        part, spec, table["outer"], table["outer_back"], table["inner"],
        table["inner_back"], table["twist"],
    )


ERFC_SHIFT = 4.0
ERFC_POLY = (
    -5.9986000529477224e-05, 1.1337793270330845, 4.308175452878655, 20.093023854033866,
    -8.594175483206275, 489.91788674098177, -1701.7584635921016, 1704.126720738659,
)


def pair_scalars(s2):
    u = lax.rsqrt(s2)
    gauss = jnp.exp2(s2 * (-0.25 * math.log2(math.e)))
    t = pl.reciprocal(s2 * u + ERFC_SHIFT, approx=True)
    w = ERFC_POLY[-1]
    for coefficient in ERFC_POLY[-2::-1]:
        w = w * t + coefficient
    u2 = u * u
    wu = w * u
    along = gauss * (wu * (0.0625 * u2 + 0.375) + 0.125)
    across = (gauss * u2) * (wu * (0.375 - 0.1875 * u2) - 0.125)
    return along, across


def both_halves(v):
    low_half = lax.broadcasted_iota(jnp.int32, (1, 128), 1) < 64
    other = pltpu.roll(v, 64, 1)
    return jnp.where(low_half, v, other), jnp.where(low_half, other, v)


def stage_nodes(ref, weight_stage, right_stage):
    x = [ref[c] for c in range(3)]
    f = [ref[3 + c] for c in range(3)]
    xf = x[0] * f[0] + x[1] * f[1] + x[2] * f[2]
    rows = f + [xf]
    rows += [x[a] * f[b] for a in range(3) for b in range(3)]
    rows += [x[a] * xf for a in range(3)]
    for c, plane in enumerate(rows):
        weight_stage[pl.ds(c, 128, stride=16), :] = plane
    norm = x[0] * x[0] + x[1] * x[1] + x[2] * x[2]
    first, second = [], []
    for h, m, l in [split3(v) for v in x]:
        first += [h, h, m, m, h, l]
        second += [h, m, h, m, l, h]
    one = jnp.ones((128, 128), f32)
    first = [-2.0 * v for v in first] + list(split3(norm)) + [one] * 3
    second += [one] * 3 + list(split3(norm + 0.25))
    for c, plane in enumerate(second):
        right_stage[pl.ds(c, 128, stride=FEATURES), :] = plane
    return first


def build_tables(base, weight_stage, right_stage, weight_ref, right_ref):
    blank = jnp.zeros((32 - FEATURES, 128), f32)

    def build(r, _):
        w = weight_stage[pl.ds(pl.multiple_of(r * 16, 8), 16), :]
        for k, v in enumerate(both_halves(w)):
            hi = v.astype(bf16)
            lo = (v - hi.astype(f32)).astype(bf16)
            weight_ref[base + 2 * r + k] = jnp.concatenate([hi, lo], axis=0)
        w = right_stage[pl.ds(pl.multiple_of(r * FEATURES, 8), FEATURES), :]
        for k, v in enumerate(both_halves(w)):
            right_ref[base + 2 * r + k] = jnp.concatenate([v, blank], axis=0).astype(bf16)
        return 0

    lax.fori_loop(0, 128, build, 0, unroll=16)


def build_left(first, left_stage, left_ref):
    for c, plane in enumerate(first):
        left_stage[pl.ds(c, 128, stride=FEATURES), :] = plane
    eye = jnp.where(
        lax.broadcasted_iota(jnp.int32, (128, 128), 0)
        == lax.broadcasted_iota(jnp.int32, (128, 128), 1),
        1.0,
        0.0,
    ).astype(bf16)
    blank = jnp.zeros((32 - FEATURES, 128), f32)

    def turn_left(r, _):
        v = left_stage[pl.ds(pl.multiple_of(r * FEATURES, 8), FEATURES), :]
        v = jnp.concatenate([v, blank], axis=0).astype(bf16)
        nodes = dot_t(eye, jnp.concatenate([v] * 4, axis=0)).astype(bf16)
        left_ref[2 * r] = nodes[0:64]
        left_ref[2 * r + 1] = nodes[64:128]
        return 0

    lax.fori_loop(0, 128, turn_left, 0, unroll=8)


def pair_kernel(
    list_ref, count_ref, own_ref, beside_ref, own_vel_ref, far_vel_ref,
    weight_ref, right_ref, left_ref, weight_stage, right_stage, left_stage,
    near_acc, far_acc, s2_a, s2_b, tile_a, tile_b,
):
    first = stage_nodes(own_ref, weight_stage, right_stage)
    build_left(first, left_stage, left_ref)
    build_tables(0, weight_stage, right_stage, weight_ref, right_ref)
    stage_nodes(beside_ref, weight_stage, right_stage)
    build_tables(BLOCKS, weight_stage, right_stage, weight_ref, right_ref)

    lane = lax.broadcasted_iota(jnp.int32, (1, 128), 1)
    low_half = lane < 64
    count = count_ref[0]

    def clear(r, _):
        blank = jnp.zeros((W_ROWS, 128), f32)
        far_acc[pl.ds(pl.multiple_of(r * 2 * W_ROWS, 8), W_ROWS), :] = blank
        far_acc[pl.ds(pl.multiple_of(r * 2 * W_ROWS + W_ROWS, 8), W_ROWS), :] = blank
        near_acc[pl.ds(pl.multiple_of(r * W_ROWS, 8), W_ROWS), :] = blank
        return 0

    lax.fori_loop(0, BLOCKS, clear, 0, unroll=8)

    wide = lax.broadcasted_iota(jnp.int32, (64, 128), 1)
    wide_low = wide < 64
    wide_even = (wide & 32) == 0
    narrow = lax.broadcasted_iota(jnp.int32, (32, 128), 1) < 64
    nothing = jnp.zeros((32, 128), bf16)

    def half_of(v, half):
        return jnp.where(narrow, nothing, v) if half else jnp.where(narrow, v, nothing)

    half_keep = [(lane >> 6) == s for s in range(2)]
    blank = jnp.zeros((64, 128), bf16)

    def blocks_of(pair):
        return list_ref[0, pair], list_ref[1, pair]

    def distance_dots(step):
        found = []
        for g in range(GROUPS):
            pairs = [blocks_of((step * GROUPS + g) * STEP + s) for s in range(STEP)]
            left = [left_ref[pairs[s][0]] for s in range(STEP)]
            left = jnp.where(
                wide_low,
                jnp.where(wide_even, left[0], left[1]),
                jnp.where(wide_even, left[2], left[3]),
            )
            right = [half_of(right_ref[pairs[s][1]], s % 2) for s in range(STEP)]
            right = jnp.concatenate(
                [
                    jnp.concatenate([right[0], right[1], blank], axis=0),
                    jnp.concatenate([blank, right[2], right[3]], axis=0),
                ],
                axis=1,
            )
            found.append(dot(left, right))
        return found

    def scalars(s2_ref, tile_ref, pack):
        half = pack % 2
        along, across = pair_scalars(s2_ref[pack // 2, :, half * 128 : (half + 1) * 128])
        for at, value in ((0, across), (128, along)):
            hi, lo = split2(value)
            tile_ref[pack, at : at + 64, :] = hi
            tile_ref[pack, at + 64 : at + 128, :] = lo

    def sum_dots(step, tile_ref, pack):
        tile = tile_ref[pack]
        pairs = [blocks_of((step * 2 * GROUPS + pack) * 2 + s) for s in range(2)]
        a = jnp.concatenate([weight_ref[i] for i, _ in pairs], axis=0)
        b = jnp.concatenate(
            [half_of(weight_ref[j], s) for s, (_, j) in enumerate(pairs)], axis=0
        )
        to_far = dot(a, jnp.concatenate([tile[0:128], tile[128:256]], axis=1))
        return dot_t(b, tile), to_far

    def add_sums(step, pack, to_near, to_far):
        for s in range(2):
            number = (step * 2 * GROUPS + pack) * 2 + s
            for out, acc_ref, row, keep in (
                (to_near, near_acc, list_ref[2, number], None),
                (to_far, far_acc, list_ref[3, number], half_keep[s]),
            ):
                top = 32 * s
                add_h = out[top : top + 16, 0:128] + out[top + 16 : top + 32, 0:128]
                add_f = out[top : top + 8, 128:256] + out[top + 16 : top + 24, 128:256]
                add = jnp.concatenate([add_h, add_f], axis=0)
                if keep is not None:
                    add = jnp.where(keep, add, 0.0)
                acc_ref[pl.ds(pl.multiple_of(row, 8), W_ROWS), :] += add

    packs = range(2 * GROUPS)

    def keep_distances(found, s2_ref):
        for g in range(GROUPS):
            s2_ref[g] = found[g]

    def stage(k, s2_next, s2_now, tile_now, tile_last):
        for pack in packs:
            scalars(s2_now, tile_now, pack)
        for pack in packs:
            add_sums(k - 1, pack, *sum_dots(k - 1, tile_last, pack))
        keep_distances(distance_dots(k + 1), s2_next)

    steps = (count + (STEP * GROUPS - 1)) // (STEP * GROUPS)
    keep_distances(distance_dots(0), s2_a)
    for pack in packs:
        scalars(s2_a, tile_a, pack)
    keep_distances(distance_dots(1), s2_b)

    def body(j, _):
        k = 2 * j + 1
        stage(k, s2_a, s2_b, tile_b, tile_a)
        stage(k + 1, s2_b, s2_a, tile_a, tile_b)
        return 0

    lax.fori_loop(0, (steps + 1) // 2, body, 0)

    chunk = 32
    for side, ref, out_ref in ((0, own_ref, own_vel_ref), (1, beside_ref, far_vel_ref)):
        for top in range(0, 128, chunk):
            planes = []
            for c in range(19):
                at = (2 * top) * W_ROWS + c
                even = far_acc[pl.ds(side * BLOCKS * W_ROWS + at, chunk, stride=2 * W_ROWS), :]
                at += W_ROWS
                odd = far_acc[pl.ds(side * BLOCKS * W_ROWS + at, chunk, stride=2 * W_ROWS), :]
                if side == 0:
                    even += near_acc[pl.ds(at - W_ROWS, chunk, stride=2 * W_ROWS), :]
                    odd += near_acc[pl.ds(at, chunk, stride=2 * W_ROWS), :]
                even = even + pltpu.roll(even, 64, 1)
                odd = odd + pltpu.roll(odd, 64, 1)
                planes.append(jnp.where(low_half, even, odd))
            x = [ref[c, top : top + chunk, :] for c in range(3)]
            h_f, h_xf, h_x_f, h_x_xf, along = (
                planes[0:3], planes[3], planes[4:13], planes[13:16], planes[16:19],
            )
            x_h_f = x[0] * h_f[0] + x[1] * h_f[1] + x[2] * h_f[2] - h_xf
            for c in range(3):
                out_ref[c, top : top + chunk, :] = (
                    along[c]
                    + x[c] * x_h_f
                    - (x[0] * h_x_f[3 * c] + x[1] * h_x_f[3 * c + 1] + x[2] * h_x_f[3 * c + 2])
                    + h_x_xf[c]
                )


def pair_lists(first_list, second_list, count):
    live = jnp.arange(PAIRS, dtype=jnp.int32) < count
    lists = jnp.stack(
        [
            first_list,
            second_list,
            jnp.where(live, first_list, BLOCKS) * W_ROWS,
            jnp.where(live & (first_list != second_list), second_list, 2 * BLOCKS) * W_ROWS,
        ]
    )
    spare = jnp.array([0, 0, BLOCKS * W_ROWS, 2 * BLOCKS * W_ROWS], jnp.int32)
    return jnp.concatenate([lists, jnp.broadcast_to(spare[:, None], (4, 128))], axis=1)


def pair_velocities(own, beside, lists, count):
    plane = jax.ShapeDtypeStruct((3, 128, 128), f32)
    return pl.pallas_call(
        pair_kernel,
        out_shape=[plane, plane],
        in_specs=[pl.BlockSpec(memory_space=pltpu.SMEM)] * 2 + vmem(2),
        out_specs=vmem(2),
        scratch_shapes=[
            pltpu.VMEM((2 * BLOCKS, 32, 128), bf16),
            pltpu.VMEM((2 * BLOCKS, 32, 128), bf16),
            pltpu.VMEM((BLOCKS, 64, 128), bf16),
            pltpu.VMEM((128 * 16, 128), f32),
            pltpu.VMEM((128 * FEATURES, 128), f32),
            pltpu.VMEM((128 * FEATURES, 128), f32),
            pltpu.VMEM(((BLOCKS + 1) * W_ROWS, 128), f32),
            pltpu.VMEM(((2 * BLOCKS + 1) * W_ROWS, 128), f32),
            pltpu.VMEM((GROUPS, 64, 256), f32),
            pltpu.VMEM((GROUPS, 64, 256), f32),
            pltpu.VMEM((2 * GROUPS, 256, 128), bf16),
            pltpu.VMEM((2 * GROUPS, 256, 128), bf16),
        ],
        compiler_params=pltpu.CompilerParams(vmem_limit_bytes=PAIR_VMEM),
        cost_estimate=cost(50),
        name="pairs",
    )(lists, count, own, beside)


def reply_kernel(
    members, n_gx, n_gy, own_ref, far_ref, flow_ref, order_ref, z_ref, in_ref, out_ref,
    wave_ref, beside_ref, hi_ref, lo_ref, low_a, low_b, send_sem, recv_sem, far_send, far_recv,
    wave_send, wave_recv,
):
    g_x = lax.axis_index("gx")
    me = g_x * n_gy + lax.axis_index("gy")
    greet_all(n_gx, n_gy)
    wait_for_all(members)
    far = pltpu.make_async_remote_copy(
        src_ref=far_ref,
        dst_ref=beside_ref,
        send_sem=far_send,
        recv_sem=far_recv,
        device_id=(wrapped(g_x + 1, n_gx), lax.axis_index("gy")),
        device_id_type=pl.DeviceIdType.MESH,
    )
    far.start()
    send_rows(flow_ref, wave_ref, me, n_gx, n_gy, wave_send, wave_recv)
    wave_ref[me] = flow_ref[me]
    far.wait()
    wait_rows(flow_ref, wave_ref, members, wave_send, wave_recv)
    for c in range(3):
        kind = 0 if c < 2 else 1
        hi, lo = split2(jnp.transpose(wave_ref[:, c, :]))
        wave = dot3(hi, lo, z_ref[0, kind], z_ref[1, kind])
        fill_table(c, own_ref[c] + beside_ref[c] + wave, hi_ref, lo_ref)

    def row_at(g, n):
        return g * WIDTH + n

    def put(g, c, n, row):
        out_ref[row_at(g, n), c : c + 1, :] = row

    gather_rows(
        3, members // WIDTH, row_at, hi_ref, lo_ref, order_ref, (low_a, low_b), put
    )

    send_rows(out_ref, in_ref, me, n_gx, n_gy, send_sem, recv_sem)
    in_ref[me] = out_ref[me]
    wait_rows(out_ref, in_ref, members, send_sem, recv_sem)


def reply_message(own_vel, far_vel, wave, order, z_table):
    n_gx, n_gy = lax.axis_size("gx"), lax.axis_size("gy")
    members = n_gx * n_gy
    return pl.pallas_call(
        partial(reply_kernel, members, n_gx, n_gy),
        out_shape=jax.ShapeDtypeStruct((128, 3, 128), f32),
        in_specs=vmem(5),
        out_specs=pl.BlockSpec(memory_space=pltpu.VMEM),
        scratch_shapes=[
            pltpu.VMEM((128, 3, 128), f32),
            pltpu.VMEM((128, 3, 128), f32),
            pltpu.VMEM((3, 128, 128), f32),
            pltpu.VMEM((192, 256), bf16),
            pltpu.VMEM((192, 256), bf16),
            pltpu.VMEM((256, WIDTH * 128), bf16),
            pltpu.VMEM((256, WIDTH * 128), bf16),
            pltpu.SemaphoreType.DMA,
            pltpu.SemaphoreType.DMA,
            pltpu.SemaphoreType.DMA,
            pltpu.SemaphoreType.DMA,
            pltpu.SemaphoreType.DMA,
            pltpu.SemaphoreType.DMA,
        ],
        compiler_params=pltpu.CompilerParams(
            vmem_limit_bytes=VMEM_LIMIT, collective_id=2, has_side_effects=True
        ),
        name="reply",
    )(own_vel, far_vel, wave, order, z_table)


def move_kernel(
    in_ref, route_ref, pos_ref, noise_ref, moved_ref, drift_ref, hi_ref, lo_ref, vel_ref, low_a,
    low_b,
):
    rows = route_ref.shape[0]
    for c in range(3):
        fill_table(c, in_ref[:, c, :], hi_ref, lo_ref)

    def row_at(g, n):
        return g * WIDTH + n

    def put(g, c, n, row):
        vel_ref[c, pl.ds(row_at(g, n), 1), :] = row

    gather_rows(3, rows // WIDTH, row_at, hi_ref, lo_ref, route_ref, (low_a, low_b), put)
    for c in range(3):
        for r in range(rows):
            drift_ref[c : c + 1, r * 128 : (r + 1) * 128] = time_step * vel_ref[c, r : r + 1, :]
    moved_ref[...] = pos_ref[...] + drift_ref[...] + noise_ref[...]


def move_beads(arrived, route, positions, noise):
    flat = jax.ShapeDtypeStruct(positions.shape, f32)
    return pl.pallas_call(
        move_kernel,
        out_shape=[flat, flat],
        in_specs=vmem(4),
        out_specs=vmem(2),
        scratch_shapes=[
            pltpu.VMEM((192, 256), bf16),
            pltpu.VMEM((192, 256), bf16),
            pltpu.VMEM((3, 64, 128), f32),
            pltpu.VMEM((256, WIDTH * 128), bf16),
            pltpu.VMEM((256, WIDTH * 128), bf16),
        ],
        compiler_params=pltpu.CompilerParams(vmem_limit_bytes=VMEM_LIMIT),
        name="move",
    )(arrived, route, positions, noise)


def shards(positions, noise, route, node_perm, pair_first, pair_second, pair_count):
    table = {name: jnp.asarray(value) for name, value in tables().items()}
    row_gx = lax.axis_index("gx")
    member = row_gx * lax.axis_size("gy") + lax.axis_index("gy")
    route = route.reshape(64, 128)
    order = lax.dynamic_index_in_dim(node_perm, row_gx, 0, keepdims=False).reshape(128, 128)
    incoming = send_message(positions, route)
    grid, beside, spec = place_on_grid(incoming, order, table["z"])
    wave = wave_flow(spec, table, member)
    grid, wave = lax.optimization_barrier((grid, wave))
    lists = pair_lists(pair_first[0], pair_second[0], pair_count[0])
    own_vel, far_vel = pair_velocities(grid, beside, lists, pair_count)
    reply = reply_message(own_vel, far_vel, wave, order, table["z"])
    return tuple(move_beads(reply, route, positions, noise))


def solution(mesh):
    in_specs = (
        P(None, ("gx", "gy")),
        P(None, ("gx", "gy")),
        P(("gx", "gy")),
        P(None, "gy", None),
        P(("gx", "gy"), None),
        P(("gx", "gy"), None),
        P(("gx", "gy")),
    )
    out_specs = (P(None, ("gx", "gy")), P(None, ("gx", "gy")))
    return jax.shard_map(shards, mesh=mesh, in_specs=in_specs, out_specs=out_specs, check_vma=False)
```

```python
from functools import partial
import math

import numpy as np
import jax
import jax.numpy as jnp
from jax import lax
from jax.experimental import pallas as pl
from jax.experimental.pallas import tpu as pltpu
from jax.sharding import PartitionSpec as P

G = 128
BLOCKS = 256
PAIRS = 1024
STEP = 4
W_ROWS = 24
GROUPS = 2
FEATURES = 24

fene_k = 30.0
fene_reach = 1.5
bend_k = 2.0
time_step = 0.01
grid_spacing = 4.0

f32 = jnp.float32
bf16 = jnp.bfloat16
VMEM_LIMIT = 24 * 1024 * 1024
PAIR_VMEM = 40 * 1024 * 1024


def dot(a, b):
    return lax.dot_general(a, b, (((1,), (0,)), ((), ())), preferred_element_type=f32)


def dot_t(a, b):
    return lax.dot_general(a, b, (((1,), (1,)), ((), ())), preferred_element_type=f32)


def split2(x):
    hi = x.astype(bf16)
    return hi, (x - hi.astype(f32)).astype(bf16)


def split3(x):
    hi = x.astype(bf16).astype(f32)
    rest = x - hi
    mid = rest.astype(bf16).astype(f32)
    return hi, mid, (rest - mid).astype(bf16).astype(f32)


def dot3(a_hi, a_lo, b_hi, b_lo, form=dot):
    return form(a_hi, b_hi) + form(a_hi, b_lo) + form(a_lo, b_hi)


def split_table(table):
    table = np.asarray(table, np.float64)
    hi = table.astype(np.float32).astype(jnp.bfloat16)
    lo = (table - hi.astype(np.float64)).astype(np.float32).astype(jnp.bfloat16)
    return np.stack([hi, lo])


def tables():
    n = np.arange(G)
    turn = 2.0 * np.pi / G
    member = np.arange(128)
    freq = np.where(member < 64, member + 1, (member - 63) % 64)
    wave = turn * (freq[:, None] * n[None, :] % G)
    even, odd = np.cos(wave), -np.sin(wave)
    special = (member % 64) == 63
    first = (member < 64)[:, None]
    even = np.where(special[:, None], np.cos(wave), even)
    z_xy = np.where(special[:, None] | first, even, odd)
    z_z = np.where(special[:, None] | ~first, even, odd)
    k1, k2 = n // 8, n % 8
    outer = 2.0 * np.pi * (k1[:, None] * k1[None, :] / 16.0 + k2[:, None] * k2[None, :] / 8.0)
    a, b = n // 16, n % 16
    inner = 2.0 * np.pi * (a[:, None] * a[None, :] / 8.0 + b[:, None] * b[None, :] / 16.0)
    twist = turn * (k1[:, None] * a[None, :] + k2[:, None] * b[None, :])
    c_out, s_out, c_in, s_in = np.cos(outer), np.sin(outer), np.cos(inner), np.sin(inner)
    return {
        "z": split_table(np.stack([z_xy, z_z])),
        "outer": split_table(np.concatenate([c_out, -s_out], 0)),
        "outer_back": split_table(np.concatenate([c_out, -s_out], 1)),
        "inner": split_table(np.block([[c_in, -s_in], [s_in, c_in]])),
        "inner_back": split_table(np.block([[c_in, s_in], [-s_in, c_in]])),
        "twist": np.stack([np.cos(twist), np.sin(twist)]).astype(np.float32),
    }


def cost(micros):
    return pl.CostEstimate(flops=int(micros * 1e9), bytes_accessed=1 << 20, transcendentals=0)


def onehot(index, size, width):
    rows = lax.broadcasted_iota(jnp.int32, (size, width), 0)
    return jnp.where(rows == index, 1.0, 0.0).astype(bf16)


def high_part(place):
    return (place >> 7) & 63


def low_part(place):
    return ((place >> 13) << 7) | (place & 127)


WIDTH = 4


def scatter_rows(channels, rows, value_row, place_ref, left_ref, sum_ref):
    group = left_ref.shape[1] // 128
    span = 128 * group

    def turn(g, _):
        low = []
        for j in range(group):
            place = place_ref[pl.ds(g * group + j, 1), :]
            high_hot = onehot(high_part(place), 64, 128)
            low.append(onehot(low_part(place), 256, 128))
            for c in range(channels):
                hi, lo = split2(value_row(c, g * group + j))
                left_ref[c * 128 : c * 128 + 64, j * 128 : (j + 1) * 128] = high_hot * hi
                left_ref[c * 128 + 64 : c * 128 + 128, j * 128 : (j + 1) * 128] = high_hot * lo
        moved = dot_t(left_ref[...], jnp.concatenate(low, axis=1))
        for c in range(channels):
            sum_ref[c * 64 : (c + 1) * 64, :] += (
                moved[c * 128 : c * 128 + 64] + moved[c * 128 + 64 : c * 128 + 128]
            )
        return 0

    sum_ref[...] = jnp.zeros_like(sum_ref)
    lax.fori_loop(0, rows // group, turn, 0)


def unpack_sums(channels, sum_ref, put):
    for c in range(channels):
        for half in range(2):
            put(c, half, sum_ref[c * 64 : (c + 1) * 64, half * 128 : (half + 1) * 128])


def gather_rows(channels, turns, row_at, table_hi_ref, table_lo_ref, place_ref, low, put):
    def build(g, side):
        for n in range(WIDTH):
            place = place_ref[pl.ds(row_at(g, n), 1), :]
            low[side][:, n * 128 : (n + 1) * 128] = onehot(low_part(place), 256, 128)

    def use(g, side):
        found = dot(table_hi_ref[...], low[side][...]) + dot(table_lo_ref[...], low[side][...])
        for n in range(WIDTH):
            high = high_part(place_ref[pl.ds(row_at(g, n), 1), :])
            rows_of = lax.broadcasted_iota(jnp.int32, (64, 128), 0) == high
            for c in range(channels):
                part = found[c * 64 : (c + 1) * 64, n * 128 : (n + 1) * 128]
                put(g, c, n, jnp.sum(jnp.where(rows_of, part, 0.0), axis=0, keepdims=True))

    build(0, 0)

    def turn(h, _):
        build(2 * h + 1, 1)
        use(2 * h, 0)
        build(2 * h + 2, 0)
        use(2 * h + 1, 1)
        return 0

    lax.fori_loop(0, turns // 2 - 1, turn, 0)
    build(turns - 1, 1)
    use(turns - 2, 0)
    use(turns - 1, 1)


def fill_table(c, plane, table_hi_ref, table_lo_ref):
    hi, lo = split2(plane)
    for ref, part in ((table_hi_ref, hi), (table_lo_ref, lo)):
        ref[c * 64 : (c + 1) * 64, 0:128] = part[0:64]
        ref[c * 64 : (c + 1) * 64, 128:256] = part[64:128]


def wrapped(index, size):
    return jnp.where(index >= size, index - size, index)


def for_peers(n_gx, n_gy, do):
    me_x, me_y = lax.axis_index("gx"), lax.axis_index("gy")
    ys = [wrapped(me_y + d, n_gy) for d in range(n_gy)]
    for y in ys[1:]:
        do(me_x, y)

    def turn(d, _):
        x = wrapped(me_x + d, n_gx)
        for y in ys:
            do(x, y)
        return 0

    lax.fori_loop(1, n_gx, turn, 0)


def greet_all(n_gx, n_gy):
    barrier = pltpu.get_barrier_semaphore()

    def greet(x, y):
        pl.semaphore_signal(
            barrier, inc=1, device_id=(x, y), device_id_type=pl.DeviceIdType.MESH
        )

    for_peers(n_gx, n_gy, greet)


def wait_for_all(members):
    pl.semaphore_wait(pltpu.get_barrier_semaphore(), members - 1)


def send_rows(out_ref, in_ref, me, n_gx, n_gy, send_sem, recv_sem):
    def send(x, y):
        pltpu.make_async_remote_copy(
            src_ref=out_ref.at[x * n_gy + y],
            dst_ref=in_ref.at[me],
            send_sem=send_sem,
            recv_sem=recv_sem,
            device_id=(x, y),
            device_id_type=pl.DeviceIdType.MESH,
        ).start()

    for_peers(n_gx, n_gy, send)


def wait_rows(out_ref, in_ref, members, send_sem, recv_sem):
    every = pltpu.make_async_remote_copy(
        src_ref=out_ref.at[pl.ds(0, members - 1)],
        dst_ref=in_ref.at[pl.ds(0, members - 1)],
        send_sem=send_sem,
        recv_sem=recv_sem,
        device_id=(0, 0),
        device_id_type=pl.DeviceIdType.MESH,
    )
    every.wait_send()
    every.wait_recv()


def chain_forces(x):
    lane = lax.broadcasted_iota(jnp.int32, x[0].shape, 1) & 63
    last = lane == 63
    ahead = lambda v: pltpu.roll(v, 127, 1)
    behind = lambda v: pltpu.roll(v, 1, 1)
    bond = [jnp.where(last, 0.5, ahead(v) - v) for v in x]
    square = bond[0] * bond[0] + bond[1] * bond[1] + bond[2] * bond[2]
    inverse = lax.rsqrt(square)
    unit = [v * inverse for v in bond]
    following = [ahead(v) for v in unit]
    cosine = unit[0] * following[0] + unit[1] * following[1] + unit[2] * following[2]
    bends = lane < 62
    stretch = fene_k / (1.0 - square / fene_reach**2)
    before = behind(jnp.where(bends, 1.0, 0.0))
    cosine_before = behind(cosine)
    grad = []
    for c in range(3):
        pull = jnp.where(bends, following[c] - cosine * unit[c], 0.0)
        push = before * (behind(unit[c]) - cosine_before * unit[c])
        push = jnp.where(lane == 0, 0.0, push)
        grad.append(
            jnp.where(last, 0.0, stretch * bond[c] - bend_k * inverse * (pull + push))
        )
    return [g - jnp.where(lane == 0, 0.0, behind(g)) for g in grad]


def send_kernel(
    members, n_gx, n_gy, pos_ref, route_ref, in_ref, out_ref, plane_ref, left_ref, sum_ref, send_sem,
    recv_sem,
):
    me = lax.axis_index("gx") * n_gy + lax.axis_index("gy")
    greet_all(n_gx, n_gy)
    rows = route_ref.shape[0]
    for c in range(3):
        for r in range(rows):
            plane_ref[c, r : r + 1, :] = pos_ref[c : c + 1, r * 128 : (r + 1) * 128]
    forces = chain_forces([plane_ref[c] for c in range(3)])
    for c in range(3):
        plane_ref[3 + c] = forces[c]
    scatter_rows(
        6, rows, lambda c, r: plane_ref[c, pl.ds(r, 1), :], route_ref, left_ref, sum_ref
    )
    for c in range(6):
        out_ref[0:64, c, :] = sum_ref[c * 64 : (c + 1) * 64, 0:128]
        out_ref[64:128, c, :] = sum_ref[c * 64 : (c + 1) * 64, 128:256]
    wait_for_all(members)

    send_rows(out_ref, in_ref, me, n_gx, n_gy, send_sem, recv_sem)
    in_ref[me] = out_ref[me]
    wait_rows(out_ref, in_ref, members, send_sem, recv_sem)


def vmem(n):
    return [pl.BlockSpec(memory_space=pltpu.VMEM)] * n


def send_message(positions, route):
    n_gx, n_gy = lax.axis_size("gx"), lax.axis_size("gy")
    members = n_gx * n_gy
    return pl.pallas_call(
        partial(send_kernel, members, n_gx, n_gy),
        out_shape=jax.ShapeDtypeStruct((128, 6, 128), f32),
        in_specs=vmem(2),
        out_specs=pl.BlockSpec(memory_space=pltpu.VMEM),
        scratch_shapes=[
            pltpu.VMEM((128, 6, 128), f32),
            pltpu.VMEM((6, 64, 128), f32),
            pltpu.VMEM((768, 1024), bf16),
            pltpu.VMEM((384, 256), f32),
            pltpu.SemaphoreType.DMA,
            pltpu.SemaphoreType.DMA,
        ],
        compiler_params=pltpu.CompilerParams(
            vmem_limit_bytes=VMEM_LIMIT, collective_id=1, has_side_effects=True
        ),
        name="send",
    )(positions, route)


def place_kernel(
    members, n_gx, n_gy, part_ref, in_ref, order_ref, z_ref, outer_ref, outer_back_ref, inner_ref,
    inner_back_ref, twist_ref, grid_ref, beside_ref, flow_ref, left_ref, sum_ref, spec_ref,
    spec_in_ref, mid_ref, spec_send, spec_recv, side_send, side_recv,
):
    g_x = lax.axis_index("gx")
    me = g_x * n_gy + lax.axis_index("gy")
    greet_all(n_gx, n_gy)
    scatter_rows(
        6, members, lambda c, r: in_ref[r, c : c + 1, :], order_ref, left_ref, sum_ref
    )

    def to_grid(c, half, value):
        grid_ref[c, half * 64 : (half + 1) * 64, :] = value

    unpack_sums(6, sum_ref, to_grid)
    for c in range(3):
        hi, lo = split2(grid_ref[3 + c])
        kind = 0 if c < 2 else 1
        spec_ref[:, c, :] = dot3(z_ref[0, kind], z_ref[1, kind], hi, lo, dot_t)
    wait_for_all(members)
    side = pltpu.make_async_remote_copy(
        src_ref=grid_ref,
        dst_ref=beside_ref,
        send_sem=side_send,
        recv_sem=side_recv,
        device_id=(wrapped(g_x + n_gx - 1, n_gx), lax.axis_index("gy")),
        device_id_type=pl.DeviceIdType.MESH,
    )

    send_rows(spec_ref, spec_in_ref, me, n_gx, n_gy, spec_send, spec_recv)
    side.start()
    spec_in_ref[me] = spec_ref[me]
    wait_rows(spec_ref, spec_in_ref, members, spec_send, spec_recv)
    wave_part(
        part_ref, spec_in_ref, outer_ref, outer_back_ref, inner_ref, inner_back_ref, twist_ref,
        flow_ref, mid_ref,
    )
    side.wait()


def place_on_grid(incoming, order, table, member):
    n_gx, n_gy = lax.axis_size("gx"), lax.axis_size("gy")
    members = n_gx * n_gy
    return pl.pallas_call(
        partial(place_kernel, members, n_gx, n_gy),
        out_shape=[
            jax.ShapeDtypeStruct((6, 128, 128), f32),
            jax.ShapeDtypeStruct((6, 128, 128), f32),
            jax.ShapeDtypeStruct((128, 3, 128), f32),
        ],
        in_specs=[pl.BlockSpec(memory_space=pltpu.SMEM)] + vmem(8),
        out_specs=vmem(3),
        scratch_shapes=[
            pltpu.VMEM((768, 1024), bf16),
            pltpu.VMEM((384, 256), f32),
            pltpu.VMEM((128, 3, 128), f32),
            pltpu.VMEM((128, 3, 128), f32),
            pltpu.VMEM((128, 256), f32),
            pltpu.SemaphoreType.DMA,
            pltpu.SemaphoreType.DMA,
            pltpu.SemaphoreType.DMA,
            pltpu.SemaphoreType.DMA,
        ],
        compiler_params=pltpu.CompilerParams(
            vmem_limit_bytes=VMEM_LIMIT, collective_id=3, has_side_effects=True
        ),
        name="place",
    )(
        frequency_part(member), incoming, order, table["z"], table["outer"],
        table["outer_back"], table["inner"], table["inner_back"], table["twist"],
    )


def wave_part(
    part_ref, in_ref, outer_ref, outer_back_ref, inner_ref, inner_back_ref, twist_ref,
    out_ref, mid_ref,
):
    freq, turn_re, turn_im, weight = (part_ref[i] for i in range(4))
    cos_t, sin_t = twist_ref[0], twist_ref[1]
    spectrum = []
    for c in range(3):
        hi, lo = split2(in_ref[:, c, :])
        both = dot3(outer_ref[0], outer_ref[1], hi, lo)
        re, im = both[0:128], both[128:256]
        mid_ref[:, 0:128] = re * cos_t + im * sin_t
        mid_ref[:, 128:256] = im * cos_t - re * sin_t
        hi, lo = split2(mid_ref[...])
        both = dot3(hi, lo, inner_ref[0], inner_ref[1])
        spectrum.append((both[:, 0:128], both[:, 128:256]))
    row = lax.broadcasted_iota(jnp.int32, (128, 128), 0)
    col = lax.broadcasted_iota(jnp.int32, (128, 128), 1)
    n_x = (row >> 3) + 16 * (col >> 4)
    n_y = (row & 7) + 8 * (col & 15)
    unit = 2.0 * math.pi / (G * grid_spacing)
    signed = lambda n: jnp.where(n < G // 2, n, n - G).astype(f32) * unit
    k_x, k_y = signed(n_x), signed(n_y)
    k_z = jnp.full((128, 128), freq * unit, f32)
    edge_x = jnp.where(n_x == G // 2, 1.0, 0.0)
    edge_y = jnp.where(n_y == G // 2, 1.0, 0.0)
    edge_z = jnp.where(jnp.full((128, 128), freq, f32) < -63.5, 1.0, 0.0)
    square = k_x * k_x + k_y * k_y + k_z * k_z
    positive = square > 0.0
    safe = jnp.where(positive, square, 1.0)
    green = jnp.where(
        positive,
        (1.0 - 0.25 * square / 3.0) * (1.0 + square) * jnp.exp(-square) / safe,
        0.0,
    ) * (weight / float(G**3))
    over = green / safe
    g_xy = jnp.where(edge_x == edge_y, -over * k_x * k_y, 0.0)
    g_xz = jnp.where(edge_x == edge_z, -over * k_x * k_z, 0.0)
    g_yz = jnp.where(edge_y == edge_z, -over * k_y * k_z, 0.0)
    g_xx = green - over * k_x * k_x
    g_yy = green - over * k_y * k_y
    g_zz = green - over * k_z * k_z
    (x_re, x_im), (y_re, y_im), (z_re, z_im) = spectrum
    z_re, z_im = turn_re * z_re - turn_im * z_im, turn_re * z_im + turn_im * z_re
    flow = [
        (g_xx * x_re + g_xy * y_re + g_xz * z_re, g_xx * x_im + g_xy * y_im + g_xz * z_im),
        (g_xy * x_re + g_yy * y_re + g_yz * z_re, g_xy * x_im + g_yy * y_im + g_yz * z_im),
    ]
    w_re = g_xz * x_re + g_yz * y_re + g_zz * z_re
    w_im = g_xz * x_im + g_yz * y_im + g_zz * z_im
    flow.append((turn_re * w_re + turn_im * w_im, turn_re * w_im - turn_im * w_re))
    for c in range(3):
        mid_ref[:, 0:128], mid_ref[:, 128:256] = flow[c]
        hi, lo = split2(mid_ref[...])
        both = dot3(hi, lo, inner_back_ref[0], inner_back_ref[1])
        re, im = both[:, 0:128], both[:, 128:256]
        hi, lo = split2(
            jnp.concatenate([re * cos_t - im * sin_t, im * cos_t + re * sin_t], axis=0)
        )
        out_ref[:, c, :] = dot3(outer_back_ref[0], outer_back_ref[1], hi, lo)


def frequency_part(member):
    special = member % 64 == 63
    freq = jnp.where(member < 64, member + 1, (member - 63) % 64)
    freq = jnp.where(member == 63, -64, freq)
    side = jnp.where(member < 64, 1.0, -1.0)
    return jnp.stack(
        [
            freq.astype(f32),
            jnp.where(special, 1.0, 0.0),
            jnp.where(special, 0.0, side),
            jnp.where(special, 1.0, 2.0),
        ]
    ).astype(f32)


ERFC_SHIFT = 4.0
ERFC_POLY = (
    -5.9986000529477224e-05, 1.1337793270330845, 4.308175452878655, 20.093023854033866,
    -8.594175483206275, 489.91788674098177, -1701.7584635921016, 1704.126720738659,
)


def pair_scalars(s2):
    u = lax.rsqrt(s2)
    gauss = jnp.exp2(s2 * (-0.25 * math.log2(math.e)))
    t = pl.reciprocal(s2 * u + ERFC_SHIFT, approx=True)
    w = ERFC_POLY[-1]
    for coefficient in ERFC_POLY[-2::-1]:
        w = w * t + coefficient
    u2 = u * u
    wu = w * u
    along = gauss * (wu * (0.0625 * u2 + 0.375) + 0.125)
    across = (gauss * u2) * (wu * (0.375 - 0.1875 * u2) - 0.125)
    return along, across


def both_halves(v):
    low_half = lax.broadcasted_iota(jnp.int32, (1, 128), 1) < 64
    other = pltpu.roll(v, 64, 1)
    return jnp.where(low_half, v, other), jnp.where(low_half, other, v)


def stage_nodes(ref, weight_stage, right_stage):
    x = [ref[c] for c in range(3)]
    f = [ref[3 + c] for c in range(3)]
    xf = x[0] * f[0] + x[1] * f[1] + x[2] * f[2]
    rows = f + [xf]
    rows += [x[a] * f[b] for a in range(3) for b in range(3)]
    rows += [x[a] * xf for a in range(3)]
    for c, plane in enumerate(rows):
        weight_stage[pl.ds(c, 128, stride=16), :] = plane
    norm = x[0] * x[0] + x[1] * x[1] + x[2] * x[2]
    first, second = [], []
    for h, m, l in [split3(v) for v in x]:
        first += [h, h, m, m, h, l]
        second += [h, m, h, m, l, h]
    one = jnp.ones((128, 128), f32)
    first = [-2.0 * v for v in first] + list(split3(norm)) + [one] * 3
    second += [one] * 3 + list(split3(norm + 0.25))
    for c, plane in enumerate(second):
        right_stage[pl.ds(c, 128, stride=FEATURES), :] = plane
    return first


def build_tables(base, weight_stage, right_stage, weight_ref, right_ref):
    blank = jnp.zeros((32 - FEATURES, 128), f32)

    def build(r, _):
        w = weight_stage[pl.ds(pl.multiple_of(r * 16, 8), 16), :]
        for k, v in enumerate(both_halves(w)):
            hi = v.astype(bf16)
            lo = (v - hi.astype(f32)).astype(bf16)
            weight_ref[base + 2 * r + k] = jnp.concatenate([hi, lo], axis=0)
        w = right_stage[pl.ds(pl.multiple_of(r * FEATURES, 8), FEATURES), :]
        for k, v in enumerate(both_halves(w)):
            right_ref[base + 2 * r + k] = jnp.concatenate([v, blank], axis=0).astype(bf16)
        return 0

    lax.fori_loop(0, 128, build, 0, unroll=16)


def build_left(first, left_stage, left_ref):
    for c, plane in enumerate(first):
        left_stage[pl.ds(c, 128, stride=FEATURES), :] = plane
    eye = jnp.where(
        lax.broadcasted_iota(jnp.int32, (128, 128), 0)
        == lax.broadcasted_iota(jnp.int32, (128, 128), 1),
        1.0,
        0.0,
    ).astype(bf16)
    blank = jnp.zeros((32 - FEATURES, 128), f32)

    def turn_left(r, _):
        v = left_stage[pl.ds(pl.multiple_of(r * FEATURES, 8), FEATURES), :]
        v = jnp.concatenate([v, blank], axis=0).astype(bf16)
        nodes = dot_t(eye, jnp.concatenate([v] * 4, axis=0)).astype(bf16)
        left_ref[2 * r] = nodes[0:64]
        left_ref[2 * r + 1] = nodes[64:128]
        return 0

    lax.fori_loop(0, 128, turn_left, 0, unroll=8)


def pair_kernel(
    list_ref, count_ref, own_ref, beside_ref, own_vel_ref, far_vel_ref,
    weight_ref, right_ref, left_ref, weight_stage, right_stage, left_stage,
    near_acc, far_acc, s2_a, s2_b, tile_a, tile_b,
):
    first = stage_nodes(own_ref, weight_stage, right_stage)
    build_left(first, left_stage, left_ref)
    build_tables(0, weight_stage, right_stage, weight_ref, right_ref)
    stage_nodes(beside_ref, weight_stage, right_stage)
    build_tables(BLOCKS, weight_stage, right_stage, weight_ref, right_ref)

    lane = lax.broadcasted_iota(jnp.int32, (1, 128), 1)
    low_half = lane < 64
    count = count_ref[0]

    def clear(r, _):
        blank = jnp.zeros((W_ROWS, 128), f32)
        far_acc[pl.ds(pl.multiple_of(r * 2 * W_ROWS, 8), W_ROWS), :] = blank
        far_acc[pl.ds(pl.multiple_of(r * 2 * W_ROWS + W_ROWS, 8), W_ROWS), :] = blank
        near_acc[pl.ds(pl.multiple_of(r * W_ROWS, 8), W_ROWS), :] = blank
        return 0

    lax.fori_loop(0, BLOCKS, clear, 0, unroll=8)

    wide = lax.broadcasted_iota(jnp.int32, (64, 128), 1)
    wide_low = wide < 64
    wide_even = (wide & 32) == 0
    narrow = lax.broadcasted_iota(jnp.int32, (32, 128), 1) < 64
    nothing = jnp.zeros((32, 128), bf16)

    def half_of(v, half):
        return jnp.where(narrow, nothing, v) if half else jnp.where(narrow, v, nothing)

    half_keep = [(lane >> 6) == s for s in range(2)]
    blank = jnp.zeros((64, 128), bf16)

    def blocks_of(pair):
        return list_ref[0, pair], list_ref[1, pair]

    def distance_dots(step):
        found = []
        for g in range(GROUPS):
            pairs = [blocks_of((step * GROUPS + g) * STEP + s) for s in range(STEP)]
            left = [left_ref[pairs[s][0]] for s in range(STEP)]
            left = jnp.where(
                wide_low,
                jnp.where(wide_even, left[0], left[1]),
                jnp.where(wide_even, left[2], left[3]),
            )
            right = [half_of(right_ref[pairs[s][1]], s % 2) for s in range(STEP)]
            right = jnp.concatenate(
                [
                    jnp.concatenate([right[0], right[1], blank], axis=0),
                    jnp.concatenate([blank, right[2], right[3]], axis=0),
                ],
                axis=1,
            )
            found.append(dot(left, right))
        return found

    def scalars(s2_ref, tile_ref, pack):
        half = pack % 2
        along, across = pair_scalars(s2_ref[pack // 2, :, half * 128 : (half + 1) * 128])
        for at, value in ((0, across), (128, along)):
            hi, lo = split2(value)
            tile_ref[pack, at : at + 64, :] = hi
            tile_ref[pack, at + 64 : at + 128, :] = lo

    def sum_dots(step, tile_ref, pack):
        tile = tile_ref[pack]
        pairs = [blocks_of((step * 2 * GROUPS + pack) * 2 + s) for s in range(2)]
        a = jnp.concatenate([weight_ref[i] for i, _ in pairs], axis=0)
        b = jnp.concatenate(
            [half_of(weight_ref[j], s) for s, (_, j) in enumerate(pairs)], axis=0
        )
        to_far = dot(a, jnp.concatenate([tile[0:128], tile[128:256]], axis=1))
        return dot_t(b, tile), to_far

    def add_sums(step, pack, to_near, to_far):
        for s in range(2):
            number = (step * 2 * GROUPS + pack) * 2 + s
            for out, acc_ref, row, keep in (
                (to_near, near_acc, list_ref[2, number], None),
                (to_far, far_acc, list_ref[3, number], half_keep[s]),
            ):
                top = 32 * s
                add_h = out[top : top + 16, 0:128] + out[top + 16 : top + 32, 0:128]
                add_f = out[top : top + 8, 128:256] + out[top + 16 : top + 24, 128:256]
                add = jnp.concatenate([add_h, add_f], axis=0)
                if keep is not None:
                    add = jnp.where(keep, add, 0.0)
                acc_ref[pl.ds(pl.multiple_of(row, 8), W_ROWS), :] += add

    packs = range(2 * GROUPS)

    def keep_distances(found, s2_ref):
        for g in range(GROUPS):
            s2_ref[g] = found[g]

    def stage(k, s2_next, s2_now, tile_now, tile_last):
        for pack in packs:
            scalars(s2_now, tile_now, pack)
        for pack in packs:
            add_sums(k - 1, pack, *sum_dots(k - 1, tile_last, pack))
        keep_distances(distance_dots(k + 1), s2_next)

    steps = (count + (STEP * GROUPS - 1)) // (STEP * GROUPS)
    keep_distances(distance_dots(0), s2_a)
    for pack in packs:
        scalars(s2_a, tile_a, pack)
    keep_distances(distance_dots(1), s2_b)

    def body(j, _):
        k = 2 * j + 1
        stage(k, s2_a, s2_b, tile_b, tile_a)
        stage(k + 1, s2_b, s2_a, tile_a, tile_b)
        return 0

    lax.fori_loop(0, (steps + 1) // 2, body, 0)

    chunk = 32
    for side, ref, out_ref in ((0, own_ref, own_vel_ref), (1, beside_ref, far_vel_ref)):
        for top in range(0, 128, chunk):
            planes = []
            for c in range(19):
                at = (2 * top) * W_ROWS + c
                even = far_acc[pl.ds(side * BLOCKS * W_ROWS + at, chunk, stride=2 * W_ROWS), :]
                at += W_ROWS
                odd = far_acc[pl.ds(side * BLOCKS * W_ROWS + at, chunk, stride=2 * W_ROWS), :]
                if side == 0:
                    even += near_acc[pl.ds(at - W_ROWS, chunk, stride=2 * W_ROWS), :]
                    odd += near_acc[pl.ds(at, chunk, stride=2 * W_ROWS), :]
                even = even + pltpu.roll(even, 64, 1)
                odd = odd + pltpu.roll(odd, 64, 1)
                planes.append(jnp.where(low_half, even, odd))
            x = [ref[c, top : top + chunk, :] for c in range(3)]
            h_f, h_xf, h_x_f, h_x_xf, along = (
                planes[0:3], planes[3], planes[4:13], planes[13:16], planes[16:19],
            )
            x_h_f = x[0] * h_f[0] + x[1] * h_f[1] + x[2] * h_f[2] - h_xf
            for c in range(3):
                out_ref[c, top : top + chunk, :] = (
                    along[c]
                    + x[c] * x_h_f
                    - (x[0] * h_x_f[3 * c] + x[1] * h_x_f[3 * c + 1] + x[2] * h_x_f[3 * c + 2])
                    + h_x_xf[c]
                )


def pair_lists(first_list, second_list, count):
    live = jnp.arange(PAIRS, dtype=jnp.int32) < count
    lists = jnp.stack(
        [
            first_list,
            second_list,
            jnp.where(live, first_list, BLOCKS) * W_ROWS,
            jnp.where(live & (first_list != second_list), second_list, 2 * BLOCKS) * W_ROWS,
        ]
    )
    spare = jnp.array([0, 0, BLOCKS * W_ROWS, 2 * BLOCKS * W_ROWS], jnp.int32)
    return jnp.concatenate([lists, jnp.broadcast_to(spare[:, None], (4, 128))], axis=1)


def pair_velocities(own, beside, lists, count):
    plane = jax.ShapeDtypeStruct((3, 128, 128), f32)
    return pl.pallas_call(
        pair_kernel,
        out_shape=[plane, plane],
        in_specs=[pl.BlockSpec(memory_space=pltpu.SMEM)] * 2 + vmem(2),
        out_specs=vmem(2),
        scratch_shapes=[
            pltpu.VMEM((2 * BLOCKS, 32, 128), bf16),
            pltpu.VMEM((2 * BLOCKS, 32, 128), bf16),
            pltpu.VMEM((BLOCKS, 64, 128), bf16),
            pltpu.VMEM((128 * 16, 128), f32),
            pltpu.VMEM((128 * FEATURES, 128), f32),
            pltpu.VMEM((128 * FEATURES, 128), f32),
            pltpu.VMEM(((BLOCKS + 1) * W_ROWS, 128), f32),
            pltpu.VMEM(((2 * BLOCKS + 1) * W_ROWS, 128), f32),
            pltpu.VMEM((GROUPS, 64, 256), f32),
            pltpu.VMEM((GROUPS, 64, 256), f32),
            pltpu.VMEM((2 * GROUPS, 256, 128), bf16),
            pltpu.VMEM((2 * GROUPS, 256, 128), bf16),
        ],
        compiler_params=pltpu.CompilerParams(vmem_limit_bytes=PAIR_VMEM),
        cost_estimate=cost(50),
        name="pairs",
    )(lists, count, own, beside)


def reply_kernel(
    members, n_gx, n_gy, own_ref, far_ref, flow_ref, order_ref, z_ref, in_ref, out_ref,
    wave_ref, beside_ref, hi_ref, lo_ref, low_a, low_b, send_sem, recv_sem, far_send, far_recv,
    wave_send, wave_recv,
):
    g_x = lax.axis_index("gx")
    me = g_x * n_gy + lax.axis_index("gy")
    greet_all(n_gx, n_gy)
    wait_for_all(members)
    far = pltpu.make_async_remote_copy(
        src_ref=far_ref,
        dst_ref=beside_ref,
        send_sem=far_send,
        recv_sem=far_recv,
        device_id=(wrapped(g_x + 1, n_gx), lax.axis_index("gy")),
        device_id_type=pl.DeviceIdType.MESH,
    )
    far.start()
    send_rows(flow_ref, wave_ref, me, n_gx, n_gy, wave_send, wave_recv)
    wave_ref[me] = flow_ref[me]
    far.wait()
    wait_rows(flow_ref, wave_ref, members, wave_send, wave_recv)
    for c in range(3):
        kind = 0 if c < 2 else 1
        hi, lo = split2(jnp.transpose(wave_ref[:, c, :]))
        wave = dot3(hi, lo, z_ref[0, kind], z_ref[1, kind])
        fill_table(c, own_ref[c] + beside_ref[c] + wave, hi_ref, lo_ref)

    def row_at(g, n):
        return g * WIDTH + n

    def put(g, c, n, row):
        out_ref[row_at(g, n), c : c + 1, :] = row

    gather_rows(
        3, members // WIDTH, row_at, hi_ref, lo_ref, order_ref, (low_a, low_b), put
    )

    send_rows(out_ref, in_ref, me, n_gx, n_gy, send_sem, recv_sem)
    in_ref[me] = out_ref[me]
    wait_rows(out_ref, in_ref, members, send_sem, recv_sem)


def reply_message(own_vel, far_vel, wave, order, z_table):
    n_gx, n_gy = lax.axis_size("gx"), lax.axis_size("gy")
    members = n_gx * n_gy
    return pl.pallas_call(
        partial(reply_kernel, members, n_gx, n_gy),
        out_shape=jax.ShapeDtypeStruct((128, 3, 128), f32),
        in_specs=vmem(5),
        out_specs=pl.BlockSpec(memory_space=pltpu.VMEM),
        scratch_shapes=[
            pltpu.VMEM((128, 3, 128), f32),
            pltpu.VMEM((128, 3, 128), f32),
            pltpu.VMEM((3, 128, 128), f32),
            pltpu.VMEM((192, 256), bf16),
            pltpu.VMEM((192, 256), bf16),
            pltpu.VMEM((256, WIDTH * 128), bf16),
            pltpu.VMEM((256, WIDTH * 128), bf16),
            pltpu.SemaphoreType.DMA,
            pltpu.SemaphoreType.DMA,
            pltpu.SemaphoreType.DMA,
            pltpu.SemaphoreType.DMA,
            pltpu.SemaphoreType.DMA,
            pltpu.SemaphoreType.DMA,
        ],
        compiler_params=pltpu.CompilerParams(
            vmem_limit_bytes=VMEM_LIMIT, collective_id=2, has_side_effects=True
        ),
        name="reply",
    )(own_vel, far_vel, wave, order, z_table)


def move_kernel(
    in_ref, route_ref, pos_ref, noise_ref, moved_ref, drift_ref, hi_ref, lo_ref, vel_ref, low_a,
    low_b,
):
    rows = route_ref.shape[0]
    for c in range(3):
        fill_table(c, in_ref[:, c, :], hi_ref, lo_ref)

    def row_at(g, n):
        return g * WIDTH + n

    def put(g, c, n, row):
        vel_ref[c, pl.ds(row_at(g, n), 1), :] = row

    gather_rows(3, rows // WIDTH, row_at, hi_ref, lo_ref, route_ref, (low_a, low_b), put)
    for c in range(3):
        for r in range(rows):
            drift_ref[c : c + 1, r * 128 : (r + 1) * 128] = time_step * vel_ref[c, r : r + 1, :]
    moved_ref[...] = pos_ref[...] + drift_ref[...] + noise_ref[...]


def move_beads(arrived, route, positions, noise):
    flat = jax.ShapeDtypeStruct(positions.shape, f32)
    return pl.pallas_call(
        move_kernel,
        out_shape=[flat, flat],
        in_specs=vmem(4),
        out_specs=vmem(2),
        scratch_shapes=[
            pltpu.VMEM((192, 256), bf16),
            pltpu.VMEM((192, 256), bf16),
            pltpu.VMEM((3, 64, 128), f32),
            pltpu.VMEM((256, WIDTH * 128), bf16),
            pltpu.VMEM((256, WIDTH * 128), bf16),
        ],
        compiler_params=pltpu.CompilerParams(vmem_limit_bytes=VMEM_LIMIT),
        name="move",
    )(arrived, route, positions, noise)


def shards(positions, noise, route, node_perm, pair_first, pair_second, pair_count):
    table = {name: jnp.asarray(value) for name, value in tables().items()}
    row_gx = lax.axis_index("gx")
    member = row_gx * lax.axis_size("gy") + lax.axis_index("gy")
    route = route.reshape(64, 128)
    order = lax.dynamic_index_in_dim(node_perm, row_gx, 0, keepdims=False).reshape(128, 128)
    incoming = send_message(positions, route)
    grid, beside, wave = place_on_grid(incoming, order, table, member)
    lists = pair_lists(pair_first[0], pair_second[0], pair_count[0])
    own_vel, far_vel = pair_velocities(grid, beside, lists, pair_count)
    reply = reply_message(own_vel, far_vel, wave, order, table["z"])
    return tuple(move_beads(reply, route, positions, noise))


def solution(mesh):
    in_specs = (
        P(None, ("gx", "gy")),
        P(None, ("gx", "gy")),
        P(("gx", "gy")),
        P(None, "gy", None),
        P(("gx", "gy"), None),
        P(("gx", "gy"), None),
        P(("gx", "gy")),
    )
    out_specs = (P(None, ("gx", "gy")), P(None, ("gx", "gy")))
    return jax.shard_map(shards, mesh=mesh, in_specs=in_specs, out_specs=out_specs, check_vma=False)
```

```python
from functools import partial
import math

import numpy as np
import jax
import jax.numpy as jnp
from jax import lax
from jax.experimental import pallas as pl
from jax.experimental.pallas import tpu as pltpu
from jax.sharding import PartitionSpec as P

G = 128
BLOCKS = 256
PAIRS = 1024
STEP = 4
W_ROWS = 24
GROUPS = 2
FEATURES = 24

fene_k = 30.0
fene_reach = 1.5
bend_k = 2.0
time_step = 0.01
grid_spacing = 4.0

f32 = jnp.float32
bf16 = jnp.bfloat16
VMEM_LIMIT = 24 * 1024 * 1024
PAIR_VMEM = 40 * 1024 * 1024


def dot(a, b):
    return lax.dot_general(a, b, (((1,), (0,)), ((), ())), preferred_element_type=f32)


def dot_t(a, b):
    return lax.dot_general(a, b, (((1,), (1,)), ((), ())), preferred_element_type=f32)


def split2(x):
    hi = x.astype(bf16)
    return hi, (x - hi.astype(f32)).astype(bf16)


def split3(x):
    hi = x.astype(bf16).astype(f32)
    rest = x - hi
    mid = rest.astype(bf16).astype(f32)
    return hi, mid, (rest - mid).astype(bf16).astype(f32)


def dot3(a_hi, a_lo, b_hi, b_lo, form=dot):
    return form(a_hi, b_hi) + form(a_hi, b_lo) + form(a_lo, b_hi)


def split_table(table):
    table = np.asarray(table, np.float64)
    hi = table.astype(np.float32).astype(jnp.bfloat16)
    lo = (table - hi.astype(np.float64)).astype(np.float32).astype(jnp.bfloat16)
    return np.stack([hi, lo])


def tables():
    n = np.arange(G)
    turn = 2.0 * np.pi / G
    member = np.arange(128)
    freq = np.where(member < 64, member + 1, (member - 63) % 64)
    wave = turn * (freq[:, None] * n[None, :] % G)
    even, odd = np.cos(wave), -np.sin(wave)
    special = (member % 64) == 63
    first = (member < 64)[:, None]
    even = np.where(special[:, None], np.cos(wave), even)
    z_xy = np.where(special[:, None] | first, even, odd)
    z_z = np.where(special[:, None] | ~first, even, odd)
    k1, k2 = n // 8, n % 8
    outer = 2.0 * np.pi * (k1[:, None] * k1[None, :] / 16.0 + k2[:, None] * k2[None, :] / 8.0)
    a, b = n // 16, n % 16
    inner = 2.0 * np.pi * (a[:, None] * a[None, :] / 8.0 + b[:, None] * b[None, :] / 16.0)
    twist = turn * (k1[:, None] * a[None, :] + k2[:, None] * b[None, :])
    c_out, s_out, c_in, s_in = np.cos(outer), np.sin(outer), np.cos(inner), np.sin(inner)
    inner = np.block([[c_in, -s_in], [s_in, c_in]])
    inner_back = np.block([[c_in, s_in], [-s_in, c_in]])
    outer_and_z = np.block([[c_out, z_xy], [-s_out, z_z]])
    outer_back = np.concatenate([c_out, -s_out], 1)
    return {
        "z": split_table(np.stack([z_xy, z_z])),
        "all": split_table(np.concatenate([inner, inner_back, outer_and_z, outer_back], 0)),
        "twist": np.stack([np.cos(twist), np.sin(twist)]).astype(np.float32),
    }


def cost(micros):
    return pl.CostEstimate(flops=int(micros * 1e9), bytes_accessed=1 << 20, transcendentals=0)


def onehot(index, size, width):
    rows = lax.broadcasted_iota(jnp.int32, (size, width), 0)
    return jnp.where(rows == index, 1.0, 0.0).astype(bf16)


def high_part(place):
    return (place >> 7) & 63


def low_part(place):
    return ((place >> 13) << 7) | (place & 127)


WIDTH = 4


def scatter_rows(channels, rows, value_row, place_ref, left_ref, sum_ref):
    group = left_ref.shape[1] // 128
    span = 128 * group

    def turn(g, _):
        low = []
        for j in range(group):
            place = place_ref[pl.ds(g * group + j, 1), :]
            high_hot = onehot(high_part(place), 64, 128)
            low.append(onehot(low_part(place), 256, 128))
            for c in range(channels):
                hi, lo = split2(value_row(c, g * group + j))
                left_ref[c * 128 : c * 128 + 64, j * 128 : (j + 1) * 128] = high_hot * hi
                left_ref[c * 128 + 64 : c * 128 + 128, j * 128 : (j + 1) * 128] = high_hot * lo
        moved = dot_t(left_ref[...], jnp.concatenate(low, axis=1))
        for c in range(channels):
            sum_ref[c * 64 : (c + 1) * 64, :] += (
                moved[c * 128 : c * 128 + 64] + moved[c * 128 + 64 : c * 128 + 128]
            )
        return 0

    sum_ref[...] = jnp.zeros_like(sum_ref)
    lax.fori_loop(0, rows // group, turn, 0)


def unpack_sums(channels, sum_ref, put):
    for c in range(channels):
        for half in range(2):
            put(c, half, sum_ref[c * 64 : (c + 1) * 64, half * 128 : (half + 1) * 128])


def gather_rows(channels, turns, row_at, table_hi_ref, table_lo_ref, place_ref, low, put):
    def build(g, side):
        for n in range(WIDTH):
            place = place_ref[pl.ds(row_at(g, n), 1), :]
            low[side][:, n * 128 : (n + 1) * 128] = onehot(low_part(place), 256, 128)

    def use(g, side):
        found = dot(table_hi_ref[...], low[side][...]) + dot(table_lo_ref[...], low[side][...])
        for n in range(WIDTH):
            high = high_part(place_ref[pl.ds(row_at(g, n), 1), :])
            rows_of = lax.broadcasted_iota(jnp.int32, (64, 128), 0) == high
            for c in range(channels):
                part = found[c * 64 : (c + 1) * 64, n * 128 : (n + 1) * 128]
                put(g, c, n, jnp.sum(jnp.where(rows_of, part, 0.0), axis=0, keepdims=True))

    build(0, 0)

    def turn(h, _):
        build(2 * h + 1, 1)
        use(2 * h, 0)
        build(2 * h + 2, 0)
        use(2 * h + 1, 1)
        return 0

    lax.fori_loop(0, turns // 2 - 1, turn, 0)
    build(turns - 1, 1)
    use(turns - 2, 0)
    use(turns - 1, 1)


def fill_table(c, plane, table_hi_ref, table_lo_ref):
    hi, lo = split2(plane)
    for ref, part in ((table_hi_ref, hi), (table_lo_ref, lo)):
        ref[c * 64 : (c + 1) * 64, 0:128] = part[0:64]
        ref[c * 64 : (c + 1) * 64, 128:256] = part[64:128]


def wrapped(index, size):
    return jnp.where(index >= size, index - size, index)


def for_peers(n_gx, n_gy, do):
    me_x, me_y = lax.axis_index("gx"), lax.axis_index("gy")
    ys = [wrapped(me_y + d, n_gy) for d in range(n_gy)]
    for y in ys[1:]:
        do(me_x, y)

    def turn(d, _):
        x = wrapped(me_x + d, n_gx)
        for y in ys:
            do(x, y)
        return 0

    lax.fori_loop(1, n_gx, turn, 0)


def greet_all(n_gx, n_gy):
    barrier = pltpu.get_barrier_semaphore()

    def greet(x, y):
        pl.semaphore_signal(
            barrier, inc=1, device_id=(x, y), device_id_type=pl.DeviceIdType.MESH
        )

    for_peers(n_gx, n_gy, greet)


def wait_for_all(members):
    pl.semaphore_wait(pltpu.get_barrier_semaphore(), members - 1)


def send_rows(out_ref, in_ref, me, n_gx, n_gy, send_sem, recv_sem):
    def send(x, y):
        pltpu.make_async_remote_copy(
            src_ref=out_ref.at[x * n_gy + y],
            dst_ref=in_ref.at[me],
            send_sem=send_sem,
            recv_sem=recv_sem,
            device_id=(x, y),
            device_id_type=pl.DeviceIdType.MESH,
        ).start()

    for_peers(n_gx, n_gy, send)


def wait_rows(out_ref, in_ref, members, send_sem, recv_sem):
    every = pltpu.make_async_remote_copy(
        src_ref=out_ref.at[pl.ds(0, members - 1)],
        dst_ref=in_ref.at[pl.ds(0, members - 1)],
        send_sem=send_sem,
        recv_sem=recv_sem,
        device_id=(0, 0),
        device_id_type=pl.DeviceIdType.MESH,
    )
    every.wait_send()
    every.wait_recv()


def chain_forces(x):
    lane = lax.broadcasted_iota(jnp.int32, x[0].shape, 1) & 63
    last = lane == 63
    ahead = lambda v: pltpu.roll(v, 127, 1)
    behind = lambda v: pltpu.roll(v, 1, 1)
    bond = [jnp.where(last, 0.5, ahead(v) - v) for v in x]
    square = bond[0] * bond[0] + bond[1] * bond[1] + bond[2] * bond[2]
    inverse = lax.rsqrt(square)
    unit = [v * inverse for v in bond]
    following = [ahead(v) for v in unit]
    cosine = unit[0] * following[0] + unit[1] * following[1] + unit[2] * following[2]
    bends = lane < 62
    stretch = fene_k / (1.0 - square / fene_reach**2)
    before = behind(jnp.where(bends, 1.0, 0.0))
    cosine_before = behind(cosine)
    grad = []
    for c in range(3):
        pull = jnp.where(bends, following[c] - cosine * unit[c], 0.0)
        push = before * (behind(unit[c]) - cosine_before * unit[c])
        push = jnp.where(lane == 0, 0.0, push)
        grad.append(
            jnp.where(last, 0.0, stretch * bond[c] - bend_k * inverse * (pull + push))
        )
    return [g - jnp.where(lane == 0, 0.0, behind(g)) for g in grad]


def send_kernel(
    members, n_gx, n_gy, pos_ref, route_ref, in_ref, out_ref, plane_ref, left_ref, sum_ref, send_sem,
    recv_sem,
):
    me = lax.axis_index("gx") * n_gy + lax.axis_index("gy")
    greet_all(n_gx, n_gy)
    rows = route_ref.shape[0]
    for c in range(3):
        for r in range(rows):
            plane_ref[c, r : r + 1, :] = pos_ref[c : c + 1, r * 128 : (r + 1) * 128]
    forces = chain_forces([plane_ref[c] for c in range(3)])
    for c in range(3):
        plane_ref[3 + c] = forces[c]
    scatter_rows(
        6, rows, lambda c, r: plane_ref[c, pl.ds(r, 1), :], route_ref, left_ref, sum_ref
    )
    for c in range(6):
        out_ref[0:64, c, :] = sum_ref[c * 64 : (c + 1) * 64, 0:128]
        out_ref[64:128, c, :] = sum_ref[c * 64 : (c + 1) * 64, 128:256]
    wait_for_all(members)

    send_rows(out_ref, in_ref, me, n_gx, n_gy, send_sem, recv_sem)
    in_ref[me] = out_ref[me]
    wait_rows(out_ref, in_ref, members, send_sem, recv_sem)


def vmem(n):
    return [pl.BlockSpec(memory_space=pltpu.VMEM)] * n


def send_message(positions, route):
    n_gx, n_gy = lax.axis_size("gx"), lax.axis_size("gy")
    members = n_gx * n_gy
    return pl.pallas_call(
        partial(send_kernel, members, n_gx, n_gy),
        out_shape=jax.ShapeDtypeStruct((128, 6, 128), f32),
        in_specs=vmem(2),
        out_specs=pl.BlockSpec(memory_space=pltpu.VMEM),
        scratch_shapes=[
            pltpu.VMEM((128, 6, 128), f32),
            pltpu.VMEM((6, 64, 128), f32),
            pltpu.VMEM((768, 1024), bf16),
            pltpu.VMEM((384, 256), f32),
            pltpu.SemaphoreType.DMA,
            pltpu.SemaphoreType.DMA,
        ],
        compiler_params=pltpu.CompilerParams(
            vmem_limit_bytes=VMEM_LIMIT, collective_id=1, has_side_effects=True
        ),
        name="send",
    )(positions, route)


def place_kernel(
    members, n_gx, n_gy, part_ref, in_ref, order_ref, all_ref, twist_ref, grid_ref, beside_ref, flow_ref, left_ref, sum_ref, spec_ref,
    spec_in_ref, mid_ref, spec_send, spec_recv, side_send, side_recv,
):
    g_x = lax.axis_index("gx")
    me = g_x * n_gy + lax.axis_index("gy")
    greet_all(n_gx, n_gy)
    inner_ref, inner_back_ref = all_ref.at[:, 0:256, :], all_ref.at[:, 256:512, :]
    outer_ref, outer_back_ref = all_ref.at[:, 512:768, 0:128], all_ref.at[:, 768:896, :]
    scatter_rows(
        6, members, lambda c, r: in_ref[r, c : c + 1, :], order_ref, left_ref, sum_ref
    )

    def to_grid(c, half, value):
        grid_ref[c, half * 64 : (half + 1) * 64, :] = value

    unpack_sums(6, sum_ref, to_grid)
    for c in range(3):
        hi, lo = split2(grid_ref[3 + c])
        kind = slice(512, 640) if c < 2 else slice(640, 768)
        spec_ref[:, c, :] = dot3(all_ref[0, kind, 128:256], all_ref[1, kind, 128:256], hi, lo, dot_t)
    wait_for_all(members)
    side = pltpu.make_async_remote_copy(
        src_ref=grid_ref,
        dst_ref=beside_ref,
        send_sem=side_send,
        recv_sem=side_recv,
        device_id=(wrapped(g_x + n_gx - 1, n_gx), lax.axis_index("gy")),
        device_id_type=pl.DeviceIdType.MESH,
    )

    send_rows(spec_ref, spec_in_ref, me, n_gx, n_gy, spec_send, spec_recv)
    side.start()
    spec_in_ref[me] = spec_ref[me]
    wait_rows(spec_ref, spec_in_ref, members, spec_send, spec_recv)
    wave_part(
        part_ref, spec_in_ref, outer_ref, outer_back_ref, inner_ref, inner_back_ref, twist_ref,
        flow_ref, mid_ref,
    )
    side.wait()


def place_on_grid(incoming, order, table, member):
    n_gx, n_gy = lax.axis_size("gx"), lax.axis_size("gy")
    members = n_gx * n_gy
    return pl.pallas_call(
        partial(place_kernel, members, n_gx, n_gy),
        out_shape=[
            jax.ShapeDtypeStruct((6, 128, 128), f32),
            jax.ShapeDtypeStruct((6, 128, 128), f32),
            jax.ShapeDtypeStruct((128, 3, 128), f32),
        ],
        in_specs=[pl.BlockSpec(memory_space=pltpu.SMEM)] + vmem(4),
        out_specs=vmem(3),
        scratch_shapes=[
            pltpu.VMEM((768, 1024), bf16),
            pltpu.VMEM((384, 256), f32),
            pltpu.VMEM((128, 3, 128), f32),
            pltpu.VMEM((128, 3, 128), f32),
            pltpu.VMEM((128, 256), f32),
            pltpu.SemaphoreType.DMA,
            pltpu.SemaphoreType.DMA,
            pltpu.SemaphoreType.DMA,
            pltpu.SemaphoreType.DMA,
        ],
        compiler_params=pltpu.CompilerParams(
            vmem_limit_bytes=VMEM_LIMIT, collective_id=3, has_side_effects=True
        ),
        name="place",
    )(
        frequency_part(member), incoming, order, table["all"], table["twist"]
    )


def wave_part(
    part_ref, in_ref, outer_ref, outer_back_ref, inner_ref, inner_back_ref, twist_ref,
    out_ref, mid_ref,
):
    freq, turn_re, turn_im, weight = (part_ref[i] for i in range(4))
    cos_t, sin_t = twist_ref[0], twist_ref[1]
    spectrum = []
    for c in range(3):
        hi, lo = split2(in_ref[:, c, :])
        both = dot3(outer_ref[0], outer_ref[1], hi, lo)
        re, im = both[0:128], both[128:256]
        mid_ref[:, 0:128] = re * cos_t + im * sin_t
        mid_ref[:, 128:256] = im * cos_t - re * sin_t
        hi, lo = split2(mid_ref[...])
        both = dot3(hi, lo, inner_ref[0], inner_ref[1])
        spectrum.append((both[:, 0:128], both[:, 128:256]))
    row = lax.broadcasted_iota(jnp.int32, (128, 128), 0)
    col = lax.broadcasted_iota(jnp.int32, (128, 128), 1)
    n_x = (row >> 3) + 16 * (col >> 4)
    n_y = (row & 7) + 8 * (col & 15)
    unit = 2.0 * math.pi / (G * grid_spacing)
    signed = lambda n: jnp.where(n < G // 2, n, n - G).astype(f32) * unit
    k_x, k_y = signed(n_x), signed(n_y)
    k_z = jnp.full((128, 128), freq * unit, f32)
    edge_x = jnp.where(n_x == G // 2, 1.0, 0.0)
    edge_y = jnp.where(n_y == G // 2, 1.0, 0.0)
    edge_z = jnp.where(jnp.full((128, 128), freq, f32) < -63.5, 1.0, 0.0)
    square = k_x * k_x + k_y * k_y + k_z * k_z
    positive = square > 0.0
    safe = jnp.where(positive, square, 1.0)
    green = jnp.where(
        positive,
        (1.0 - 0.25 * square / 3.0) * (1.0 + square) * jnp.exp(-square) / safe,
        0.0,
    ) * (weight / float(G**3))
    over = green / safe
    g_xy = jnp.where(edge_x == edge_y, -over * k_x * k_y, 0.0)
    g_xz = jnp.where(edge_x == edge_z, -over * k_x * k_z, 0.0)
    g_yz = jnp.where(edge_y == edge_z, -over * k_y * k_z, 0.0)
    g_xx = green - over * k_x * k_x
    g_yy = green - over * k_y * k_y
    g_zz = green - over * k_z * k_z
    (x_re, x_im), (y_re, y_im), (z_re, z_im) = spectrum
    z_re, z_im = turn_re * z_re - turn_im * z_im, turn_re * z_im + turn_im * z_re
    flow = [
        (g_xx * x_re + g_xy * y_re + g_xz * z_re, g_xx * x_im + g_xy * y_im + g_xz * z_im),
        (g_xy * x_re + g_yy * y_re + g_yz * z_re, g_xy * x_im + g_yy * y_im + g_yz * z_im),
    ]
    w_re = g_xz * x_re + g_yz * y_re + g_zz * z_re
    w_im = g_xz * x_im + g_yz * y_im + g_zz * z_im
    flow.append((turn_re * w_re + turn_im * w_im, turn_re * w_im - turn_im * w_re))
    for c in range(3):
        mid_ref[:, 0:128], mid_ref[:, 128:256] = flow[c]
        hi, lo = split2(mid_ref[...])
        both = dot3(hi, lo, inner_back_ref[0], inner_back_ref[1])
        re, im = both[:, 0:128], both[:, 128:256]
        hi, lo = split2(
            jnp.concatenate([re * cos_t - im * sin_t, im * cos_t + re * sin_t], axis=0)
        )
        out_ref[:, c, :] = dot3(outer_back_ref[0], outer_back_ref[1], hi, lo)


def frequency_part(member):
    special = member % 64 == 63
    freq = jnp.where(member < 64, member + 1, (member - 63) % 64)
    freq = jnp.where(member == 63, -64, freq)
    side = jnp.where(member < 64, 1.0, -1.0)
    return jnp.stack(
        [
            freq.astype(f32),
            jnp.where(special, 1.0, 0.0),
            jnp.where(special, 0.0, side),
            jnp.where(special, 1.0, 2.0),
        ]
    ).astype(f32)


ERFC_SHIFT = 4.0
ERFC_POLY = (
    -5.9986000529477224e-05, 1.1337793270330845, 4.308175452878655, 20.093023854033866,
    -8.594175483206275, 489.91788674098177, -1701.7584635921016, 1704.126720738659,
)


def pair_scalars(s2):
    u = lax.rsqrt(s2)
    gauss = jnp.exp2(s2 * (-0.25 * math.log2(math.e)))
    t = pl.reciprocal(s2 * u + ERFC_SHIFT, approx=True)
    w = ERFC_POLY[-1]
    for coefficient in ERFC_POLY[-2::-1]:
        w = w * t + coefficient
    u2 = u * u
    wu = w * u
    along = gauss * (wu * (0.0625 * u2 + 0.375) + 0.125)
    across = (gauss * u2) * (wu * (0.375 - 0.1875 * u2) - 0.125)
    return along, across


def both_halves(v):
    low_half = lax.broadcasted_iota(jnp.int32, (1, 128), 1) < 64
    other = pltpu.roll(v, 64, 1)
    return jnp.where(low_half, v, other), jnp.where(low_half, other, v)


def stage_nodes(ref, weight_stage, right_stage):
    x = [ref[c] for c in range(3)]
    f = [ref[3 + c] for c in range(3)]
    xf = x[0] * f[0] + x[1] * f[1] + x[2] * f[2]
    rows = f + [xf]
    rows += [x[a] * f[b] for a in range(3) for b in range(3)]
    rows += [x[a] * xf for a in range(3)]
    for c, plane in enumerate(rows):
        weight_stage[pl.ds(c, 128, stride=16), :] = plane
    norm = x[0] * x[0] + x[1] * x[1] + x[2] * x[2]
    first, second = [], []
    for h, m, l in [split3(v) for v in x]:
        first += [h, h, m, m, h, l]
        second += [h, m, h, m, l, h]
    one = jnp.ones((128, 128), f32)
    first = [-2.0 * v for v in first] + list(split3(norm)) + [one] * 3
    second += [one] * 3 + list(split3(norm + 0.25))
    for c, plane in enumerate(second):
        right_stage[pl.ds(c, 128, stride=FEATURES), :] = plane
    return first


def build_tables(base, weight_stage, right_stage, weight_ref, right_ref):
    blank = jnp.zeros((32 - FEATURES, 128), f32)

    def build(r, _):
        w = weight_stage[pl.ds(pl.multiple_of(r * 16, 8), 16), :]
        for k, v in enumerate(both_halves(w)):
            hi = v.astype(bf16)
            lo = (v - hi.astype(f32)).astype(bf16)
            weight_ref[base + 2 * r + k] = jnp.concatenate([hi, lo], axis=0)
        w = right_stage[pl.ds(pl.multiple_of(r * FEATURES, 8), FEATURES), :]
        for k, v in enumerate(both_halves(w)):
            right_ref[base + 2 * r + k] = jnp.concatenate([v, blank], axis=0).astype(bf16)
        return 0

    lax.fori_loop(0, 128, build, 0, unroll=16)


def build_left(first, left_stage, left_ref):
    for c, plane in enumerate(first):
        left_stage[pl.ds(c, 128, stride=FEATURES), :] = plane
    eye = jnp.where(
        lax.broadcasted_iota(jnp.int32, (128, 128), 0)
        == lax.broadcasted_iota(jnp.int32, (128, 128), 1),
        1.0,
        0.0,
    ).astype(bf16)
    blank = jnp.zeros((32 - FEATURES, 128), f32)

    def turn_left(r, _):
        v = left_stage[pl.ds(pl.multiple_of(r * FEATURES, 8), FEATURES), :]
        v = jnp.concatenate([v, blank], axis=0).astype(bf16)
        nodes = dot_t(eye, jnp.concatenate([v] * 4, axis=0)).astype(bf16)
        left_ref[2 * r] = nodes[0:64]
        left_ref[2 * r + 1] = nodes[64:128]
        return 0

    lax.fori_loop(0, 128, turn_left, 0, unroll=8)


def pair_kernel(
    list_ref, count_ref, own_ref, beside_ref, own_vel_ref, far_vel_ref,
    weight_ref, right_ref, left_ref, weight_stage, right_stage, left_stage,
    near_acc, far_acc, s2_a, s2_b, tile_a, tile_b,
):
    first = stage_nodes(own_ref, weight_stage, right_stage)
    build_left(first, left_stage, left_ref)
    build_tables(0, weight_stage, right_stage, weight_ref, right_ref)
    stage_nodes(beside_ref, weight_stage, right_stage)
    build_tables(BLOCKS, weight_stage, right_stage, weight_ref, right_ref)

    lane = lax.broadcasted_iota(jnp.int32, (1, 128), 1)
    low_half = lane < 64
    count = count_ref[0]

    def clear(r, _):
        blank = jnp.zeros((W_ROWS, 128), f32)
        far_acc[pl.ds(pl.multiple_of(r * 2 * W_ROWS, 8), W_ROWS), :] = blank
        far_acc[pl.ds(pl.multiple_of(r * 2 * W_ROWS + W_ROWS, 8), W_ROWS), :] = blank
        near_acc[pl.ds(pl.multiple_of(r * W_ROWS, 8), W_ROWS), :] = blank
        return 0

    lax.fori_loop(0, BLOCKS, clear, 0, unroll=8)

    wide = lax.broadcasted_iota(jnp.int32, (64, 128), 1)
    wide_low = wide < 64
    wide_even = (wide & 32) == 0
    narrow = lax.broadcasted_iota(jnp.int32, (32, 128), 1) < 64
    nothing = jnp.zeros((32, 128), bf16)

    def half_of(v, half):
        return jnp.where(narrow, nothing, v) if half else jnp.where(narrow, v, nothing)

    half_keep = [(lane >> 6) == s for s in range(2)]
    blank = jnp.zeros((64, 128), bf16)

    def blocks_of(pair):
        return list_ref[0, pair], list_ref[1, pair]

    def distance_dots(step):
        found = []
        for g in range(GROUPS):
            pairs = [blocks_of((step * GROUPS + g) * STEP + s) for s in range(STEP)]
            left = [left_ref[pairs[s][0]] for s in range(STEP)]
            left = jnp.where(
                wide_low,
                jnp.where(wide_even, left[0], left[1]),
                jnp.where(wide_even, left[2], left[3]),
            )
            right = [half_of(right_ref[pairs[s][1]], s % 2) for s in range(STEP)]
            right = jnp.concatenate(
                [
                    jnp.concatenate([right[0], right[1], blank], axis=0),
                    jnp.concatenate([blank, right[2], right[3]], axis=0),
                ],
                axis=1,
            )
            found.append(dot(left, right))
        return found

    def scalars(s2_ref, tile_ref, pack):
        half = pack % 2
        along, across = pair_scalars(s2_ref[pack // 2, :, half * 128 : (half + 1) * 128])
        for at, value in ((0, across), (128, along)):
            hi, lo = split2(value)
            tile_ref[pack, at : at + 64, :] = hi
            tile_ref[pack, at + 64 : at + 128, :] = lo

    def sum_dots(step, tile_ref, pack):
        tile = tile_ref[pack]
        pairs = [blocks_of((step * 2 * GROUPS + pack) * 2 + s) for s in range(2)]
        a = jnp.concatenate([weight_ref[i] for i, _ in pairs], axis=0)
        b = jnp.concatenate(
            [half_of(weight_ref[j], s) for s, (_, j) in enumerate(pairs)], axis=0
        )
        to_far = dot(a, jnp.concatenate([tile[0:128], tile[128:256]], axis=1))
        return dot_t(b, tile), to_far

    def add_sums(step, pack, to_near, to_far):
        for s in range(2):
            number = (step * 2 * GROUPS + pack) * 2 + s
            for out, acc_ref, row, keep in (
                (to_near, near_acc, list_ref[2, number], None),
                (to_far, far_acc, list_ref[3, number], half_keep[s]),
            ):
                top = 32 * s
                add_h = out[top : top + 16, 0:128] + out[top + 16 : top + 32, 0:128]
                add_f = out[top : top + 8, 128:256] + out[top + 16 : top + 24, 128:256]
                add = jnp.concatenate([add_h, add_f], axis=0)
                if keep is not None:
                    add = jnp.where(keep, add, 0.0)
                acc_ref[pl.ds(pl.multiple_of(row, 8), W_ROWS), :] += add

    packs = range(2 * GROUPS)

    def keep_distances(found, s2_ref):
        for g in range(GROUPS):
            s2_ref[g] = found[g]

    def stage(k, s2_next, s2_now, tile_now, tile_last):
        for pack in packs:
            scalars(s2_now, tile_now, pack)
        for pack in packs:
            add_sums(k - 1, pack, *sum_dots(k - 1, tile_last, pack))
        keep_distances(distance_dots(k + 1), s2_next)

    steps = (count + (STEP * GROUPS - 1)) // (STEP * GROUPS)
    keep_distances(distance_dots(0), s2_a)
    for pack in packs:
        scalars(s2_a, tile_a, pack)
    keep_distances(distance_dots(1), s2_b)

    def body(j, _):
        k = 2 * j + 1
        stage(k, s2_a, s2_b, tile_b, tile_a)
        stage(k + 1, s2_b, s2_a, tile_a, tile_b)
        return 0

    lax.fori_loop(0, (steps + 1) // 2, body, 0)

    chunk = 32
    for side, ref, out_ref in ((0, own_ref, own_vel_ref), (1, beside_ref, far_vel_ref)):
        for top in range(0, 128, chunk):
            planes = []
            for c in range(19):
                at = (2 * top) * W_ROWS + c
                even = far_acc[pl.ds(side * BLOCKS * W_ROWS + at, chunk, stride=2 * W_ROWS), :]
                at += W_ROWS
                odd = far_acc[pl.ds(side * BLOCKS * W_ROWS + at, chunk, stride=2 * W_ROWS), :]
                if side == 0:
                    even += near_acc[pl.ds(at - W_ROWS, chunk, stride=2 * W_ROWS), :]
                    odd += near_acc[pl.ds(at, chunk, stride=2 * W_ROWS), :]
                even = even + pltpu.roll(even, 64, 1)
                odd = odd + pltpu.roll(odd, 64, 1)
                planes.append(jnp.where(low_half, even, odd))
            x = [ref[c, top : top + chunk, :] for c in range(3)]
            h_f, h_xf, h_x_f, h_x_xf, along = (
                planes[0:3], planes[3], planes[4:13], planes[13:16], planes[16:19],
            )
            x_h_f = x[0] * h_f[0] + x[1] * h_f[1] + x[2] * h_f[2] - h_xf
            for c in range(3):
                out_ref[c, top : top + chunk, :] = (
                    along[c]
                    + x[c] * x_h_f
                    - (x[0] * h_x_f[3 * c] + x[1] * h_x_f[3 * c + 1] + x[2] * h_x_f[3 * c + 2])
                    + h_x_xf[c]
                )


def pair_lists(first_list, second_list, count):
    live = jnp.arange(PAIRS, dtype=jnp.int32) < count
    lists = jnp.stack(
        [
            first_list,
            second_list,
            jnp.where(live, first_list, BLOCKS) * W_ROWS,
            jnp.where(live & (first_list != second_list), second_list, 2 * BLOCKS) * W_ROWS,
        ]
    )
    spare = jnp.array([0, 0, BLOCKS * W_ROWS, 2 * BLOCKS * W_ROWS], jnp.int32)
    return jnp.concatenate([lists, jnp.broadcast_to(spare[:, None], (4, 128))], axis=1)


def pair_velocities(own, beside, lists, count):
    plane = jax.ShapeDtypeStruct((3, 128, 128), f32)
    return pl.pallas_call(
        pair_kernel,
        out_shape=[plane, plane],
        in_specs=[pl.BlockSpec(memory_space=pltpu.SMEM)] * 2 + vmem(2),
        out_specs=vmem(2),
        scratch_shapes=[
            pltpu.VMEM((2 * BLOCKS, 32, 128), bf16),
            pltpu.VMEM((2 * BLOCKS, 32, 128), bf16),
            pltpu.VMEM((BLOCKS, 64, 128), bf16),
            pltpu.VMEM((128 * 16, 128), f32),
            pltpu.VMEM((128 * FEATURES, 128), f32),
            pltpu.VMEM((128 * FEATURES, 128), f32),
            pltpu.VMEM(((BLOCKS + 1) * W_ROWS, 128), f32),
            pltpu.VMEM(((2 * BLOCKS + 1) * W_ROWS, 128), f32),
            pltpu.VMEM((GROUPS, 64, 256), f32),
            pltpu.VMEM((GROUPS, 64, 256), f32),
            pltpu.VMEM((2 * GROUPS, 256, 128), bf16),
            pltpu.VMEM((2 * GROUPS, 256, 128), bf16),
        ],
        compiler_params=pltpu.CompilerParams(vmem_limit_bytes=PAIR_VMEM),
        cost_estimate=cost(50),
        name="pairs",
    )(lists, count, own, beside)


def reply_kernel(
    members, n_gx, n_gy, own_ref, far_ref, flow_ref, order_ref, z_ref, in_ref, out_ref,
    wave_ref, beside_ref, hi_ref, lo_ref, low_a, low_b, send_sem, recv_sem, far_send, far_recv,
    wave_send, wave_recv,
):
    g_x = lax.axis_index("gx")
    me = g_x * n_gy + lax.axis_index("gy")
    greet_all(n_gx, n_gy)
    wait_for_all(members)
    far = pltpu.make_async_remote_copy(
        src_ref=far_ref,
        dst_ref=beside_ref,
        send_sem=far_send,
        recv_sem=far_recv,
        device_id=(wrapped(g_x + 1, n_gx), lax.axis_index("gy")),
        device_id_type=pl.DeviceIdType.MESH,
    )
    far.start()
    send_rows(flow_ref, wave_ref, me, n_gx, n_gy, wave_send, wave_recv)
    wave_ref[me] = flow_ref[me]
    far.wait()
    wait_rows(flow_ref, wave_ref, members, wave_send, wave_recv)
    for c in range(3):
        kind = 0 if c < 2 else 1
        hi, lo = split2(jnp.transpose(wave_ref[:, c, :]))
        wave = dot3(hi, lo, z_ref[0, kind], z_ref[1, kind])
        fill_table(c, own_ref[c] + beside_ref[c] + wave, hi_ref, lo_ref)

    def row_at(g, n):
        return g * WIDTH + n

    def put(g, c, n, row):
        out_ref[row_at(g, n), c : c + 1, :] = row

    gather_rows(
        3, members // WIDTH, row_at, hi_ref, lo_ref, order_ref, (low_a, low_b), put
    )

    send_rows(out_ref, in_ref, me, n_gx, n_gy, send_sem, recv_sem)
    in_ref[me] = out_ref[me]
    wait_rows(out_ref, in_ref, members, send_sem, recv_sem)


def reply_message(own_vel, far_vel, wave, order, z_table):
    n_gx, n_gy = lax.axis_size("gx"), lax.axis_size("gy")
    members = n_gx * n_gy
    return pl.pallas_call(
        partial(reply_kernel, members, n_gx, n_gy),
        out_shape=jax.ShapeDtypeStruct((128, 3, 128), f32),
        in_specs=vmem(5),
        out_specs=pl.BlockSpec(memory_space=pltpu.VMEM),
        scratch_shapes=[
            pltpu.VMEM((128, 3, 128), f32),
            pltpu.VMEM((128, 3, 128), f32),
            pltpu.VMEM((3, 128, 128), f32),
            pltpu.VMEM((192, 256), bf16),
            pltpu.VMEM((192, 256), bf16),
            pltpu.VMEM((256, WIDTH * 128), bf16),
            pltpu.VMEM((256, WIDTH * 128), bf16),
            pltpu.SemaphoreType.DMA,
            pltpu.SemaphoreType.DMA,
            pltpu.SemaphoreType.DMA,
            pltpu.SemaphoreType.DMA,
            pltpu.SemaphoreType.DMA,
            pltpu.SemaphoreType.DMA,
        ],
        compiler_params=pltpu.CompilerParams(
            vmem_limit_bytes=VMEM_LIMIT, collective_id=2, has_side_effects=True
        ),
        name="reply",
    )(own_vel, far_vel, wave, order, z_table)


def move_kernel(
    in_ref, route_ref, pos_ref, noise_ref, moved_ref, drift_ref, hi_ref, lo_ref, vel_ref, low_a,
    low_b,
):
    rows = route_ref.shape[0]
    for c in range(3):
        fill_table(c, in_ref[:, c, :], hi_ref, lo_ref)

    def row_at(g, n):
        return g * WIDTH + n

    def put(g, c, n, row):
        vel_ref[c, pl.ds(row_at(g, n), 1), :] = row

    gather_rows(3, rows // WIDTH, row_at, hi_ref, lo_ref, route_ref, (low_a, low_b), put)
    for c in range(3):
        for r in range(rows):
            drift_ref[c : c + 1, r * 128 : (r + 1) * 128] = time_step * vel_ref[c, r : r + 1, :]
    moved_ref[...] = pos_ref[...] + drift_ref[...] + noise_ref[...]


def move_beads(arrived, route, positions, noise):
    flat = jax.ShapeDtypeStruct(positions.shape, f32)
    return pl.pallas_call(
        move_kernel,
        out_shape=[flat, flat],
        in_specs=vmem(4),
        out_specs=vmem(2),
        scratch_shapes=[
            pltpu.VMEM((192, 256), bf16),
            pltpu.VMEM((192, 256), bf16),
            pltpu.VMEM((3, 64, 128), f32),
            pltpu.VMEM((256, WIDTH * 128), bf16),
            pltpu.VMEM((256, WIDTH * 128), bf16),
        ],
        compiler_params=pltpu.CompilerParams(vmem_limit_bytes=VMEM_LIMIT),
        name="move",
    )(arrived, route, positions, noise)


def shards(positions, noise, route, node_perm, pair_first, pair_second, pair_count):
    table = {name: jnp.asarray(value) for name, value in tables().items()}
    row_gx = lax.axis_index("gx")
    member = row_gx * lax.axis_size("gy") + lax.axis_index("gy")
    route = route.reshape(64, 128)
    order = lax.dynamic_index_in_dim(node_perm, row_gx, 0, keepdims=False).reshape(128, 128)
    incoming = send_message(positions, route)
    grid, beside, wave = place_on_grid(incoming, order, table, member)
    lists = pair_lists(pair_first[0], pair_second[0], pair_count[0])
    own_vel, far_vel = pair_velocities(grid, beside, lists, pair_count)
    reply = reply_message(own_vel, far_vel, wave, order, table["z"])
    return tuple(move_beads(reply, route, positions, noise))


def solution(mesh):
    in_specs = (
        P(None, ("gx", "gy")),
        P(None, ("gx", "gy")),
        P(("gx", "gy")),
        P(None, "gy", None),
        P(("gx", "gy"), None),
        P(("gx", "gy"), None),
        P(("gx", "gy")),
    )
    out_specs = (P(None, ("gx", "gy")), P(None, ("gx", "gy")))
    return jax.shard_map(shards, mesh=mesh, in_specs=in_specs, out_specs=out_specs, check_vma=False)
```
